32 devices in a mesh: seq: 8 (over z, x), rep: 4 (over y, core).
Axes of the slice: x: 2, y: 2, z: 4, core: 2. Of those that a mesh axis runs over, the one named last changes fastest.
Arguments:
- tokens: bfloat16 [1024, 1440], P('seq'), may hold values from -36 to 36
- norm_gain: float32 [1440], replicated, may hold values from 0.1 to 1.9
- expert_ids: int32 [1024, 4], P('seq'), may hold values from 0 to 7, all different within a row; in each aligned block of 128 rows (0 to 127, 128 to 255, ...) at most 128 rows name the same one
- route_weights: float32 [1024, 4], P('seq'), may hold values from 0.1 to 0.6
- gate_weight: bfloat16 [8, 1440, 1440], P('seq', None, 'rep'), may hold values from -0.15625 to 0.15625
- gate_bias: float32 [8, 1440], P('seq', 'rep'), may hold values from -3 to 3
- up_weight: bfloat16 [8, 1440, 1440], P('seq', None, 'rep'), may hold values from -0.15625 to 0.15625
- up_bias: float32 [8, 1440], P('seq', 'rep'), may hold values from -3 to 3
- down_weight: bfloat16 [8, 1440, 1440], P('seq', 'rep'), may hold values from -0.15625 to 0.15625
- down_bias: float32 [8, 1440], P('seq', 'rep'), may hold values from -3 to 3
Outputs:
- mixed: bfloat16 [1024, 1440], P('seq', 'rep')
The draws below stay inside these ranges and needn't reach their ends.
Inputs may be any that keep to these rules, and one draw needn't show every extreme that they name: `expert_ids`: each row names 4 different experts. Among the 128 rows of one index of seq no expert is named more than 128 times, and in every draw some expert is named exactly 128 times by the rows of one index.
All inputs are finite; a program needn't handle non-finite values.
Results may differ from the reference program's by a relative error of at most 0.014.
Values may be sent and summed in bfloat16 or wider, within the bound.
No kernel may reach another device: no remote copies, remote signals or barrier semaphores. Data moves between devices by JAX's collectives and lax.ppermute only.
A program may use at most 64 MiB of HBM per device.

```python
import math
import jax
import jax.numpy as jnp
import numpy as np
from jax import lax

D = 1440
EXPERT_HIDDEN = 1440
TOP = 4
TOK_DEV = 128
EXPERTS = 8
CAP = 128
TOKENS = 1024
N_SEQ = 8
N_REP = 4


def draw_tokens(key, part):
    base_key, row_key, col_key = jax.random.split(jax.random.fold_in(key, 11), 3)
    base = jax.random.truncated_normal(base_key, -4.0, 4.0, (TOKENS, D), jnp.float32)
    row_scale = jnp.exp(jax.random.uniform(row_key, (TOKENS, 1), jnp.float32, math.log(0.3), math.log(3.0)))
    col_scale = jnp.exp(jax.random.uniform(col_key, (1, D), jnp.float32, math.log(0.3), math.log(3.0)))
    return (base * row_scale * col_scale).astype(jnp.bfloat16)


def block_scale(own_key, shape, pieces, least, largest):
    factor_of = 1.0
    for axis_at, blocks in pieces:
        steps = jax.random.uniform(jax.random.fold_in(jax.random.fold_in(own_key, 6), axis_at), (blocks,), jnp.float32, least / len(pieces), largest / len(pieces))
        factor_of = factor_of * jnp.repeat(jnp.exp(steps), shape[axis_at] // blocks).reshape((-1,) + (1,) * (len(shape) - 1 - axis_at))
    return factor_of


def deal_out(rng, own, number, rows, amount, top, limit, lean):
    sequence = jax.random.permutation(rng, amount)
    packed, ordinary = load_shares(amount, rows * top, limit, lean, True), load_shares(amount, rows * top, limit, lean, False)
    places = jnp.arange(amount)

    def named(tallies, offset_by):
        used = int((tallies > 0).sum())
        fixed = max(1, used // 4)
        shifted = fixed + (places - fixed + offset_by * (used - fixed)) % max(1, amount - fixed)
        return jnp.zeros((amount,), jnp.int32).at[sequence[jnp.where(places < fixed, places, shifted)]].set(jnp.asarray(tallies, jnp.int32))

    tallies = jnp.where(number % 4 == 0, named(packed, number // 4), named(ordinary, number - number // 4 - 1))
    mixed = jax.random.permutation(jax.random.fold_in(own, 3), amount)
    source_of, sink = mixed[0:amount // 2 * 2:2], mixed[1:amount // 2 * 2:2]
    slack = jnp.minimum(tallies[source_of] - 1, limit - tallies[sink]) // 2
    slack = jnp.where((source_of == sequence[0]) | (sink == sequence[0]) | (tallies[sink] == 0), 0, jnp.maximum(slack, 0))
    shifted = jax.random.randint(jax.random.fold_in(own, 4), (amount // 2,), 0, 1 << 20) % (slack + 1)
    tallies = tallies.at[source_of].add(-shifted).at[sink].add(shifted)
    items = jnp.searchsorted(jnp.cumsum(tallies), jnp.arange(rows * top), side="right").astype(jnp.int32)
    grid = items.reshape(top, rows).T
    grid = grid[jax.random.permutation(jax.random.fold_in(own, 1), rows)]
    offset_by = jax.random.randint(jax.random.fold_in(own, 2), (rows, 1), 0, top)
    return jnp.take_along_axis(grid, (jnp.arange(top)[None, :] + offset_by) % top, axis=1)


def load_shares(number_of, total, bound, skew, full):
    loads = [(1 << 20) // math.isqrt(rank ** skew) + 1 for rank in range(1, number_of + 1)]
    largest = bound if full else min(bound, max(-(-total // number_of), total * loads[0] // sum(loads)))
    least = 1 if total - largest >= number_of - 1 else 0
    counts, spare = [largest] + [least] * (number_of - 1), total - largest - least * (number_of - 1)
    while spare > 0:
        candidates = [i for i in range(1, number_of) if counts[i] < largest] or [i for i in range(1, number_of) if counts[i] < bound]
        pool, left = sum([loads[i] for i in candidates]), spare
        for i in candidates:
            more = min(bound - counts[i], max(1, left * loads[i] // pool), spare)
            counts[i] = counts[i] + more
            spare = spare - more
    return np.array(counts)


def scatter_about(own_key, shape, deviation, limit, cuts=(), kind=jnp.bfloat16):
    level = block_scale(own_key, shape, cuts, -0.22, 0.18) if cuts else 1.0
    entries = jax.random.normal(own_key, shape, jnp.float32) * deviation * level
    return jnp.minimum(jnp.maximum(entries, -limit), limit).astype(kind)


def setup_inputs(seed: int = 0) -> dict:
    streams_of = jax.random.split(jax.random.key(seed), 11)
    tokens = draw_tokens(jax.random.fold_in(streams_of[10], 71), 0)
    norm_gain = jnp.clip(1.0 + 0.18 * jax.random.normal(streams_of[1], (D,), jnp.float32), 0.1, 1.9)
    expert_ids_keys = jax.random.split(jax.random.fold_in(streams_of[2], 1), TOKENS // TOK_DEV)
    expert_ids_turns = jax.random.permutation(jax.random.fold_in(streams_of[2], 3), TOKENS // TOK_DEV)
    expert_ids = jax.vmap(lambda own, number: deal_out(jax.random.fold_in(streams_of[2], 2), own, number, TOK_DEV, EXPERTS, TOP, CAP, 2))(expert_ids_keys, expert_ids_turns).reshape((TOKENS, TOP))
    route_weights = jnp.clip(0.1 + 0.5 * jax.random.uniform(streams_of[3], (TOKENS, TOP), jnp.float32) ** block_scale(streams_of[3], (TOKENS, TOP), ((0, 8),), -0.2, 0.2), 0.1, 0.6)
    gate_weight = scatter_about(streams_of[4], (EXPERTS, D, EXPERT_HIDDEN), D ** -0.5, 0.15625, ((0, 8), (2, 4)))
    gate_bias = scatter_about(streams_of[5], (EXPERTS, EXPERT_HIDDEN), 0.5, 3.0, ((0, 8), (1, 4)), jnp.float32)
    up_weight = scatter_about(streams_of[6], (EXPERTS, D, EXPERT_HIDDEN), D ** -0.5, 0.15625, ((0, 8), (2, 4)))
    up_bias = scatter_about(streams_of[7], (EXPERTS, EXPERT_HIDDEN), 0.5, 3.0, ((0, 8), (1, 4)), jnp.float32)
    down_weight = scatter_about(streams_of[8], (EXPERTS, EXPERT_HIDDEN, D), EXPERT_HIDDEN ** -0.5, 0.15625, ((0, 8), (1, 4)))
    down_bias = scatter_about(streams_of[9], (EXPERTS, D), 0.5, 3.0, ((0, 8), (1, 4)), jnp.float32)
    return dict(tokens=tokens, norm_gain=norm_gain, expert_ids=expert_ids, route_weights=route_weights, gate_weight=gate_weight, gate_bias=gate_bias, up_weight=up_weight, up_bias=up_bias, down_weight=down_weight, down_bias=down_bias)


def reference(tokens, norm_gain, expert_ids, route_weights, gate_weight, gate_bias, up_weight, up_bias, down_weight, down_bias):
    values = tokens.astype(jnp.float32)
    normed = (values * lax.rsqrt(lax.optimization_barrier(jnp.mean(values * values, axis=-1, keepdims=True)) + 1e-05) * norm_gain).astype(jnp.bfloat16)
    pairs = TOK_DEV * TOP
    grouped = expert_ids.reshape(N_SEQ, pairs)
    onehot = (grouped[:, :, None] == jnp.arange(EXPERTS, dtype=jnp.int32)[None, None, :]).astype(jnp.int32)
    before = jnp.cumsum(onehot, axis=1) - onehot
    slot_index = lax.optimization_barrier(jnp.sum(before * onehot, axis=2)).astype(jnp.int32)
    source = jnp.broadcast_to(jnp.arange(N_SEQ, dtype=jnp.int32)[:, None], (N_SEQ, pairs))
    token_row = (jnp.arange(pairs, dtype=jnp.int32) // TOP)[None, :] + source * TOK_DEV
    table = jnp.full((EXPERTS, N_SEQ, CAP), TOKENS, jnp.int32).at[grouped, source, slot_index].set(token_row)
    padded = jnp.concatenate([normed, jnp.zeros((1, D), jnp.bfloat16)], axis=0)
    block_units = EXPERT_HIDDEN // N_REP

    def one_expert(operands):
        rows_table, w_gate, b_gate, w_up, b_up, w_down, b_down = operands
        in_rows = padded[rows_table.reshape(-1)]
        gate_pre = jnp.dot(in_rows, w_gate, preferred_element_type=jnp.float32) + b_gate
        up_pre = jnp.dot(in_rows, w_up, preferred_element_type=jnp.float32) + b_up
        activated = (gate_pre * jax.nn.sigmoid(1.702 * gate_pre) * (up_pre + 1.0)).astype(jnp.bfloat16)
        blocks = activated.reshape(-1, N_REP, block_units).astype(jnp.float32)
        down_blocks = w_down.reshape(N_REP, block_units, D).astype(jnp.float32)
        parts = jnp.einsum('nbh,bhd->nbd', blocks, down_blocks).astype(jnp.bfloat16)
        total = lax.optimization_barrier(jnp.sum(parts.astype(jnp.float32), axis=1)) + b_down
        return total.astype(jnp.bfloat16)
    outputs = lax.map(one_expert, (table, gate_weight, gate_bias, up_weight, up_bias, down_weight, down_bias))
    flat_out = outputs.reshape(EXPERTS * N_SEQ * CAP, D)
    position = (grouped * N_SEQ + source) * CAP + slot_index
    picked = flat_out[position.reshape(-1)].reshape(TOKENS, TOP, D)
    mixed = lax.optimization_barrier(jnp.sum(route_weights[:, :, None] * picked.astype(jnp.float32), axis=1))
    return mixed.astype(jnp.bfloat16)
```

```python
import jax
import jax.numpy as jnp
from jax import lax
from jax.sharding import PartitionSpec as P


def rms_normed(values, norm_gain, axis):
    values = values.astype(jnp.float32)
    scale = lax.rsqrt(jnp.mean(values * values, axis=axis, keepdims=True) + 1e-05)
    return (values * scale * norm_gain).astype(jnp.bfloat16)


def gated(gate_pre, up_pre):
    return (gate_pre * jax.nn.sigmoid(1.702 * gate_pre) * (up_pre + 1.0)).astype(jnp.bfloat16)


def routed(
    tokens,
    norm_gain,
    expert_ids,
    route_weights,
    gate_weight,
    gate_bias,
    up_weight,
    up_bias,
    down_weight,
    down_bias,
    capacity,
):
    tok_rows, features = tokens.shape
    per_token = expert_ids.shape[1]
    experts = lax.axis_size("seq")
    quarter = features // lax.axis_size("rep")
    normed = rms_normed(tokens, norm_gain, -1)
    flat_ids = expert_ids.reshape(-1)
    onehot = (flat_ids[:, None] == jnp.arange(experts, dtype=jnp.int32)[None, :]).astype(jnp.int32)
    before = jnp.cumsum(onehot, axis=0) - onehot
    slot_index = jnp.sum(before * onehot, axis=1)
    destination = flat_ids * capacity + slot_index
    owner_row = jnp.arange(tok_rows * per_token, dtype=jnp.int32) // per_token
    buffer = jnp.zeros((experts * capacity, features), jnp.bfloat16)
    buffer = buffer.at[destination].set(normed[owner_row])
    received = lax.all_to_all(
        buffer.reshape(experts, capacity, features), "seq", split_axis=0, concat_axis=0, tiled=True
    )
    in_rows = received.reshape(-1, features)
    gate_pre = jnp.dot(in_rows, gate_weight[0], preferred_element_type=jnp.float32) + gate_bias[0]
    up_pre = jnp.dot(in_rows, up_weight[0], preferred_element_type=jnp.float32) + up_bias[0]
    partial_value = jnp.dot(
        gated(gate_pre, up_pre), down_weight[0], preferred_element_type=jnp.float32
    ).astype(jnp.bfloat16)
    summed = lax.psum_scatter(
        partial_value.reshape(experts, capacity, features),
        "rep",
        scatter_dimension=2,
        tiled=True,
    ).astype(jnp.float32)
    expert_out = (summed + down_bias[0][None, None, :]).astype(jnp.bfloat16)
    returned = lax.all_to_all(expert_out, "seq", split_axis=0, concat_axis=0, tiled=True)
    picked = returned.reshape(-1, quarter)[destination].reshape(tok_rows, per_token, quarter)
    mixed = jnp.sum(route_weights[:, :, None] * picked.astype(jnp.float32), axis=1)
    return mixed.astype(jnp.bfloat16)


def dense(
    tokens,
    norm_gain,
    expert_ids,
    route_weights,
    gate_weight,
    gate_bias,
    up_weight,
    up_bias,
    down_weight,
    down_bias,
):
    tok_rows, features = tokens.shape
    experts = lax.axis_size("seq")
    groups = lax.axis_size("rep")
    quarter = features // groups
    rep = lax.axis_index("rep")
    own = lax.dynamic_slice_in_dim(tokens.T, rep * quarter, quarter, 0)
    every = lax.all_gather(own, ("seq", "rep"), axis=0, tiled=True)
    every = every.reshape(experts, features, tok_rows)
    chosen = expert_ids.T[None] == jnp.arange(experts, dtype=jnp.int32)[:, None, None]
    shares = jnp.sum(jnp.where(chosen, route_weights.T[None], 0.0), axis=1)
    shares = lax.all_to_all(shares, "seq", split_axis=0, concat_axis=0, tiled=True)
    normed = rms_normed(every, norm_gain[:, None], 1)
    gate_pre = jnp.einsum("dh,sdt->sht", gate_weight[0], normed, preferred_element_type=jnp.float32)
    up_pre = jnp.einsum("dh,sdt->sht", up_weight[0], normed, preferred_element_type=jnp.float32)
    activated = gated(gate_pre + gate_bias[0][:, None], up_pre + up_bias[0][:, None])
    part = jnp.einsum("hd,sht->sdt", down_weight[0], activated, preferred_element_type=jnp.float32)
    bias = lax.dynamic_update_slice_in_dim(
        jnp.zeros((features,), jnp.float32), down_bias[0], rep * quarter, 0
    )
    part = ((part + bias[:, None]) * shares[:, None, :]).astype(jnp.bfloat16)
    mixed = lax.psum_scatter(
        part.reshape(experts * features, tok_rows), ("seq", "rep"), scatter_dimension=0, tiled=True
    )
    return mixed.T


def on_device(*args):
    tokens, expert_ids = args[0], args[2]
    capacity = 2 * tokens.shape[0] * expert_ids.shape[1] // lax.axis_size("seq")
    if capacity >= tokens.shape[0]:
        return dense(*args)
    return routed(*args, capacity)


def solution(mesh):
    placed = (
        P("seq", None),
        P(),
        P("seq", None),
        P("seq", None),
        P("seq", None, "rep"),
        P("seq", "rep"),
        P("seq", None, "rep"),
        P("seq", "rep"),
        P("seq", "rep", None),
        P("seq", "rep"),
    )
    return jax.shard_map(
        on_device, mesh=mesh, in_specs=placed, out_specs=P("seq", "rep"), check_vma=False
    )
```

```python
import functools

import jax
import jax.numpy as jnp
from jax import lax
from jax.experimental import pallas as pl
from jax.experimental.pallas import tpu as pltpu
from jax.sharding import PartitionSpec as P


def rms_normed(values, norm_gain, axis):
    values = values.astype(jnp.float32)
    scale = lax.rsqrt(jnp.mean(values * values, axis=axis, keepdims=True) + 1e-05)
    return (values * scale * norm_gain).astype(jnp.bfloat16)


def gated(gate_pre, up_pre):
    return (gate_pre * jax.nn.sigmoid(1.702 * gate_pre) * (up_pre + 1.0)).astype(jnp.bfloat16)


def routed(
    tokens,
    norm_gain,
    expert_ids,
    route_weights,
    gate_weight,
    gate_bias,
    up_weight,
    up_bias,
    down_weight,
    down_bias,
    capacity,
):
    tok_rows, features = tokens.shape
    per_token = expert_ids.shape[1]
    experts = lax.axis_size("seq")
    quarter = features // lax.axis_size("rep")
    normed = rms_normed(tokens, norm_gain, -1)
    flat_ids = expert_ids.reshape(-1)
    onehot = (flat_ids[:, None] == jnp.arange(experts, dtype=jnp.int32)[None, :]).astype(jnp.int32)
    before = jnp.cumsum(onehot, axis=0) - onehot
    slot_index = jnp.sum(before * onehot, axis=1)
    destination = flat_ids * capacity + slot_index
    owner_row = jnp.arange(tok_rows * per_token, dtype=jnp.int32) // per_token
    buffer = jnp.zeros((experts * capacity, features), jnp.bfloat16)
    buffer = buffer.at[destination].set(normed[owner_row])
    received = lax.all_to_all(
        buffer.reshape(experts, capacity, features), "seq", split_axis=0, concat_axis=0, tiled=True
    )
    in_rows = received.reshape(-1, features)
    gate_pre = jnp.dot(in_rows, gate_weight[0], preferred_element_type=jnp.float32) + gate_bias[0]
    up_pre = jnp.dot(in_rows, up_weight[0], preferred_element_type=jnp.float32) + up_bias[0]
    partial_value = jnp.dot(
        gated(gate_pre, up_pre), down_weight[0], preferred_element_type=jnp.float32
    ).astype(jnp.bfloat16)
    summed = lax.psum_scatter(
        partial_value.reshape(experts, capacity, features),
        "rep",
        scatter_dimension=2,
        tiled=True,
    ).astype(jnp.float32)
    expert_out = (summed + down_bias[0][None, None, :]).astype(jnp.bfloat16)
    returned = lax.all_to_all(expert_out, "seq", split_axis=0, concat_axis=0, tiled=True)
    picked = returned.reshape(-1, quarter)[destination].reshape(tok_rows, per_token, quarter)
    mixed = jnp.sum(route_weights[:, :, None] * picked.astype(jnp.float32), axis=1)
    return mixed.astype(jnp.bfloat16)


def round_up(number, step):
    return -(-number // step) * step


def add_up(*terms):
    total = terms[0].astype(jnp.float32)
    for term in terms[1:]:
        total = total + term.astype(jnp.float32)
    return total.astype(jnp.bfloat16)


def expert_kernel(
    quarter,
    features,
    p0,
    p1,
    p2,
    p3,
    gate_up_ref,
    down_ref,
    gain_ref,
    bias_ref,
    down_bias_ref,
    pick_ref,
    keep_ref,
    send_ref,
    rows_ref,
):
    pieces = (p0, p1, p2, p3)
    count, piece_rows, lanes = p0.shape
    block = gain_ref.shape[1]
    hidden = gate_up_ref.shape[0] // 2

    @pl.when(pl.program_id(0) == 0)
    def _():
        rows_ref[...] = jnp.zeros_like(rows_ref)

    shares = []
    for j in range(count):
        squares = jnp.zeros((1, lanes), jnp.float32)
        share = jnp.zeros((1, lanes), jnp.float32)
        for k, piece in enumerate(pieces):
            values = piece[j].astype(jnp.float32)
            body = values[:quarter]
            squares += jnp.sum(body * body, axis=0, keepdims=True)
            share += jnp.sum(values[quarter:] * pick_ref[k], axis=0, keepdims=True)
        scale = lax.rsqrt(squares * (1.0 / features) + 1e-05)
        for k, piece in enumerate(pieces):
            values = piece[j].astype(jnp.float32)
            rows_ref[k * block : k * block + piece_rows, j * lanes : (j + 1) * lanes] = (
                values * scale * gain_ref[k, :piece_rows]
            ).astype(jnp.bfloat16)
        shares.append(share)
    wide = jnp.concatenate(shares, axis=1)
    both = jnp.dot(gate_up_ref[...], rows_ref[...], preferred_element_type=jnp.float32)
    bias = jnp.concatenate([bias_ref[...]] * count, axis=1)
    both = both + bias
    activated = gated(both[:hidden], both[hidden:])
    part = jnp.dot(down_ref[...], activated, preferred_element_type=jnp.float32)
    for k in range(len(pieces)):
        rows = part[k * block : k * block + quarter]
        if k == 0:
            rows = rows + jnp.concatenate([down_bias_ref[...]] * count, axis=1)
        rows = (rows * wide).astype(jnp.bfloat16)
        target = send_ref if k % 2 else keep_ref
        for j in range(count):
            target[k // 2, j] = rows[:, j * lanes : (j + 1) * lanes]


def run_expert(pieces, weights, quarter, features):
    chunks, piece_rows, lanes = pieces[0].shape
    count = 2
    gate_up, down = weights[0], weights[1]
    flops = 2 * chunks * lanes * (gate_up.size + down.size)
    out = jax.ShapeDtypeStruct((2, chunks, quarter, lanes), jnp.bfloat16)
    return pl.pallas_call(
        functools.partial(expert_kernel, quarter, features),
        grid=(chunks // count,),
        in_specs=[pl.BlockSpec((count, piece_rows, lanes), lambda i: (i, 0, 0))] * 4
        + [pl.BlockSpec(w.shape, lambda i, n=w.ndim: (0,) * n) for w in weights],
        out_specs=[pl.BlockSpec((2, count, quarter, lanes), lambda i: (0, i, 0, 0))] * 2,
        out_shape=[out, out],
        scratch_shapes=[pltpu.VMEM((gate_up.shape[1], count * lanes), jnp.bfloat16)],
        compiler_params=pltpu.CompilerParams(vmem_limit_bytes=40 * 2**20),
        cost_estimate=pl.CostEstimate(
            flops=flops, bytes_accessed=2 * (gate_up.size + down.size), transcendentals=0
        ),
    )(*pieces, *weights)


def arrange(gate_weight, up_weight, down_weight, gate_bias, up_bias, norm_gain, down_bias, rep, groups, lanes):
    features, hidden = gate_weight.shape
    quarter = features // groups
    hidden_pad, block = round_up(hidden, 128), round_up(quarter, 128)

    def relative(array):
        return jnp.stack(
            [lax.dynamic_index_in_dim(array, rep ^ k, 0, keepdims=False) for k in range(groups)]
        )

    def inward(weight):
        blocks = relative(weight.reshape(groups, quarter, hidden))
        blocks = jnp.pad(blocks, ((0, 0), (0, block - quarter), (0, hidden_pad - hidden)))
        return blocks.reshape(groups * block, hidden_pad).T

    def column(vector, size):
        return jnp.broadcast_to(jnp.pad(vector, (0, size - vector.shape[0]))[:, None], (size, lanes))

    gate_up = jnp.concatenate([inward(gate_weight), inward(up_weight)], axis=0)
    outward = relative(down_weight.T.reshape(groups, quarter, hidden))
    outward = jnp.pad(outward, ((0, 0), (0, block - quarter), (0, hidden_pad - hidden)))
    outward = outward.reshape(groups * block, hidden_pad)
    gain = relative(norm_gain.reshape(groups, quarter))
    gain = jnp.pad(gain, ((0, 0), (0, block - quarter)))
    gain = jnp.broadcast_to(gain[:, :, None], (groups, block, lanes))
    bias = jnp.concatenate([column(gate_bias, hidden_pad), column(up_bias, hidden_pad)], axis=0)
    return gate_up, outward, gain, bias, column(down_bias, quarter)


def dense(
    tokens,
    norm_gain,
    expert_ids,
    route_weights,
    gate_weight,
    gate_bias,
    up_weight,
    up_bias,
    down_weight,
    down_bias,
):
    lanes, features = tokens.shape
    experts = lax.axis_size("seq")
    groups = lax.axis_size("rep")
    quarter = features // groups
    rep, seq = lax.axis_index("rep"), lax.axis_index("seq")
    devices = experts * groups
    lines = experts // 2
    half = lines // 2
    core, along_y, along_x, along_z = 1, 2, groups, 2 * groups

    def swap(array, step):
        return lax.ppermute(array, ("seq", "rep"), [(i, i ^ step) for i in range(devices)])

    per = -(-experts // groups)
    piece_rows = round_up(quarter + 3 * per, 16)
    tail = piece_rows - quarter
    chosen = expert_ids.T[None] == jnp.arange(experts, dtype=jnp.int32)[:, None, None]
    shares = jnp.sum(jnp.where(chosen, route_weights.T[None], 0.0), axis=1)
    high = lax.reduce_precision(shares, 8, 7)
    middle = lax.reduce_precision(shares - high, 8, 7)
    low = lax.reduce_precision(shares - high - middle, 8, 7)
    terms = jnp.stack([high, middle, low], axis=1).reshape(3 * experts, lanes)
    terms = jnp.pad(terms, ((0, 3 * per * groups - 3 * experts), (0, 0)))
    terms = lax.dynamic_slice_in_dim(terms, rep * 3 * per, 3 * per, 0).astype(jnp.bfloat16)
    own = lax.dynamic_slice_in_dim(tokens.T, rep * quarter, quarter, 0)
    own = jnp.concatenate([own, jnp.pad(terms, ((0, tail - 3 * per), (0, 0)))], axis=0)
    source = rep ^ jnp.arange(groups, dtype=jnp.int32)
    row = jnp.arange(tail, dtype=jnp.int32)
    pick = (source[:, None] * per + row[None, :] // 3 == seq) & (row[None, :] < 3 * per)
    pick = jnp.broadcast_to(pick.astype(jnp.float32)[:, :, None], (groups, tail, lanes))

    here = jnp.stack([own] + [swap(own, k * along_z) for k in range(1, lines)])
    from_x, from_y = swap(here, along_x), swap(here, along_y)
    here_core = swap(here, core)
    corner = jnp.concatenate(
        [swap(from_x[:half], along_y), swap(from_y[half:], along_x)], axis=0
    )
    from_y_core = swap(from_y, core)
    from_x_core = swap(from_x, core)
    corner_core = swap(corner, core)

    weights = arrange(
        gate_weight[0],
        up_weight[0],
        down_weight[0],
        gate_bias[0],
        up_bias[0],
        norm_gain,
        down_bias[0],
        rep,
        groups,
        lanes,
    ) + (pick,)
    keep, send = run_expert((here, here_core, from_y, from_y_core), weights, quarter, features)
    near = add_up(keep, swap(send, core))
    near_y = swap(near[1, :half], along_y)
    keep, send = run_expert((from_x, from_x_core, corner, corner_core), weights, quarter, features)
    far = add_up(keep, swap(send, core))
    far_y = swap(far[1, :half], along_y)
    far_x = swap(far[:, half:], along_x)
    last_x = swap(add_up(far[0, :half], far_y), along_x)
    last_y = swap(add_up(near[1, half:], far_x[1]), along_y)
    first = add_up(near[0, :half], near_y, last_x)
    second = add_up(near[0, half:], far_x[0], last_y)
    columns = [first[k] for k in range(half)] + [second[k] for k in range(lines - half)]
    mixed = add_up(columns[0], *[swap(columns[k], k * along_z) for k in range(1, lines)])
    return mixed.T


def on_device(*args):
    tokens, expert_ids = args[0], args[2]
    experts, groups = lax.axis_size("seq"), lax.axis_size("rep")
    capacity = 2 * tokens.shape[0] * expert_ids.shape[1] // experts
    if capacity >= tokens.shape[0] and experts & (experts - 1) == 0 and experts > 3 and groups == 4:
        return dense(*args)
    return routed(*args, capacity)


def solution(mesh):
    placed = (
        P("seq", None),
        P(),
        P("seq", None),
        P("seq", None),
        P("seq", None, "rep"),
        P("seq", "rep"),
        P("seq", None, "rep"),
        P("seq", "rep"),
        P("seq", "rep", None),
        P("seq", "rep"),
    )
    return jax.shard_map(
        on_device, mesh=mesh, in_specs=placed, out_specs=P("seq", "rep"), check_vma=False
    )
```

```python
import functools

import jax
import jax.numpy as jnp
from jax import lax
from jax.experimental import pallas as pl
from jax.experimental.pallas import tpu as pltpu
from jax.sharding import PartitionSpec as P


def rms_normed(values, norm_gain, axis):
    values = values.astype(jnp.float32)
    scale = lax.rsqrt(jnp.mean(values * values, axis=axis, keepdims=True) + 1e-05)
    return (values * scale * norm_gain).astype(jnp.bfloat16)


def gated(gate_pre, up_pre):
    return (gate_pre * jax.nn.sigmoid(1.702 * gate_pre) * (up_pre + 1.0)).astype(jnp.bfloat16)


def routed(
    tokens,
    norm_gain,
    expert_ids,
    route_weights,
    gate_weight,
    gate_bias,
    up_weight,
    up_bias,
    down_weight,
    down_bias,
    capacity,
):
    tok_rows, features = tokens.shape
    per_token = expert_ids.shape[1]
    experts = lax.axis_size("seq")
    quarter = features // lax.axis_size("rep")
    normed = rms_normed(tokens, norm_gain, -1)
    flat_ids = expert_ids.reshape(-1)
    onehot = (flat_ids[:, None] == jnp.arange(experts, dtype=jnp.int32)[None, :]).astype(jnp.int32)
    before = jnp.cumsum(onehot, axis=0) - onehot
    slot_index = jnp.sum(before * onehot, axis=1)
    destination = flat_ids * capacity + slot_index
    owner_row = jnp.arange(tok_rows * per_token, dtype=jnp.int32) // per_token
    buffer = jnp.zeros((experts * capacity, features), jnp.bfloat16)
    buffer = buffer.at[destination].set(normed[owner_row])
    received = lax.all_to_all(
        buffer.reshape(experts, capacity, features), "seq", split_axis=0, concat_axis=0, tiled=True
    )
    in_rows = received.reshape(-1, features)
    gate_pre = jnp.dot(in_rows, gate_weight[0], preferred_element_type=jnp.float32) + gate_bias[0]
    up_pre = jnp.dot(in_rows, up_weight[0], preferred_element_type=jnp.float32) + up_bias[0]
    partial_value = jnp.dot(
        gated(gate_pre, up_pre), down_weight[0], preferred_element_type=jnp.float32
    ).astype(jnp.bfloat16)
    summed = lax.psum_scatter(
        partial_value.reshape(experts, capacity, features),
        "rep",
        scatter_dimension=2,
        tiled=True,
    ).astype(jnp.float32)
    expert_out = (summed + down_bias[0][None, None, :]).astype(jnp.bfloat16)
    returned = lax.all_to_all(expert_out, "seq", split_axis=0, concat_axis=0, tiled=True)
    picked = returned.reshape(-1, quarter)[destination].reshape(tok_rows, per_token, quarter)
    mixed = jnp.sum(route_weights[:, :, None] * picked.astype(jnp.float32), axis=1)
    return mixed.astype(jnp.bfloat16)


def round_up(number, step):
    return -(-number // step) * step


def add_up(*terms):
    total = terms[0].astype(jnp.float32)
    for term in terms[1:]:
        total = total + term.astype(jnp.float32)
    return total.astype(jnp.bfloat16)


def arrange_kernel(
    groups,
    gate_ref,
    up_ref,
    down_ref,
    gate_bias_ref,
    up_bias_ref,
    down_bias_ref,
    gate_up_out,
    down_out,
    bias_out,
    down_bias_out,
):
    features, hidden = gate_ref.shape
    quarter = features // groups
    hidden_pad, block = round_up(hidden, 128), round_up(quarter, 128)
    lanes = bias_out.shape[1]

    def padded(array, rows, columns):
        return jnp.pad(array, ((0, rows - array.shape[0]), (0, columns - array.shape[1])))

    def column(row, size):
        return jnp.broadcast_to(padded(row, 1, size), (lanes, size)).T

    for n, (weight, bias) in enumerate(((gate_ref, gate_bias_ref), (up_ref, up_bias_ref))):
        values = weight[...].astype(jnp.float32)
        rows = slice(n * hidden_pad, (n + 1) * hidden_pad)
        for q in range(groups):
            part = padded(values[q * quarter : (q + 1) * quarter], block, hidden_pad)
            gate_up_out[rows, q * block : (q + 1) * block] = part.T.astype(jnp.bfloat16)
        bias_out[rows] = column(bias[...], hidden_pad)
    values = padded(down_ref[...].astype(jnp.float32), hidden_pad, round_up(features, 128)).T
    for q in range(groups):
        part = padded(values[q * quarter : (q + 1) * quarter], block, hidden_pad)
        down_out[q * block : (q + 1) * block] = part.astype(jnp.bfloat16)
    down_bias_out[...] = column(down_bias_ref[...], block)


def arrange(groups, lanes, gate, up, down, gate_bias, up_bias, down_bias):
    features, hidden = gate.shape
    hidden_pad, block = round_up(hidden, 128), round_up(features // groups, 128)
    return pl.pallas_call(
        functools.partial(arrange_kernel, groups),
        out_shape=[
            jax.ShapeDtypeStruct((2 * hidden_pad, groups * block), jnp.bfloat16),
            jax.ShapeDtypeStruct((groups * block, hidden_pad), jnp.bfloat16),
            jax.ShapeDtypeStruct((2 * hidden_pad, lanes), jnp.float32),
            jax.ShapeDtypeStruct((block, lanes), jnp.float32),
        ],
        compiler_params=pltpu.CompilerParams(vmem_limit_bytes=40 * 2**20),
        cost_estimate=pl.CostEstimate(
            flops=0, bytes_accessed=8 * gate.size * 2, transcendentals=0
        ),
    )(gate, up, down, gate_bias, up_bias, down_bias)


def expert_kernel(
    quarter,
    per,
    place_ref,
    p0,
    p1,
    p2,
    p3,
    gate_up_ref,
    down_ref,
    bias_ref,
    down_bias_ref,
    keep_ref,
    send_ref,
    rows_ref,
    sums_ref,
):
    pieces = (p0, p1, p2, p3)
    count, piece_rows, lanes = p0.shape
    groups = len(pieces)
    block = gate_up_ref.shape[1] // groups
    hidden = gate_up_ref.shape[0] // 2
    rep, seq = place_ref[0], place_ref[1]

    @pl.when(pl.program_id(0) == 0)
    def _():
        rows_ref[...] = jnp.zeros_like(rows_ref)

    shares = [jnp.zeros((1, lanes), jnp.float32)] * count
    for k, piece in enumerate(pieces):
        source = rep ^ k
        row = lax.broadcasted_iota(jnp.int32, (piece_rows - quarter, lanes), 0)
        first = 3 * (seq - source * per)
        mine = (row >= first) & (row < first + 3)
        for j in range(count):
            values = piece[j]
            rows_ref[pl.ds(pl.multiple_of(source * block, block), piece_rows), j * lanes : (j + 1) * lanes] = values
            tail = values.astype(jnp.float32)[quarter:]
            shares[j] += jnp.sum(jnp.where(mine, tail, 0.0), axis=0, keepdims=True)
    wide = jnp.concatenate(shares, axis=1)
    both = jnp.dot(gate_up_ref[...], rows_ref[...], preferred_element_type=jnp.float32)
    both = both + jnp.concatenate([bias_ref[...]] * count, axis=1)
    activated = gated(both[:hidden], both[hidden:])
    sums_ref[...] = jnp.dot(down_ref[...], activated, preferred_element_type=jnp.float32)
    for k in range(groups):
        rows = sums_ref[pl.ds(pl.multiple_of((rep ^ k) * block, block), block), :]
        if k == 0:
            rows = rows + jnp.concatenate([down_bias_ref[...]] * count, axis=1)
        rows = (rows * wide).astype(jnp.bfloat16)
        target = send_ref if k % 2 else keep_ref
        for j in range(count):
            target[k // 2, j] = rows[:quarter, j * lanes : (j + 1) * lanes]


def run_expert(place, pieces, weights, quarter, per, count):
    chunks, piece_rows, lanes = pieces[0].shape
    gate_up, down = weights[0], weights[1]
    flops = 2 * chunks * lanes * (gate_up.size + down.size)
    out = jax.ShapeDtypeStruct((2, chunks, quarter, lanes), jnp.bfloat16)
    return pl.pallas_call(
        functools.partial(expert_kernel, quarter, per),
        grid_spec=pltpu.PrefetchScalarGridSpec(
            num_scalar_prefetch=1,
            grid=(chunks // count,),
            in_specs=[pl.BlockSpec((count, piece_rows, lanes), lambda i, place: (i, 0, 0))] * 4
            + [pl.BlockSpec(w.shape, lambda i, place: (0, 0)) for w in weights],
            out_specs=[pl.BlockSpec((2, count, quarter, lanes), lambda i, place: (0, i, 0, 0))] * 2,
            scratch_shapes=[
                pltpu.VMEM((gate_up.shape[1], count * lanes), jnp.bfloat16),
                pltpu.VMEM((down.shape[0], count * lanes), jnp.float32),
            ],
        ),
        out_shape=[out, out],
        compiler_params=pltpu.CompilerParams(vmem_limit_bytes=40 * 2**20),
        cost_estimate=pl.CostEstimate(
            flops=flops, bytes_accessed=2 * (gate_up.size + down.size), transcendentals=0
        ),
    )(place, *pieces, *weights)


def dense(
    tokens,
    norm_gain,
    expert_ids,
    route_weights,
    gate_weight,
    gate_bias,
    up_weight,
    up_bias,
    down_weight,
    down_bias,
):
    lanes, features = tokens.shape
    experts = lax.axis_size("seq")
    groups = lax.axis_size("rep")
    quarter = features // groups
    rep, seq = lax.axis_index("rep"), lax.axis_index("seq")
    devices = experts * groups
    lines = experts // 2
    half = lines // 2
    core, along_y, along_x, along_z = 1, 2, groups, 2 * groups

    def swap(array, step):
        return lax.ppermute(array, ("seq", "rep"), [(i, i ^ step) for i in range(devices)])

    per = -(-experts // groups)
    piece_rows = round_up(quarter + 3 * per, 16)
    tail = piece_rows - quarter
    chosen = expert_ids.T[None] == jnp.arange(experts, dtype=jnp.int32)[:, None, None]
    shares = jnp.sum(jnp.where(chosen, route_weights.T[None], 0.0), axis=1)
    high = lax.reduce_precision(shares, 8, 7)
    middle = lax.reduce_precision(shares - high, 8, 7)
    low = lax.reduce_precision(shares - high - middle, 8, 7)
    terms = jnp.stack([high, middle, low], axis=1).reshape(3 * experts, lanes)
    terms = jnp.pad(terms, ((0, 3 * per * groups - 3 * experts), (0, 0)))
    terms = lax.dynamic_slice_in_dim(terms, rep * 3 * per, 3 * per, 0).astype(jnp.bfloat16)
    values = tokens.T.astype(jnp.float32)
    scale = lax.rsqrt(jnp.mean(values * values, axis=0, keepdims=True) + 1e-05)
    own = lax.dynamic_slice_in_dim(tokens.T, rep * quarter, quarter, 0).astype(jnp.float32)
    gain = lax.dynamic_slice_in_dim(norm_gain, rep * quarter, quarter, 0)
    own = (own * scale * gain[:, None]).astype(jnp.bfloat16)
    own = jnp.concatenate([own, jnp.pad(terms, ((0, tail - 3 * per), (0, 0)))], axis=0)
    place = jnp.stack([rep, seq]).astype(jnp.int32)

    here = jnp.stack([own] + [swap(own, k * along_z) for k in range(1, lines)])
    from_x, from_y = swap(here, along_x), swap(here, along_y)
    here_core = swap(here, core)
    corner = jnp.concatenate(
        [swap(from_x[:half], along_y), swap(from_y[half:], along_x)], axis=0
    )
    from_y_core = swap(from_y, core)
    from_x_core = swap(from_x, core)
    corner_core = swap(corner, core)

    weights = arrange(
        groups, lanes, gate_weight[0], up_weight[0], down_weight[0], gate_bias, up_bias, down_bias
    )
    keep, send = run_expert(place, (here, here_core, from_y, from_y_core), weights, quarter, per, 2)
    near = add_up(keep, swap(send, core))
    near_y = swap(near[1, :half], along_y)
    keep, send = run_expert(
        place, (from_x, from_x_core, corner, corner_core), weights, quarter, per, 2
    )
    far = add_up(keep, swap(send, core))
    far_y = swap(far[1, :half], along_y)
    far_x = swap(far[:, half:], along_x)
    last_x = swap(add_up(far[0, :half], far_y), along_x)
    last_y = swap(add_up(near[1, half:], far_x[1]), along_y)
    first = add_up(near[0, :half], near_y, last_x)
    second = add_up(near[0, half:], far_x[0], last_y)
    columns = [first[k] for k in range(half)] + [second[k] for k in range(lines - half)]
    mixed = add_up(columns[0], *[swap(columns[k], k * along_z) for k in range(1, lines)])
    return mixed.T


def on_device(*args):
    tokens, expert_ids = args[0], args[2]
    experts, groups = lax.axis_size("seq"), lax.axis_size("rep")
    capacity = 2 * tokens.shape[0] * expert_ids.shape[1] // experts
    if capacity >= tokens.shape[0] and experts & (experts - 1) == 0 and experts > 3 and groups == 4:
        return dense(*args)
    return routed(*args, capacity)


def solution(mesh):
    placed = (
        P("seq", None),
        P(),
        P("seq", None),
        P("seq", None),
        P("seq", None, "rep"),
        P("seq", "rep"),
        P("seq", None, "rep"),
        P("seq", "rep"),
        P("seq", "rep", None),
        P("seq", "rep"),
    )
    return jax.shard_map(
        on_device, mesh=mesh, in_specs=placed, out_specs=P("seq", "rep"), check_vma=False
    )
```

```python
import functools

import jax
import jax.numpy as jnp
from jax import lax
from jax.experimental import pallas as pl
from jax.experimental.pallas import tpu as pltpu
from jax.sharding import PartitionSpec as P


def rms_normed(values, norm_gain, axis):
    values = values.astype(jnp.float32)
    scale = lax.rsqrt(jnp.mean(values * values, axis=axis, keepdims=True) + 1e-05)
    return (values * scale * norm_gain).astype(jnp.bfloat16)


def gated(gate_pre, up_pre):
    return (gate_pre * jax.nn.sigmoid(1.702 * gate_pre) * (up_pre + 1.0)).astype(jnp.bfloat16)


def routed(
    tokens,
    norm_gain,
    expert_ids,
    route_weights,
    gate_weight,
    gate_bias,
    up_weight,
    up_bias,
    down_weight,
    down_bias,
    capacity,
):
    tok_rows, features = tokens.shape
    per_token = expert_ids.shape[1]
    experts = lax.axis_size("seq")
    quarter = features // lax.axis_size("rep")
    normed = rms_normed(tokens, norm_gain, -1)
    flat_ids = expert_ids.reshape(-1)
    onehot = (flat_ids[:, None] == jnp.arange(experts, dtype=jnp.int32)[None, :]).astype(jnp.int32)
    before = jnp.cumsum(onehot, axis=0) - onehot
    slot_index = jnp.sum(before * onehot, axis=1)
    destination = flat_ids * capacity + slot_index
    owner_row = jnp.arange(tok_rows * per_token, dtype=jnp.int32) // per_token
    buffer = jnp.zeros((experts * capacity, features), jnp.bfloat16)
    buffer = buffer.at[destination].set(normed[owner_row])
    received = lax.all_to_all(
        buffer.reshape(experts, capacity, features), "seq", split_axis=0, concat_axis=0, tiled=True
    )
    in_rows = received.reshape(-1, features)
    gate_pre = jnp.dot(in_rows, gate_weight[0], preferred_element_type=jnp.float32) + gate_bias[0]
    up_pre = jnp.dot(in_rows, up_weight[0], preferred_element_type=jnp.float32) + up_bias[0]
    partial_value = jnp.dot(
        gated(gate_pre, up_pre), down_weight[0], preferred_element_type=jnp.float32
    ).astype(jnp.bfloat16)
    summed = lax.psum_scatter(
        partial_value.reshape(experts, capacity, features),
        "rep",
        scatter_dimension=2,
        tiled=True,
    ).astype(jnp.float32)
    expert_out = (summed + down_bias[0][None, None, :]).astype(jnp.bfloat16)
    returned = lax.all_to_all(expert_out, "seq", split_axis=0, concat_axis=0, tiled=True)
    picked = returned.reshape(-1, quarter)[destination].reshape(tok_rows, per_token, quarter)
    mixed = jnp.sum(route_weights[:, :, None] * picked.astype(jnp.float32), axis=1)
    return mixed.astype(jnp.bfloat16)


def round_up(number, step):
    return -(-number // step) * step


def add_up(*terms):
    total = terms[0].astype(jnp.float32)
    for term in terms[1:]:
        total = total + term.astype(jnp.float32)
    return total.astype(jnp.bfloat16)


def arrange_kernel(
    groups,
    gate_ref,
    up_ref,
    down_ref,
    gate_bias_ref,
    up_bias_ref,
    down_bias_ref,
    gate_up_out,
    down_out,
    bias_out,
    down_bias_out,
):
    features, hidden = gate_ref.shape
    quarter = features // groups
    hidden_pad, block = round_up(hidden, 128), round_up(quarter, 128)
    lanes = bias_out.shape[1]

    def padded(array, rows, columns):
        return jnp.pad(array, ((0, rows - array.shape[0]), (0, columns - array.shape[1])))

    def column(row, size):
        return jnp.broadcast_to(padded(row, 1, size), (lanes, size)).T

    for n, (weight, bias) in enumerate(((gate_ref, gate_bias_ref), (up_ref, up_bias_ref))):
        values = weight[...].astype(jnp.float32)
        rows = slice(n * hidden_pad, (n + 1) * hidden_pad)
        for q in range(groups):
            part = padded(values[q * quarter : (q + 1) * quarter], block, hidden_pad)
            gate_up_out[rows, q * block : (q + 1) * block] = part.T.astype(jnp.bfloat16)
        bias_out[rows] = column(bias[...], hidden_pad)
    values = padded(down_ref[...].astype(jnp.float32), hidden_pad, round_up(features, 128)).T
    for q in range(groups):
        part = padded(values[q * quarter : (q + 1) * quarter], block, hidden_pad)
        down_out[q * block : (q + 1) * block] = part.astype(jnp.bfloat16)
    down_bias_out[...] = column(down_bias_ref[...], block)


def arrange(groups, lanes, gate, up, down, gate_bias, up_bias, down_bias):
    features, hidden = gate.shape
    hidden_pad, block = round_up(hidden, 128), round_up(features // groups, 128)
    return pl.pallas_call(
        functools.partial(arrange_kernel, groups),
        out_shape=[
            jax.ShapeDtypeStruct((2 * hidden_pad, groups * block), jnp.bfloat16),
            jax.ShapeDtypeStruct((groups * block, hidden_pad), jnp.bfloat16),
            jax.ShapeDtypeStruct((2 * hidden_pad, lanes), jnp.float32),
            jax.ShapeDtypeStruct((block, lanes), jnp.float32),
        ],
        compiler_params=pltpu.CompilerParams(vmem_limit_bytes=40 * 2**20),
        cost_estimate=pl.CostEstimate(
            flops=0, bytes_accessed=8 * gate.size * 2, transcendentals=0
        ),
    )(gate, up, down, gate_bias, up_bias, down_bias)


def pieces_kernel(groups, per, experts, place_ref, tokens_ref, gain_ref, ids_ref, weights_ref, one_ref, near_ref, far_ref):
    features, lanes = tokens_ref.shape
    quarter = features // groups
    tail = one_ref.shape[0] - quarter
    rep = place_ref[0]
    values = tokens_ref[...].astype(jnp.float32)
    scale = lax.rsqrt(jnp.mean(values * values, axis=0, keepdims=True) + 1e-05)
    gain = jnp.broadcast_to(gain_ref[...], (lanes, features)).T
    normed = values * scale * gain
    row = lax.broadcasted_iota(jnp.int32, (tail, lanes), 0)
    chosen = lax.broadcasted_iota(jnp.int32, (round_up(experts, 8), lanes), 0)
    shares = jnp.zeros(chosen.shape, jnp.float32)
    for k in range(ids_ref.shape[0]):
        shares += jnp.where(ids_ref[k : k + 1] == chosen, weights_ref[k : k + 1], 0.0)
    terms = []
    for _ in range(3):
        term = shares.astype(jnp.bfloat16).astype(jnp.float32)
        terms.append(term)
        shares = shares - term
    for q in range(groups):
        rows = jnp.zeros((tail, lanes), jnp.float32)
        for n, term in enumerate(terms):
            for i in range(per):
                expert = q * per + i
                if expert < experts:
                    rows = jnp.where(row == n * per + i, term[expert : expert + 1], rows)
        piece = jnp.concatenate([normed[q * quarter : (q + 1) * quarter], rows], axis=0)
        piece = piece.astype(jnp.bfloat16)
        k = rep ^ q
        for side, target in enumerate((near_ref, far_ref)):

            @pl.when(k % 2 == side)
            def _(target=target, piece=piece, k=k):
                target[k // 2] = piece

        @pl.when(k == 0)
        def _(piece=piece):
            one_ref[...] = piece


def make_pieces(place, tokens, norm_gain, expert_ids, route_weights, groups, per, experts):
    features, lanes = tokens.shape
    rows = round_up(features // groups + 3 * per, 16)
    pair = jax.ShapeDtypeStruct((groups // 2, rows, lanes), jnp.bfloat16)
    whole = pl.BlockSpec(memory_space=pltpu.VMEM)
    return pl.pallas_call(
        functools.partial(pieces_kernel, groups, per, experts),
        in_specs=[pl.BlockSpec(memory_space=pltpu.SMEM)] + [whole] * 4,
        out_specs=[whole] * 3,
        out_shape=[jax.ShapeDtypeStruct((rows, lanes), jnp.bfloat16), pair, pair],
        compiler_params=pltpu.CompilerParams(vmem_limit_bytes=40 * 2**20),
    )(place, tokens, norm_gain, expert_ids, route_weights)


def expert_kernel(quarter, per, blocks, slots, *refs):
    groups = len(blocks[0])
    counted = 1 + max(at for block in blocks for at, _ in block)
    place_ref, arrays = refs[0], refs[1 : 1 + counted]
    gate_up_ref, down_ref, bias_ref, down_bias_ref, keep_ref, send_ref = refs[1 + counted : 7 + counted]
    scratch = refs[7 + counted :]
    _, piece_rows, lanes = arrays[0].shape
    size = gate_up_ref.shape[1] // groups
    hidden = gate_up_ref.shape[0] // 2
    rep, seq = place_ref[0], place_ref[1]
    halves = len(scratch) // 2
    count = len(blocks) // halves
    row = lax.broadcasted_iota(jnp.int32, (piece_rows - quarter, lanes), 0)
    for half in range(halves):
        rows_ref, sums_ref = scratch[half], scratch[halves + half]
        if size > piece_rows:
            for k in range(groups):
                rows_ref[k * size + piece_rows : (k + 1) * size, :] = jnp.zeros(
                    (size - piece_rows, count * lanes), jnp.bfloat16
                )
        shares = [jnp.zeros((1, lanes), jnp.float32)] * count
        for k in range(groups):
            source = rep ^ k
            at_row = pl.ds(pl.multiple_of(source * size, size), piece_rows)
            mine = (lax.rem(row, per) == seq - source * per) & (row < 3 * per)
            for j in range(count):
                at, index = blocks[half * count + j][k]
                values = arrays[at][index]
                rows_ref[at_row, j * lanes : (j + 1) * lanes] = values
                terms = values.astype(jnp.float32)[quarter:]
                shares[j] += jnp.sum(jnp.where(mine, terms, 0.0), axis=0, keepdims=True)
        wide = jnp.concatenate(shares, axis=1)
        both = jnp.dot(gate_up_ref[...], rows_ref[...], preferred_element_type=jnp.float32)
        both = both + jnp.concatenate([bias_ref[...]] * count, axis=1)
        activated = gated(both[:hidden], both[hidden:])
        sums_ref[...] = jnp.dot(down_ref[...], activated, preferred_element_type=jnp.float32)
        for k in range(groups):
            rows = sums_ref[pl.ds(pl.multiple_of((rep ^ k) * size, size), size), :]
            if k == 0:
                rows = rows + jnp.concatenate([down_bias_ref[...]] * count, axis=1)
            rows = (rows * wide).astype(jnp.bfloat16)
            target = send_ref if k % 2 else keep_ref
            for j in range(count):
                target[slots[half * count + j][k // 2]] = rows[:quarter, j * lanes : (j + 1) * lanes]


def run_expert(place, arrays, blocks, slots, weights, quarter, per, halves):
    lanes = arrays[0].shape[2]
    gate_up, down = weights[0], weights[1]
    tokens = len(blocks) * lanes
    whole = pl.BlockSpec(memory_space=pltpu.VMEM)
    out = jax.ShapeDtypeStruct((2 * len(blocks), quarter, lanes), jnp.bfloat16)
    columns = tokens // halves
    return pl.pallas_call(
        functools.partial(expert_kernel, quarter, per, blocks, slots),
        in_specs=[pl.BlockSpec(memory_space=pltpu.SMEM)] + [whole] * (len(arrays) + len(weights)),
        out_specs=[whole, whole],
        out_shape=[out, out],
        scratch_shapes=[pltpu.VMEM((gate_up.shape[1], columns), jnp.bfloat16)] * halves
        + [pltpu.VMEM((down.shape[0], columns), jnp.float32)] * halves,
        compiler_params=pltpu.CompilerParams(vmem_limit_bytes=40 * 2**20),
        cost_estimate=pl.CostEstimate(
            flops=4 * tokens * (gate_up.size + down.size),
            bytes_accessed=2 * (gate_up.size + down.size),
            transcendentals=0,
        ),
    )(place, *arrays, *weights)


def dense(
    tokens,
    norm_gain,
    expert_ids,
    route_weights,
    gate_weight,
    gate_bias,
    up_weight,
    up_bias,
    down_weight,
    down_bias,
):
    lanes, features = tokens.shape
    experts = lax.axis_size("seq")
    groups = lax.axis_size("rep")
    quarter = features // groups
    rep, seq = lax.axis_index("rep"), lax.axis_index("seq")
    devices = experts * groups
    core, along_y, along_x, along_z = 1, 2, groups, 2 * groups

    def swap(array, step):
        return lax.ppermute(array, ("seq", "rep"), [(i, i ^ step) for i in range(devices)])

    per = -(-experts // groups)
    place = jnp.stack([rep, seq]).astype(jnp.int32)
    one, near, far = make_pieces(
        place, tokens.T, norm_gain[None], expert_ids.T, route_weights.T, groups, per, experts
    )
    z_2, z_3 = swap(one, 2 * along_z), swap(one, 3 * along_z)
    x_0 = swap(near, along_x)
    z_1 = swap(near, along_z)
    weights = arrange(
        groups, lanes, gate_weight[0], up_weight[0], down_weight[0], gate_bias, up_bias, down_bias
    )
    z_high = jnp.stack([z_2, z_3])
    x_high, y_high = swap(z_high, along_x), swap(z_high, along_y)
    x_1 = swap(z_1, along_x)
    corner = swap(x_high, along_y)

    low = (near, far, x_0, swap(x_0, core), z_1, swap(z_1, core), x_1, swap(x_1, core))
    high = (z_high, swap(z_high, core), y_high, swap(y_high, core))
    high = high + (x_high, swap(x_high, core), corner, swap(corner, core))
    low_blocks = [[(2 * n + k % 2, k // 2) for k in range(groups)] for n in range(4)]
    high_blocks = [
        [(4 * x + k, line) for k in range(groups)] for line in range(2) for x in range(2)
    ]
    slots = ((4, 0), (5, 1), (6, 7), (2, 3))

    def plane(keep, send):
        got = swap(send, core)
        first_y = swap(add_up(keep[0:2], got[0:2]), along_y)
        first_x = swap(add_up(keep[2:4], got[2:4]), along_x)
        last_x = swap(add_up(keep[5], got[5], first_y[1]), along_x)
        last_y = swap(add_up(keep[7], got[7], first_x[1]), along_y)
        return (
            add_up(keep[4], got[4], first_y[0], last_x),
            add_up(keep[6], got[6], first_x[0], last_y),
        )

    keep_low, send_low = run_expert(place, low, low_blocks, slots, weights, quarter, per, 2)
    keep_high, send_high = run_expert(place, high, high_blocks, slots, weights, quarter, per, 2)
    line_2, line_3 = plane(keep_high, send_high)
    line_0, line_1 = plane(keep_low, send_low)
    mixed = add_up(
        line_0, swap(line_1, along_z), swap(line_2, 2 * along_z), swap(line_3, 3 * along_z)
    )
    return mixed.T


def on_device(*args):
    tokens, expert_ids = args[0], args[2]
    experts, groups = lax.axis_size("seq"), lax.axis_size("rep")
    capacity = 2 * tokens.shape[0] * expert_ids.shape[1] // experts
    if capacity >= tokens.shape[0] and experts == 2 * groups and groups == 4:
        return dense(*args)
    return routed(*args, capacity)


def solution(mesh):
    placed = (
        P("seq", None),
        P(),
        P("seq", None),
        P("seq", None),
        P("seq", None, "rep"),
        P("seq", "rep"),
        P("seq", None, "rep"),
        P("seq", "rep"),
        P("seq", "rep", None),
        P("seq", "rep"),
    )
    return jax.shard_map(
        on_device, mesh=mesh, in_specs=placed, out_specs=P("seq", "rep"), check_vma=False
    )
```

```python
import functools

import jax
import jax.numpy as jnp
from jax import lax
from jax.experimental import pallas as pl
from jax.experimental.pallas import tpu as pltpu
from jax.sharding import PartitionSpec as P


def rms_normed(values, norm_gain, axis):
    values = values.astype(jnp.float32)
    scale = lax.rsqrt(jnp.mean(values * values, axis=axis, keepdims=True) + 1e-05)
    return (values * scale * norm_gain).astype(jnp.bfloat16)


def gated(gate_pre, up_pre):
    return (gate_pre * jax.nn.sigmoid(1.702 * gate_pre) * (up_pre + 1.0)).astype(jnp.bfloat16)


def routed(
    tokens,
    norm_gain,
    expert_ids,
    route_weights,
    gate_weight,
    gate_bias,
    up_weight,
    up_bias,
    down_weight,
    down_bias,
    capacity,
):
    tok_rows, features = tokens.shape
    per_token = expert_ids.shape[1]
    experts = lax.axis_size("seq")
    quarter = features // lax.axis_size("rep")
    normed = rms_normed(tokens, norm_gain, -1)
    flat_ids = expert_ids.reshape(-1)
    onehot = (flat_ids[:, None] == jnp.arange(experts, dtype=jnp.int32)[None, :]).astype(jnp.int32)
    before = jnp.cumsum(onehot, axis=0) - onehot
    slot_index = jnp.sum(before * onehot, axis=1)
    destination = flat_ids * capacity + slot_index
    owner_row = jnp.arange(tok_rows * per_token, dtype=jnp.int32) // per_token
    buffer = jnp.zeros((experts * capacity, features), jnp.bfloat16)
    buffer = buffer.at[destination].set(normed[owner_row])
    received = lax.all_to_all(
        buffer.reshape(experts, capacity, features), "seq", split_axis=0, concat_axis=0, tiled=True
    )
    in_rows = received.reshape(-1, features)
    gate_pre = jnp.dot(in_rows, gate_weight[0], preferred_element_type=jnp.float32) + gate_bias[0]
    up_pre = jnp.dot(in_rows, up_weight[0], preferred_element_type=jnp.float32) + up_bias[0]
    partial_value = jnp.dot(
        gated(gate_pre, up_pre), down_weight[0], preferred_element_type=jnp.float32
    ).astype(jnp.bfloat16)
    summed = lax.psum_scatter(
        partial_value.reshape(experts, capacity, features),
        "rep",
        scatter_dimension=2,
        tiled=True,
    ).astype(jnp.float32)
    expert_out = (summed + down_bias[0][None, None, :]).astype(jnp.bfloat16)
    returned = lax.all_to_all(expert_out, "seq", split_axis=0, concat_axis=0, tiled=True)
    picked = returned.reshape(-1, quarter)[destination].reshape(tok_rows, per_token, quarter)
    mixed = jnp.sum(route_weights[:, :, None] * picked.astype(jnp.float32), axis=1)
    return mixed.astype(jnp.bfloat16)


tied = lax.optimization_barrier


def round_up(number, step):
    return -(-number // step) * step


def add_up(*terms):
    total = terms[0].astype(jnp.float32)
    for term in terms[1:]:
        total = total + term.astype(jnp.float32)
    return total.astype(jnp.bfloat16)


def arrange_kernel(groups, *refs):
    gate_up_out, down_out, bias_out, down_bias_out = refs[6:10]
    gate_ref, up_ref, down_ref, gate_bias_ref, up_bias_ref, down_bias_ref = refs[10:16]
    fetch(refs[:6], refs[10:16], refs[16])
    features, hidden = gate_ref.shape
    quarter = features // groups
    hidden_pad, block = round_up(hidden, 128), round_up(quarter, 128)
    lanes = bias_out.shape[1]

    def padded(array, rows, columns):
        return jnp.pad(array, ((0, rows - array.shape[0]), (0, columns - array.shape[1])))

    def column(row, size):
        return jnp.broadcast_to(padded(row, 1, size), (lanes, size)).T

    for n, (weight, bias) in enumerate(((gate_ref, gate_bias_ref), (up_ref, up_bias_ref))):
        values = weight[...].astype(jnp.float32)
        rows = slice(n * hidden_pad, (n + 1) * hidden_pad)
        for q in range(groups):
            part = padded(values[q * quarter : (q + 1) * quarter], block, hidden_pad)
            gate_up_out[rows, q * block : (q + 1) * block] = part.T.astype(jnp.bfloat16)
        bias_out[rows] = column(bias[...], hidden_pad)
    values = padded(down_ref[...].astype(jnp.float32), hidden_pad, round_up(features, 128)).T
    for q in range(groups):
        part = padded(values[q * quarter : (q + 1) * quarter], block, hidden_pad)
        down_out[q * block : (q + 1) * block] = part.astype(jnp.bfloat16)
    down_bias_out[...] = column(down_bias_ref[...], block)


def arrange(groups, lanes, gate, up, down, gate_bias, up_bias, down_bias):
    features, hidden = gate.shape
    hidden_pad, block = round_up(hidden, 128), round_up(features // groups, 128)
    arrays = (gate, up, down, gate_bias, up_bias, down_bias)
    return pl.pallas_call(
        functools.partial(arrange_kernel, groups),
        in_specs=[pl.BlockSpec(memory_space=pltpu.HBM)] * len(arrays),
        out_specs=[pl.BlockSpec(memory_space=pltpu.VMEM)] * 4,
        scratch_shapes=[pltpu.VMEM(a.shape, a.dtype) for a in arrays]
        + [pltpu.SemaphoreType.DMA((len(arrays),))],
        out_shape=[
            jax.ShapeDtypeStruct((2 * hidden_pad, groups * block), jnp.bfloat16),
            jax.ShapeDtypeStruct((groups * block, hidden_pad), jnp.bfloat16),
            jax.ShapeDtypeStruct((2 * hidden_pad, lanes), jnp.float32),
            jax.ShapeDtypeStruct((block, lanes), jnp.float32),
        ],
        compiler_params=pltpu.CompilerParams(vmem_limit_bytes=40 * 2**20),
        cost_estimate=pl.CostEstimate(
            flops=0, bytes_accessed=8 * gate.size * 2, transcendentals=0
        ),
    )(*arrays)


def fetch(sources, targets, sems):
    copies = [
        pltpu.make_async_copy(source, target, sems.at[n])
        for n, (source, target) in enumerate(zip(sources, targets))
    ]
    for copy in copies:
        copy.start()
    for copy in copies:
        copy.wait()


def pieces_kernel(groups, per, experts, place_ref, *refs):
    sources, (one_ref, near_ref, far_ref) = refs[:4], refs[4:7]
    tokens_ref, gain_ref, ids_ref, weights_ref = refs[7:11]
    fetch(sources, refs[7:11], refs[11])
    features, lanes = tokens_ref.shape
    quarter = features // groups
    tail = one_ref.shape[0] - quarter
    rep = place_ref[0]
    values = tokens_ref[...].astype(jnp.float32)
    scale = lax.rsqrt(jnp.mean(values * values, axis=0, keepdims=True) + 1e-05)
    gain = jnp.broadcast_to(gain_ref[...].reshape(1, features), (lanes, features)).T
    normed = values * scale * gain
    row = lax.broadcasted_iota(jnp.int32, (tail, lanes), 0)
    chosen = lax.broadcasted_iota(jnp.int32, (round_up(experts, 8), lanes), 0)
    shares = jnp.zeros(chosen.shape, jnp.float32)
    for k in range(ids_ref.shape[0]):
        shares += jnp.where(ids_ref[k : k + 1] == chosen, weights_ref[k : k + 1], 0.0)
    terms = []
    for _ in range(3):
        term = shares.astype(jnp.bfloat16).astype(jnp.float32)
        terms.append(term)
        shares = shares - term
    for q in range(groups):
        rows = jnp.zeros((tail, lanes), jnp.float32)
        for n, term in enumerate(terms):
            for i in range(per):
                expert = q * per + i
                if expert < experts:
                    rows = jnp.where(row == n * per + i, term[expert : expert + 1], rows)
        piece = jnp.concatenate([normed[q * quarter : (q + 1) * quarter], rows], axis=0)
        piece = piece.astype(jnp.bfloat16)
        k = rep ^ q
        for side, target in enumerate((near_ref, far_ref)):

            @pl.when(k % 2 == side)
            def _(target=target, piece=piece, k=k):
                target[k // 2] = piece

        @pl.when(k == 0)
        def _(piece=piece):
            one_ref[...] = piece


def make_pieces(place, tokens, norm_gain, expert_ids, route_weights, groups, per, experts):
    features, lanes = tokens.shape
    rows = round_up(features // groups + 3 * per, 16)
    pair = jax.ShapeDtypeStruct((groups // 2, rows, lanes), jnp.bfloat16)
    arrays = (tokens, norm_gain, expert_ids, route_weights)
    return pl.pallas_call(
        functools.partial(pieces_kernel, groups, per, experts),
        in_specs=[pl.BlockSpec(memory_space=pltpu.SMEM)] + [pl.BlockSpec(memory_space=pltpu.HBM)] * 4,
        out_specs=[pl.BlockSpec(memory_space=pltpu.VMEM)] * 3,
        out_shape=[jax.ShapeDtypeStruct((rows, lanes), jnp.bfloat16), pair, pair],
        scratch_shapes=[pltpu.VMEM(a.shape, a.dtype) for a in arrays]
        + [pltpu.SemaphoreType.DMA((len(arrays),))],
        compiler_params=pltpu.CompilerParams(vmem_limit_bytes=40 * 2**20),
    )(place, *arrays)


def expert_kernel(quarter, per, blocks, slots, *refs):
    groups = len(blocks[0])
    counted = 1 + max(at for block in blocks for at, _ in block)
    place_ref, arrays = refs[0], refs[1 : 1 + counted]
    gate_up_ref, down_ref, bias_ref, down_bias_ref, keep_ref, send_ref = refs[1 + counted : 7 + counted]
    scratch = refs[7 + counted :]
    _, piece_rows, lanes = arrays[0].shape
    size = gate_up_ref.shape[1] // groups
    hidden = gate_up_ref.shape[0] // 2
    rep, seq = place_ref[0], place_ref[1]
    halves = len(scratch)
    count = len(blocks) // halves
    row = lax.broadcasted_iota(jnp.int32, (piece_rows - quarter, lanes), 0)
    for half in range(halves):
        rows_ref = scratch[half]
        if size > piece_rows:
            for k in range(groups):
                rows_ref[k * size + piece_rows : (k + 1) * size, :] = jnp.zeros(
                    (size - piece_rows, count * lanes), jnp.bfloat16
                )
        shares = [jnp.zeros((1, lanes), jnp.float32)] * count
        for k in range(groups):
            source = rep ^ k
            at_row = pl.ds(pl.multiple_of(source * size, size), piece_rows)
            mine = (lax.rem(row, per) == seq - source * per) & (row < 3 * per)
            for j in range(count):
                at, index = blocks[half * count + j][k]
                values = arrays[at][index]
                rows_ref[at_row, j * lanes : (j + 1) * lanes] = values
                terms = values.astype(jnp.float32)[quarter:]
                shares[j] += jnp.sum(jnp.where(mine, terms, 0.0), axis=0, keepdims=True)
        wide = jnp.concatenate(shares, axis=1)
        both = jnp.dot(gate_up_ref[...], rows_ref[...], preferred_element_type=jnp.float32)
        both = both + jnp.concatenate([bias_ref[...]] * count, axis=1)
        activated = gated(both[:hidden], both[hidden:])
        for k in range(groups):
            own_rows = down_ref[pl.ds(pl.multiple_of((rep ^ k) * size, size), size), :]
            rows = jnp.dot(own_rows, activated, preferred_element_type=jnp.float32)
            if k == 0:
                rows = rows + jnp.concatenate([down_bias_ref[...]] * count, axis=1)
            rows = (rows * wide).astype(jnp.bfloat16)
            target = send_ref if k % 2 else keep_ref
            for j in range(count):
                target[slots[half * count + j][k // 2]] = rows[:quarter, j * lanes : (j + 1) * lanes]


def run_expert(place, arrays, blocks, slots, weights, sizes, halves):
    quarter, per = sizes
    lanes = arrays[0].shape[2]
    gate_up, down = weights[0], weights[1]
    tokens = len(blocks) * lanes
    whole = pl.BlockSpec(memory_space=pltpu.VMEM)
    out = jax.ShapeDtypeStruct((2 * len(blocks), quarter, lanes), jnp.bfloat16)
    columns = tokens // halves
    return pl.pallas_call(
        functools.partial(expert_kernel, quarter, per, blocks, slots),
        in_specs=[pl.BlockSpec(memory_space=pltpu.SMEM)] + [whole] * (len(arrays) + len(weights)),
        out_specs=[whole, whole],
        out_shape=[out, out],
        scratch_shapes=[pltpu.VMEM((gate_up.shape[1], columns), jnp.bfloat16)] * halves,
        compiler_params=pltpu.CompilerParams(vmem_limit_bytes=40 * 2**20),
        cost_estimate=pl.CostEstimate(
            flops=4 * tokens * (gate_up.size + down.size),
            bytes_accessed=2 * (gate_up.size + down.size),
            transcendentals=0,
        ),
    )(place, *arrays, *weights)


def dense(
    tokens,
    norm_gain,
    expert_ids,
    route_weights,
    gate_weight,
    gate_bias,
    up_weight,
    up_bias,
    down_weight,
    down_bias,
):
    lanes, features = tokens.shape
    experts = lax.axis_size("seq")
    groups = lax.axis_size("rep")
    quarter = features // groups
    rep, seq = lax.axis_index("rep"), lax.axis_index("seq")
    devices = experts * groups
    core, along_y, along_x, along_z = 1, 2, groups, 2 * groups

    def swap(array, step):
        return lax.ppermute(array, ("seq", "rep"), [(i, i ^ step) for i in range(devices)])

    per = -(-experts // groups)
    place = jnp.stack([rep, seq]).astype(jnp.int32)
    one, near, far = make_pieces(
        place, tokens.T, norm_gain, expert_ids.T, route_weights.T, groups, per, experts
    )
    z_2, z_3 = swap(one, 2 * along_z), swap(one, 3 * along_z)
    x_0 = swap(near, along_x)
    z_1 = swap(near, along_z)
    weights = arrange(
        groups, lanes, gate_weight[0], up_weight[0], down_weight[0], gate_bias, up_bias, down_bias
    )
    z_2, z_3, weights = tied((z_2, z_3, weights))
    z_high = jnp.stack([z_2, z_3])
    x_high, y_high = swap(z_high, along_x), swap(z_high, along_y)
    z_1, x_high, y_high = tied((z_1, x_high, y_high))
    corner = swap(x_high, along_y)
    x_1 = swap(z_1, along_x)

    def pairs(first):
        return [[(first + 2 * x + k % 2, k // 2) for k in range(groups)] for x in range(2)]

    slots_a, slots_b = ((2, 0), (3, 1)), ((2, 3), (0, 1))
    high = (z_high, swap(z_high, core), y_high, swap(y_high, core))
    high = high + (x_high, swap(x_high, core), corner, swap(corner, core))
    blocks = [[(4 * x + k, line) for k in range(groups)] for line in range(2) for x in range(2)]
    slots = slots_a + tuple((4 + i, 4 + j) for i, j in slots_b)
    sizes = (quarter, per)
    keep_0, send_0 = run_expert(
        place, (near, far, x_0, swap(x_0, core)), pairs(0), slots_a, weights, sizes, 1
    )
    keep_high, send_high = run_expert(place, high, blocks, slots, weights, sizes, 2)
    got_0 = swap(send_0, core)
    got = swap(send_high, core)
    near_1 = (z_1, swap(z_1, core), x_1, swap(x_1, core))
    got, near_1 = tied((got, near_1))
    keep_1, send_1 = run_expert(place, near_1, pairs(0), slots_b, weights, sizes, 1)
    keep_0, got_0, keep_1, send_1 = tied((keep_0, got_0, keep_1, send_1))

    def plane(keep_a, got_a, keep_b, got_b):
        first_y = swap(add_up(keep_a[0:2], got_a[0:2]), along_y)
        first_x = swap(add_up(keep_b[0:2], got_b[0:2]), along_x)
        last_x = swap(add_up(keep_a[3], got_a[3], first_y[1]), along_x)
        last_y = swap(add_up(keep_b[3], got_b[3], first_x[1]), along_y)
        return (
            add_up(keep_a[2], got_a[2], first_y[0], last_x),
            add_up(keep_b[2], got_b[2], first_x[0], last_y),
        )

    line_2, line_3 = plane(keep_high[:4], got[:4], keep_high[4:], got[4:])
    line_0, line_1 = plane(keep_0, got_0, keep_1, swap(send_1, core))
    mixed = add_up(
        line_0, swap(line_1, along_z), swap(line_2, 2 * along_z), swap(line_3, 3 * along_z)
    )
    return mixed.T


def on_device(*args):
    tokens, expert_ids = args[0], args[2]
    experts, groups = lax.axis_size("seq"), lax.axis_size("rep")
    capacity = 2 * tokens.shape[0] * expert_ids.shape[1] // experts
    if capacity >= tokens.shape[0] and experts == 2 * groups and groups == 4:
        return dense(*args)
    return routed(*args, capacity)


def solution(mesh):
    placed = (
        P("seq", None),
        P(),
        P("seq", None),
        P("seq", None),
        P("seq", None, "rep"),
        P("seq", "rep"),
        P("seq", None, "rep"),
        P("seq", "rep"),
        P("seq", "rep", None),
        P("seq", "rep"),
    )
    return jax.shard_map(
        on_device, mesh=mesh, in_specs=placed, out_specs=P("seq", "rep"), check_vma=False
    )
```

```python
import functools

import jax
import jax.numpy as jnp
from jax import lax
from jax.experimental import pallas as pl
from jax.experimental.pallas import tpu as pltpu
from jax.sharding import PartitionSpec as P


def rms_normed(values, norm_gain, axis):
    values = values.astype(jnp.float32)
    scale = lax.rsqrt(jnp.mean(values * values, axis=axis, keepdims=True) + 1e-05)
    return (values * scale * norm_gain).astype(jnp.bfloat16)


def gated(gate_pre, up_pre):
    return (gate_pre * jax.nn.sigmoid(1.702 * gate_pre) * (up_pre + 1.0)).astype(jnp.bfloat16)


def routed(
    tokens,
    norm_gain,
    expert_ids,
    route_weights,
    gate_weight,
    gate_bias,
    up_weight,
    up_bias,
    down_weight,
    down_bias,
    capacity,
):
    tok_rows, features = tokens.shape
    per_token = expert_ids.shape[1]
    experts = lax.axis_size("seq")
    quarter = features // lax.axis_size("rep")
    normed = rms_normed(tokens, norm_gain, -1)
    flat_ids = expert_ids.reshape(-1)
    onehot = (flat_ids[:, None] == jnp.arange(experts, dtype=jnp.int32)[None, :]).astype(jnp.int32)
    before = jnp.cumsum(onehot, axis=0) - onehot
    slot_index = jnp.sum(before * onehot, axis=1)
    destination = flat_ids * capacity + slot_index
    owner_row = jnp.arange(tok_rows * per_token, dtype=jnp.int32) // per_token
    buffer = jnp.zeros((experts * capacity, features), jnp.bfloat16)
    buffer = buffer.at[destination].set(normed[owner_row])
    received = lax.all_to_all(
        buffer.reshape(experts, capacity, features), "seq", split_axis=0, concat_axis=0, tiled=True
    )
    in_rows = received.reshape(-1, features)
    gate_pre = jnp.dot(in_rows, gate_weight[0], preferred_element_type=jnp.float32) + gate_bias[0]
    up_pre = jnp.dot(in_rows, up_weight[0], preferred_element_type=jnp.float32) + up_bias[0]
    partial_value = jnp.dot(
        gated(gate_pre, up_pre), down_weight[0], preferred_element_type=jnp.float32
    ).astype(jnp.bfloat16)
    summed = lax.psum_scatter(
        partial_value.reshape(experts, capacity, features),
        "rep",
        scatter_dimension=2,
        tiled=True,
    ).astype(jnp.float32)
    expert_out = (summed + down_bias[0][None, None, :]).astype(jnp.bfloat16)
    returned = lax.all_to_all(expert_out, "seq", split_axis=0, concat_axis=0, tiled=True)
    picked = returned.reshape(-1, quarter)[destination].reshape(tok_rows, per_token, quarter)
    mixed = jnp.sum(route_weights[:, :, None] * picked.astype(jnp.float32), axis=1)
    return mixed.astype(jnp.bfloat16)


tied = lax.optimization_barrier


def round_up(number, step):
    return -(-number // step) * step


def add_up(*terms):
    total = terms[0].astype(jnp.float32)
    for term in terms[1:]:
        total = total + term.astype(jnp.float32)
    return total.astype(jnp.bfloat16)


def padded(array, rows, columns):
    return jnp.pad(array, ((0, rows - array.shape[0]), (0, columns - array.shape[1])))


def column(row, size, lanes):
    return jnp.broadcast_to(padded(row, 1, size), (lanes, size)).T


def inward_kernel(groups, gate_ref, up_ref, biases_ref, weight_out, bias_out):
    features, hidden = gate_ref.shape
    quarter = features // groups
    hidden_pad, size = round_up(hidden, 128), round_up(quarter, 128)
    for n, weight in enumerate((gate_ref, up_ref)):
        values = weight[...].astype(jnp.float32)
        rows = slice(n * hidden_pad, (n + 1) * hidden_pad)
        for q in range(groups):
            part = padded(values[q * quarter : (q + 1) * quarter], size, hidden_pad)
            weight_out[rows, q * size : (q + 1) * size] = part.T.astype(jnp.bfloat16)
        bias_out[rows] = column(biases_ref[n : n + 1], hidden_pad, bias_out.shape[1])


def outward_kernel(groups, down_ref, biases_ref, weight_out, bias_out):
    hidden, features = down_ref.shape
    quarter = features // groups
    hidden_pad, size = round_up(hidden, 128), round_up(quarter, 128)
    values = padded(down_ref[...].astype(jnp.float32), hidden_pad, round_up(features, 128)).T
    for q in range(groups):
        part = padded(values[q * quarter : (q + 1) * quarter], size, hidden_pad)
        weight_out[q * size : (q + 1) * size] = part.astype(jnp.bfloat16)
    bias_out[...] = column(biases_ref[2:3], size, bias_out.shape[1])


def arrange(kernel, groups, lanes, arrays, shape, bias_rows):
    return pl.pallas_call(
        functools.partial(kernel, groups),
        out_shape=[
            jax.ShapeDtypeStruct(shape, jnp.bfloat16),
            jax.ShapeDtypeStruct((bias_rows, lanes), jnp.float32),
        ],
        compiler_params=pltpu.CompilerParams(vmem_limit_bytes=40 * 2**20),
        cost_estimate=pl.CostEstimate(
            flops=0, bytes_accessed=16 * arrays[0].size, transcendentals=0
        ),
    )(*arrays)


def fetch(sources, targets, sems):
    copies = [
        pltpu.make_async_copy(source, target, sems.at[n])
        for n, (source, target) in enumerate(zip(sources, targets))
    ]
    for copy in copies:
        copy.start()
    for copy in copies:
        copy.wait()


def pieces_kernel(groups, per, experts, place_ref, *refs):
    sources, (one_ref, near_ref, far_ref) = refs[:4], refs[4:7]
    tokens_ref, gain_ref, ids_ref, weights_ref = refs[7:11]
    fetch(sources, refs[7:11], refs[11])
    features, lanes = tokens_ref.shape
    quarter = features // groups
    tail = one_ref.shape[0] - quarter
    rep = place_ref[0]
    values = tokens_ref[...].astype(jnp.float32)
    scale = lax.rsqrt(jnp.mean(values * values, axis=0, keepdims=True) + 1e-05)
    gain = jnp.broadcast_to(gain_ref[...].reshape(1, features), (lanes, features)).T
    normed = values * scale * gain
    row = lax.broadcasted_iota(jnp.int32, (tail, lanes), 0)
    chosen = lax.broadcasted_iota(jnp.int32, (round_up(experts, 8), lanes), 0)
    shares = jnp.zeros(chosen.shape, jnp.float32)
    for k in range(ids_ref.shape[0]):
        shares += jnp.where(ids_ref[k : k + 1] == chosen, weights_ref[k : k + 1], 0.0)
    terms = []
    for _ in range(3):
        term = shares.astype(jnp.bfloat16).astype(jnp.float32)
        terms.append(term)
        shares = shares - term
    for q in range(groups):
        rows = jnp.zeros((tail, lanes), jnp.float32)
        for n, term in enumerate(terms):
            for i in range(per):
                expert = q * per + i
                if expert < experts:
                    rows = jnp.where(row == n * per + i, term[expert : expert + 1], rows)
        piece = jnp.concatenate([normed[q * quarter : (q + 1) * quarter], rows], axis=0)
        piece = piece.astype(jnp.bfloat16)
        k = rep ^ q
        for side, target in enumerate((near_ref, far_ref)):

            @pl.when(k % 2 == side)
            def _(target=target, piece=piece, k=k):
                target[k // 2] = piece

        @pl.when(k == 0)
        def _(piece=piece):
            one_ref[...] = piece


def make_pieces(place, tokens, norm_gain, expert_ids, route_weights, groups, per, experts):
    features, lanes = tokens.shape
    rows = round_up(features // groups + 3 * per, 16)
    pair = jax.ShapeDtypeStruct((groups // 2, rows, lanes), jnp.bfloat16)
    arrays = (tokens, norm_gain, expert_ids, route_weights)
    return pl.pallas_call(
        functools.partial(pieces_kernel, groups, per, experts),
        in_specs=[pl.BlockSpec(memory_space=pltpu.SMEM)] + [pl.BlockSpec(memory_space=pltpu.HBM)] * 4,
        out_specs=[pl.BlockSpec(memory_space=pltpu.VMEM)] * 3,
        out_shape=[jax.ShapeDtypeStruct((rows, lanes), jnp.bfloat16), pair, pair],
        scratch_shapes=[pltpu.VMEM(a.shape, a.dtype) for a in arrays]
        + [pltpu.SemaphoreType.DMA((len(arrays),))],
        compiler_params=pltpu.CompilerParams(vmem_limit_bytes=60 * 2**20),
    )(place, *arrays)


def expert_kernel(quarter, per, blocks, slots, *refs):
    groups = len(blocks[0])
    counted = 1 + max(at for block in blocks for at, _ in block)
    place_ref, arrays = refs[0], refs[1 : 1 + counted]
    gate_up_ref, bias_ref, down_ref, down_bias_ref, keep_ref, send_ref = refs[1 + counted : 7 + counted]
    scratch = refs[7 + counted :]
    _, piece_rows, lanes = arrays[0].shape
    size = gate_up_ref.shape[1] // groups
    hidden = gate_up_ref.shape[0] // 2
    rep, seq = place_ref[0], place_ref[1]
    halves = len(scratch)
    count = len(blocks) // halves
    row = lax.broadcasted_iota(jnp.int32, (piece_rows - quarter, lanes), 0)
    for half in range(halves):
        rows_ref = scratch[half]
        if size > piece_rows:
            for k in range(groups):
                rows_ref[k * size + piece_rows : (k + 1) * size, :] = jnp.zeros(
                    (size - piece_rows, count * lanes), jnp.bfloat16
                )
        shares = [jnp.zeros((1, lanes), jnp.float32)] * count
        for k in range(groups):
            source = rep ^ k
            at_row = pl.ds(pl.multiple_of(source * size, size), piece_rows)
            mine = (lax.rem(row, per) == seq - source * per) & (row < 3 * per)
            for j in range(count):
                at, index = blocks[half * count + j][k]
                values = arrays[at][index]
                rows_ref[at_row, j * lanes : (j + 1) * lanes] = values
                terms = values.astype(jnp.float32)[quarter:]
                shares[j] += jnp.sum(jnp.where(mine, terms, 0.0), axis=0, keepdims=True)
        wide = jnp.concatenate(shares, axis=1)
        both = jnp.dot(gate_up_ref[...], rows_ref[...], preferred_element_type=jnp.float32)
        both = both + jnp.concatenate([bias_ref[...]] * count, axis=1)
        activated = gated(both[:hidden], both[hidden:])
        for k in range(groups):
            own_rows = down_ref[pl.ds(pl.multiple_of((rep ^ k) * size, size), size), :]
            rows = jnp.dot(own_rows, activated, preferred_element_type=jnp.float32)
            if k == 0:
                rows = rows + jnp.concatenate([down_bias_ref[...]] * count, axis=1)
            rows = (rows * wide).astype(jnp.bfloat16)
            target = send_ref if k % 2 else keep_ref
            for j in range(count):
                target[slots[half * count + j][k // 2]] = rows[:quarter, j * lanes : (j + 1) * lanes]


def run_expert(place, arrays, blocks, slots, weights, sizes, halves):
    quarter, per = sizes
    lanes = arrays[0].shape[2]
    gate_up, down = weights[0], weights[2]
    tokens = len(blocks) * lanes
    whole = pl.BlockSpec(memory_space=pltpu.VMEM)
    out = jax.ShapeDtypeStruct((2 * len(blocks), quarter, lanes), jnp.bfloat16)
    columns = tokens // halves
    return pl.pallas_call(
        functools.partial(expert_kernel, quarter, per, blocks, slots),
        in_specs=[pl.BlockSpec(memory_space=pltpu.SMEM)] + [whole] * (len(arrays) + len(weights)),
        out_specs=[whole, whole],
        out_shape=[out, out],
        scratch_shapes=[pltpu.VMEM((gate_up.shape[1], columns), jnp.bfloat16)] * halves,
        compiler_params=pltpu.CompilerParams(vmem_limit_bytes=40 * 2**20),
        cost_estimate=pl.CostEstimate(
            flops=4 * tokens * (gate_up.size + down.size),
            bytes_accessed=2 * (gate_up.size + down.size),
            transcendentals=0,
        ),
    )(place, *arrays, *weights)


def dense(
    tokens,
    norm_gain,
    expert_ids,
    route_weights,
    gate_weight,
    gate_bias,
    up_weight,
    up_bias,
    down_weight,
    down_bias,
):
    lanes, features = tokens.shape
    experts = lax.axis_size("seq")
    groups = lax.axis_size("rep")
    quarter = features // groups
    rep, seq = lax.axis_index("rep"), lax.axis_index("seq")
    devices = experts * groups
    core, along_y, along_x, along_z = 1, 2, groups, 2 * groups

    def swap(array, step):
        return lax.ppermute(array, ("seq", "rep"), [(i, i ^ step) for i in range(devices)])

    per = -(-experts // groups)
    place = jnp.stack([rep, seq]).astype(jnp.int32)
    one, near, far = make_pieces(
        place, tokens.T, norm_gain, expert_ids.T, route_weights.T, groups, per, experts
    )
    z_2, z_3 = swap(one, 2 * along_z), swap(one, 3 * along_z)
    x_0 = swap(near, along_x)
    z_1 = swap(near, along_z)
    hidden_pad = round_up(gate_weight.shape[2], 128)
    wide = groups * round_up(quarter, 128)
    biases = jnp.concatenate([gate_bias, up_bias, down_bias], axis=0)
    inward = arrange(
        inward_kernel,
        groups,
        lanes,
        (gate_weight[0], up_weight[0], biases),
        (2 * hidden_pad, wide),
        2 * hidden_pad,
    )
    z_2, z_3, inward = tied((z_2, z_3, inward))
    z_high = jnp.stack([z_2, z_3])
    x_high, y_high = swap(z_high, along_x), swap(z_high, along_y)
    outward = arrange(
        outward_kernel,
        groups,
        lanes,
        (down_weight[0], biases),
        (wide, hidden_pad),
        wide // groups,
    )
    z_1, x_high, y_high, x_0, outward = tied((z_1, x_high, y_high, x_0, outward))
    weights = (*inward, *outward)
    corner = swap(x_high, along_y)
    x_1 = swap(z_1, along_x)

    def pairs(first, step):
        return [[(first + step * x + k % 2, k // 2) for k in range(groups)] for x in range(2)]

    slots_a, slots_b = ((2, 0), (3, 1)), ((2, 3), (0, 1))
    sizes = (quarter, per)
    keep_0, send_0 = run_expert(
        place, (near, far, x_0, swap(x_0, core)), pairs(0, 2), slots_a, weights, sizes, 1
    )
    got_0 = swap(send_0, core)
    corner, keep_0, send_0 = tied((corner, keep_0, send_0))
    high = (z_high, swap(z_high, core), y_high, swap(y_high, core))
    high = high + (x_high, swap(x_high, core), corner, swap(corner, core))
    z_1_core = swap(z_1, core)
    keep_0, got_0, z_1_core, high = tied((keep_0, got_0, z_1_core, high))
    line = [[[(4 * x + k, n) for k in range(groups)] for x in range(2)] for n in range(2)]
    keep_2, send_2 = run_expert(place, high, line[0], slots_a, weights, sizes, 1)
    got_2 = swap(send_2, core)
    keep_2, x_1, high = tied((keep_2, x_1, high))
    near_1 = (z_1, z_1_core, x_1, swap(x_1, core))
    keep_3, send_3 = run_expert(place, high, line[1], slots_b, weights, sizes, 1)
    got_2, keep_3, send_3, near_1 = tied((got_2, keep_3, send_3, near_1))
    got_3 = swap(send_3, core)
    first_y = swap(add_up(keep_2[0:2], got_2[0:2]), along_y)
    first_x = swap(add_up(keep_3[0:2], got_3[0:2]), along_x)
    got_2, got_3, near_1 = tied((got_2, got_3, near_1))
    keep_1, send_1 = run_expert(place, near_1, pairs(0, 2), slots_b, weights, sizes, 1)
    got_1 = swap(send_1, core)

    first_y, first_x, keep_0, got_0, keep_1 = tied((first_y, first_x, keep_0, got_0, keep_1))
    last_x = swap(add_up(keep_2[3], got_2[3], first_y[1]), along_x)
    last_y = swap(add_up(keep_3[3], got_3[3], first_x[1]), along_y)
    early_y = swap(add_up(keep_0[0:2], got_0[0:2]), along_y)
    early_x = swap(add_up(keep_1[0:2], got_1[0:2]), along_x)
    line_2 = add_up(keep_2[2], got_2[2], first_y[0], last_x)
    line_3 = add_up(keep_3[2], got_3[2], first_x[0], last_y)
    back_2, back_3 = swap(line_2, 2 * along_z), swap(line_3, 3 * along_z)
    _, _, early_y, early_x = tied((line_2, line_3, early_y, early_x))
    end_x = swap(add_up(keep_0[3], got_0[3], early_y[1]), along_x)
    end_y = swap(add_up(keep_1[3], got_1[3], early_x[1]), along_y)
    line_1 = add_up(keep_1[2], got_1[2], early_x[0], end_y)
    back_1 = swap(line_1, along_z)
    mixed = add_up(keep_0[2], got_0[2], early_y[0], end_x, back_1, back_2, back_3)
    return mixed.T


def on_device(*args):
    tokens, expert_ids = args[0], args[2]
    experts, groups = lax.axis_size("seq"), lax.axis_size("rep")
    capacity = 2 * tokens.shape[0] * expert_ids.shape[1] // experts
    if capacity >= tokens.shape[0] and experts == 2 * groups and groups == 4:
        return dense(*args)
    return routed(*args, capacity)


def solution(mesh):
    placed = (
        P("seq", None),
        P(),
        P("seq", None),
        P("seq", None),
        P("seq", None, "rep"),
        P("seq", "rep"),
        P("seq", None, "rep"),
        P("seq", "rep"),
        P("seq", "rep", None),
        P("seq", "rep"),
    )
    return jax.shard_map(
        on_device, mesh=mesh, in_specs=placed, out_specs=P("seq", "rep"), check_vma=False
    )
```

```python
import functools

import jax
import jax.numpy as jnp
from jax import lax
from jax.experimental import pallas as pl
from jax.experimental.pallas import tpu as pltpu
from jax.sharding import PartitionSpec as P


def rms_normed(values, norm_gain, axis):
    values = values.astype(jnp.float32)
    scale = lax.rsqrt(jnp.mean(values * values, axis=axis, keepdims=True) + 1e-05)
    return (values * scale * norm_gain).astype(jnp.bfloat16)


def gated(gate_pre, up_pre):
    return (gate_pre * jax.nn.sigmoid(1.702 * gate_pre) * (up_pre + 1.0)).astype(jnp.bfloat16)


def routed(
    tokens,
    norm_gain,
    expert_ids,
    route_weights,
    gate_weight,
    gate_bias,
    up_weight,
    up_bias,
    down_weight,
    down_bias,
    capacity,
):
    tok_rows, features = tokens.shape
    per_token = expert_ids.shape[1]
    experts = lax.axis_size("seq")
    quarter = features // lax.axis_size("rep")
    normed = rms_normed(tokens, norm_gain, -1)
    flat_ids = expert_ids.reshape(-1)
    onehot = (flat_ids[:, None] == jnp.arange(experts, dtype=jnp.int32)[None, :]).astype(jnp.int32)
    before = jnp.cumsum(onehot, axis=0) - onehot
    slot_index = jnp.sum(before * onehot, axis=1)
    destination = flat_ids * capacity + slot_index
    owner_row = jnp.arange(tok_rows * per_token, dtype=jnp.int32) // per_token
    buffer = jnp.zeros((experts * capacity, features), jnp.bfloat16)
    buffer = buffer.at[destination].set(normed[owner_row])
    received = lax.all_to_all(
        buffer.reshape(experts, capacity, features), "seq", split_axis=0, concat_axis=0, tiled=True
    )
    in_rows = received.reshape(-1, features)
    gate_pre = jnp.dot(in_rows, gate_weight[0], preferred_element_type=jnp.float32) + gate_bias[0]
    up_pre = jnp.dot(in_rows, up_weight[0], preferred_element_type=jnp.float32) + up_bias[0]
    partial_value = jnp.dot(
        gated(gate_pre, up_pre), down_weight[0], preferred_element_type=jnp.float32
    ).astype(jnp.bfloat16)
    summed = lax.psum_scatter(
        partial_value.reshape(experts, capacity, features),
        "rep",
        scatter_dimension=2,
        tiled=True,
    ).astype(jnp.float32)
    expert_out = (summed + down_bias[0][None, None, :]).astype(jnp.bfloat16)
    returned = lax.all_to_all(expert_out, "seq", split_axis=0, concat_axis=0, tiled=True)
    picked = returned.reshape(-1, quarter)[destination].reshape(tok_rows, per_token, quarter)
    mixed = jnp.sum(route_weights[:, :, None] * picked.astype(jnp.float32), axis=1)
    return mixed.astype(jnp.bfloat16)


tied = lax.optimization_barrier


def round_up(number, step):
    return -(-number // step) * step


def add_up(*terms):
    total = terms[0].astype(jnp.float32)
    for term in terms[1:]:
        total = total + term.astype(jnp.float32)
    return total.astype(jnp.bfloat16)


def padded(array, rows, columns):
    return jnp.pad(array, ((0, rows - array.shape[0]), (0, columns - array.shape[1])))


def column(row, size, lanes):
    return jnp.broadcast_to(padded(row, 1, size), (lanes, size)).T


def inward_kernel(groups, gate_ref, up_ref, biases_ref, weight_out, bias_out):
    features, hidden = gate_ref.shape
    quarter = features // groups
    hidden_pad, size = round_up(hidden, 128), round_up(quarter, 128)
    for n, weight in enumerate((gate_ref, up_ref)):
        values = weight[...].astype(jnp.float32)
        rows = slice(n * hidden_pad, (n + 1) * hidden_pad)
        for q in range(groups):
            part = padded(values[q * quarter : (q + 1) * quarter], size, hidden_pad)
            weight_out[rows, q * size : (q + 1) * size] = part.T.astype(jnp.bfloat16)
        bias_out[rows] = column(biases_ref[n : n + 1], hidden_pad, bias_out.shape[1])


def outward_kernel(groups, down_ref, biases_ref, weight_out, bias_out):
    hidden, features = down_ref.shape
    quarter = features // groups
    hidden_pad, size = round_up(hidden, 128), round_up(quarter, 128)
    values = padded(down_ref[...].astype(jnp.float32), hidden_pad, round_up(features, 128)).T
    for q in range(groups):
        part = padded(values[q * quarter : (q + 1) * quarter], size, hidden_pad)
        weight_out[q * size : (q + 1) * size] = part.astype(jnp.bfloat16)
    bias_out[...] = column(biases_ref[2:3], size, bias_out.shape[1])


def arrange(kernel, groups, lanes, arrays, shape, bias_rows):
    return pl.pallas_call(
        functools.partial(kernel, groups),
        out_shape=[
            jax.ShapeDtypeStruct(shape, jnp.bfloat16),
            jax.ShapeDtypeStruct((bias_rows, lanes), jnp.float32),
        ],
        compiler_params=pltpu.CompilerParams(vmem_limit_bytes=40 * 2**20),
        cost_estimate=pl.CostEstimate(
            flops=0, bytes_accessed=16 * arrays[0].size, transcendentals=0
        ),
    )(*arrays)


def fetch(sources, targets, sems):
    copies = [
        pltpu.make_async_copy(source, target, sems.at[n])
        for n, (source, target) in enumerate(zip(sources, targets))
    ]
    for copy in copies:
        copy.start()
    for copy in copies:
        copy.wait()


def pieces_kernel(groups, per, experts, *refs):
    sources, (one_ref, near_ref, far_ref) = refs[:4], refs[4:7]
    tokens_ref, gain_ref, ids_ref, weights_ref = refs[7:11]
    fetch(sources, refs[7:11], refs[11])
    features, lanes = tokens_ref.shape
    quarter = features // groups
    tail = one_ref.shape[0] - quarter
    rep = lax.axis_index("rep")
    values = tokens_ref[...].astype(jnp.float32)
    scale = lax.rsqrt(jnp.mean(values * values, axis=0, keepdims=True) + 1e-05)
    gain = jnp.broadcast_to(gain_ref[...].reshape(1, features), (lanes, features)).T
    normed = values * scale * gain
    row = lax.broadcasted_iota(jnp.int32, (tail, lanes), 0)
    chosen = lax.broadcasted_iota(jnp.int32, (round_up(experts, 8), lanes), 0)
    shares = jnp.zeros(chosen.shape, jnp.float32)
    for k in range(ids_ref.shape[0]):
        shares += jnp.where(ids_ref[k : k + 1] == chosen, weights_ref[k : k + 1], 0.0)
    terms = []
    for _ in range(3):
        term = shares.astype(jnp.bfloat16).astype(jnp.float32)
        terms.append(term)
        shares = shares - term
    for q in range(groups):
        rows = jnp.zeros((tail, lanes), jnp.float32)
        for n, term in enumerate(terms):
            for i in range(per):
                expert = q * per + i
                if expert < experts:
                    rows = jnp.where(row == n * per + i, term[expert : expert + 1], rows)
        piece = jnp.concatenate([normed[q * quarter : (q + 1) * quarter], rows], axis=0)
        piece = piece.astype(jnp.bfloat16)
        k = rep ^ q
        for side, target in enumerate((near_ref, far_ref)):

            @pl.when(k % 2 == side)
            def _(target=target, piece=piece, k=k):
                target[k // 2] = piece

        @pl.when(k == 0)
        def _(piece=piece):
            one_ref[...] = piece


def make_pieces(tokens, norm_gain, expert_ids, route_weights, groups, per, experts):
    features, lanes = tokens.shape
    rows = round_up(features // groups + 3 * per, 16)
    pair = jax.ShapeDtypeStruct((groups // 2, rows, lanes), jnp.bfloat16)
    arrays = (tokens, norm_gain, expert_ids, route_weights)
    return pl.pallas_call(
        functools.partial(pieces_kernel, groups, per, experts),
        in_specs=[pl.BlockSpec(memory_space=pltpu.HBM)] * 4,
        out_specs=[pl.BlockSpec(memory_space=pltpu.VMEM)] * 3,
        out_shape=[jax.ShapeDtypeStruct((rows, lanes), jnp.bfloat16), pair, pair],
        scratch_shapes=[pltpu.VMEM(a.shape, a.dtype) for a in arrays]
        + [pltpu.SemaphoreType.DMA((len(arrays),))],
        compiler_params=pltpu.CompilerParams(vmem_limit_bytes=60 * 2**20),
    )(*arrays)


def expert_kernel(quarter, per, blocks, slots, *refs):
    groups = len(blocks[0])
    counted = 1 + max(at for block in blocks for at, _ in block)
    arrays = refs[:counted]
    gate_up_ref, bias_ref, down_ref, down_bias_ref, keep_ref, send_ref = refs[counted : 6 + counted]
    scratch = refs[6 + counted :]
    _, piece_rows, lanes = arrays[0].shape
    size = gate_up_ref.shape[1] // groups
    hidden = gate_up_ref.shape[0] // 2
    rep, seq = lax.axis_index("rep"), lax.axis_index("seq")
    halves = len(scratch)
    count = len(blocks) // halves
    row = lax.broadcasted_iota(jnp.int32, (piece_rows - quarter, lanes), 0)
    for half in range(halves):
        rows_ref = scratch[half]
        if size > piece_rows:
            for k in range(groups):
                rows_ref[k * size + piece_rows : (k + 1) * size, :] = jnp.zeros(
                    (size - piece_rows, count * lanes), jnp.bfloat16
                )
        shares = [jnp.zeros((1, lanes), jnp.float32)] * count
        for k in range(groups):
            source = rep ^ k
            at_row = pl.ds(pl.multiple_of(source * size, size), piece_rows)
            mine = (lax.rem(row, per) == seq - source * per) & (row < 3 * per)
            for j in range(count):
                at, index = blocks[half * count + j][k]
                values = arrays[at][index]
                rows_ref[at_row, j * lanes : (j + 1) * lanes] = values
                terms = values.astype(jnp.float32)[quarter:]
                shares[j] += jnp.sum(jnp.where(mine, terms, 0.0), axis=0, keepdims=True)
        wide = jnp.concatenate(shares, axis=1)
        both = jnp.dot(gate_up_ref[...], rows_ref[...], preferred_element_type=jnp.float32)
        both = both + jnp.concatenate([bias_ref[...]] * count, axis=1)
        activated = gated(both[:hidden], both[hidden:])
        for k in range(groups):
            own_rows = down_ref[pl.ds(pl.multiple_of((rep ^ k) * size, size), size), :]
            rows = jnp.dot(own_rows, activated, preferred_element_type=jnp.float32)
            if k == 0:
                rows = rows + jnp.concatenate([down_bias_ref[...]] * count, axis=1)
            rows = (rows * wide).astype(jnp.bfloat16)
            target = send_ref if k % 2 else keep_ref
            for j in range(count):
                target[slots[half * count + j][k // 2]] = rows[:quarter, j * lanes : (j + 1) * lanes]


def run_expert(arrays, blocks, slots, weights, sizes, halves):
    quarter, per = sizes
    lanes = arrays[0].shape[2]
    gate_up, down = weights[0], weights[2]
    tokens = len(blocks) * lanes
    whole = pl.BlockSpec(memory_space=pltpu.VMEM)
    out = jax.ShapeDtypeStruct((2 * len(blocks), quarter, lanes), jnp.bfloat16)
    columns = tokens // halves
    return pl.pallas_call(
        functools.partial(expert_kernel, quarter, per, blocks, slots),
        in_specs=[whole] * (len(arrays) + len(weights)),
        out_specs=[whole, whole],
        out_shape=[out, out],
        scratch_shapes=[pltpu.VMEM((gate_up.shape[1], columns), jnp.bfloat16)] * halves,
        compiler_params=pltpu.CompilerParams(vmem_limit_bytes=40 * 2**20),
        cost_estimate=pl.CostEstimate(
            flops=4 * tokens * (gate_up.size + down.size),
            bytes_accessed=2 * (gate_up.size + down.size),
            transcendentals=0,
        ),
    )(*arrays, *weights)


def dense(
    tokens,
    norm_gain,
    expert_ids,
    route_weights,
    gate_weight,
    gate_bias,
    up_weight,
    up_bias,
    down_weight,
    down_bias,
):
    lanes, features = tokens.shape
    experts = lax.axis_size("seq")
    groups = lax.axis_size("rep")
    quarter = features // groups
    devices = experts * groups
    core, along_y, along_x, along_z = 1, 2, groups, 2 * groups

    def swap(array, step):
        return lax.ppermute(array, ("seq", "rep"), [(i, i ^ step) for i in range(devices)])

    per = -(-experts // groups)
    one, near, far = make_pieces(
        tokens.T, norm_gain, expert_ids.T, route_weights.T, groups, per, experts
    )
    z_2, z_3 = swap(one, 2 * along_z), swap(one, 3 * along_z)
    x_0 = swap(near, along_x)
    z_1 = swap(near, along_z)
    hidden_pad = round_up(gate_weight.shape[2], 128)
    wide = groups * round_up(quarter, 128)
    biases = jnp.concatenate([gate_bias, up_bias, down_bias], axis=0)
    inward = arrange(
        inward_kernel,
        groups,
        lanes,
        (gate_weight[0], up_weight[0], biases),
        (2 * hidden_pad, wide),
        2 * hidden_pad,
    )
    z_2, z_3, inward = tied((z_2, z_3, inward))
    z_high = jnp.stack([z_2, z_3])
    diagonal = along_x + along_y
    x_high, y_high = swap(z_high, along_x), swap(z_high, along_y)
    d_high = swap(z_high, diagonal)
    outward = arrange(
        outward_kernel,
        groups,
        lanes,
        (down_weight[0], biases),
        (wide, hidden_pad),
        wide // groups,
    )
    x_0, outward = tied((x_0, outward))
    weights = (*inward, *outward)

    def pairs(first, step):
        return [[(first + step * x + k % 2, k // 2) for k in range(groups)] for x in range(2)]

    slots = ((0, 1), (2, 3))
    sizes = (quarter, per)
    keep_0, send_0 = run_expert(
        (near, far, x_0, swap(x_0, core)), pairs(0, 2), slots, weights, sizes, 1
    )
    z_1, x_high, y_high, d_high, keep_0, send_0 = tied(
        (z_1, x_high, y_high, d_high, keep_0, send_0)
    )
    x_1 = swap(z_1, along_x)
    got_0 = swap(send_0, core)
    high = (z_high, swap(z_high, core), y_high, swap(y_high, core))
    high = high + (x_high, swap(x_high, core), d_high, swap(d_high, core))
    z_1_core = swap(z_1, core)
    got_0, z_1_core, high = tied((got_0, z_1_core, high))
    line = [[[(4 * x + k, n) for k in range(groups)] for x in range(2)] for n in range(2)]
    keep_2, send_2 = run_expert(high, line[0], slots, weights, sizes, 1)
    got_2 = swap(send_2, core)
    keep_2, high = tied((keep_2, high))
    keep_3, send_3 = run_expert(high, line[1], slots, weights, sizes, 1)
    got_2, keep_3, x_1 = tied((got_2, keep_3, x_1))
    got_3 = swap(send_3, core)

    near_1 = (z_1, z_1_core, x_1, swap(x_1, core))
    keep_1, send_1 = run_expert(near_1, pairs(0, 2), slots, weights, sizes, 1)
    got_1 = swap(send_1, core)
    keep_1, got_3 = tied((keep_1, got_3))
    def outer(first, second, at):
        return jnp.stack([add_up(keep[at], got[at]) for keep, got in (first, second)])

    far_lines = ((keep_2, got_2), (keep_3, got_3))
    y_sum = swap(outer(*far_lines, 1), along_y)
    x_sum = swap(outer(*far_lines, 2), along_x)
    d_sum = swap(outer(*far_lines, 3), diagonal)
    line_2 = add_up(keep_2[0], got_2[0], x_sum[0], y_sum[0], d_sum[0])
    line_3 = add_up(keep_3[0], got_3[0], x_sum[1], y_sum[1], d_sum[1])
    back_2, back_3 = swap(line_2, 2 * along_z), swap(line_3, 3 * along_z)
    near_lines = ((keep_0, got_0), (keep_1, got_1))
    x_near = swap(outer(*near_lines, 2), along_x)
    y_near = swap(outer(*near_lines, 1), along_y)
    d_near = swap(outer(*near_lines, 3), diagonal)
    _, _, x_near, y_near, d_near = tied((line_2, line_3, x_near, y_near, d_near))
    line_1 = add_up(keep_1[0], got_1[0], x_near[1], y_near[1], d_near[1])
    back_1 = swap(line_1, along_z)
    mixed = add_up(
        keep_0[0], got_0[0], x_near[0], y_near[0], d_near[0], back_1, back_2, back_3
    )
    return mixed.T


def on_device(*args):
    tokens, expert_ids = args[0], args[2]
    experts, groups = lax.axis_size("seq"), lax.axis_size("rep")
    capacity = 2 * tokens.shape[0] * expert_ids.shape[1] // experts
    if capacity >= tokens.shape[0] and experts == 2 * groups and groups == 4:
        return dense(*args)
    return routed(*args, capacity)


def solution(mesh):
    placed = (
        P("seq", None),
        P(),
        P("seq", None),
        P("seq", None),
        P("seq", None, "rep"),
        P("seq", "rep"),
        P("seq", None, "rep"),
        P("seq", "rep"),
        P("seq", "rep", None),
        P("seq", "rep"),
    )
    return jax.shard_map(
        on_device, mesh=mesh, in_specs=placed, out_specs=P("seq", "rep"), check_vma=False
    )
```

```python
import functools

import jax
import jax.numpy as jnp
from jax import lax
from jax.experimental import pallas as pl
from jax.experimental.pallas import tpu as pltpu
from jax.sharding import PartitionSpec as P


def rms_normed(values, norm_gain, axis):
    values = values.astype(jnp.float32)
    scale = lax.rsqrt(jnp.mean(values * values, axis=axis, keepdims=True) + 1e-05)
    return (values * scale * norm_gain).astype(jnp.bfloat16)


def gated(gate_pre, up_pre):
    return (gate_pre * jax.nn.sigmoid(1.702 * gate_pre) * (up_pre + 1.0)).astype(jnp.bfloat16)


def routed(
    tokens,
    norm_gain,
    expert_ids,
    route_weights,
    gate_weight,
    gate_bias,
    up_weight,
    up_bias,
    down_weight,
    down_bias,
    capacity,
):
    tok_rows, features = tokens.shape
    per_token = expert_ids.shape[1]
    experts = lax.axis_size("seq")
    quarter = features // lax.axis_size("rep")
    normed = rms_normed(tokens, norm_gain, -1)
    flat_ids = expert_ids.reshape(-1)
    onehot = (flat_ids[:, None] == jnp.arange(experts, dtype=jnp.int32)[None, :]).astype(jnp.int32)
    before = jnp.cumsum(onehot, axis=0) - onehot
    slot_index = jnp.sum(before * onehot, axis=1)
    destination = flat_ids * capacity + slot_index
    owner_row = jnp.arange(tok_rows * per_token, dtype=jnp.int32) // per_token
    buffer = jnp.zeros((experts * capacity, features), jnp.bfloat16)
    buffer = buffer.at[destination].set(normed[owner_row])
    received = lax.all_to_all(
        buffer.reshape(experts, capacity, features), "seq", split_axis=0, concat_axis=0, tiled=True
    )
    in_rows = received.reshape(-1, features)
    gate_pre = jnp.dot(in_rows, gate_weight[0], preferred_element_type=jnp.float32) + gate_bias[0]
    up_pre = jnp.dot(in_rows, up_weight[0], preferred_element_type=jnp.float32) + up_bias[0]
    partial_value = jnp.dot(
        gated(gate_pre, up_pre), down_weight[0], preferred_element_type=jnp.float32
    ).astype(jnp.bfloat16)
    summed = lax.psum_scatter(
        partial_value.reshape(experts, capacity, features),
        "rep",
        scatter_dimension=2,
        tiled=True,
    ).astype(jnp.float32)
    expert_out = (summed + down_bias[0][None, None, :]).astype(jnp.bfloat16)
    returned = lax.all_to_all(expert_out, "seq", split_axis=0, concat_axis=0, tiled=True)
    picked = returned.reshape(-1, quarter)[destination].reshape(tok_rows, per_token, quarter)
    mixed = jnp.sum(route_weights[:, :, None] * picked.astype(jnp.float32), axis=1)
    return mixed.astype(jnp.bfloat16)


tied = lax.optimization_barrier


def round_up(number, step):
    return -(-number // step) * step


def add_up(*terms):
    total = terms[0].astype(jnp.float32)
    for term in terms[1:]:
        total = total + term.astype(jnp.float32)
    return total.astype(jnp.bfloat16)


def padded(array, rows, columns):
    return jnp.pad(array, ((0, rows - array.shape[0]), (0, columns - array.shape[1])))


def column(row, size, lanes):
    return jnp.broadcast_to(padded(row, 1, size), (lanes, size)).T


def inward_kernel(groups, gate_ref, up_ref, biases_ref, weight_out, bias_out):
    features, hidden = gate_ref.shape
    quarter = features // groups
    hidden_pad, size = round_up(hidden, 128), round_up(quarter, 128)
    for n, weight in enumerate((gate_ref, up_ref)):
        values = weight[...].astype(jnp.float32)
        rows = slice(n * hidden_pad, (n + 1) * hidden_pad)
        for q in range(groups):
            part = padded(values[q * quarter : (q + 1) * quarter], size, hidden_pad)
            weight_out[rows, q * size : (q + 1) * size] = part.T.astype(jnp.bfloat16)
        bias_out[rows] = column(biases_ref[n : n + 1], hidden_pad, bias_out.shape[1])


def outward_kernel(groups, down_ref, biases_ref, weight_out, bias_out):
    hidden, features = down_ref.shape
    quarter = features // groups
    hidden_pad, size = round_up(hidden, 128), round_up(quarter, 128)
    values = padded(down_ref[...].astype(jnp.float32), hidden_pad, round_up(features, 128)).T
    for q in range(groups):
        part = padded(values[q * quarter : (q + 1) * quarter], size, hidden_pad)
        weight_out[q * size : (q + 1) * size] = part.astype(jnp.bfloat16)
    bias_out[...] = column(biases_ref[2:3], size, bias_out.shape[1])


def arrange(kernel, groups, lanes, arrays, shape, bias_rows):
    return pl.pallas_call(
        functools.partial(kernel, groups),
        out_shape=[
            jax.ShapeDtypeStruct(shape, jnp.bfloat16),
            jax.ShapeDtypeStruct((bias_rows, lanes), jnp.float32),
        ],
        compiler_params=pltpu.CompilerParams(vmem_limit_bytes=40 * 2**20),
        cost_estimate=pl.CostEstimate(
            flops=0, bytes_accessed=16 * arrays[0].size, transcendentals=0
        ),
    )(*arrays)


def fetch(sources, targets, sems):
    copies = [
        pltpu.make_async_copy(source, target, sems.at[n])
        for n, (source, target) in enumerate(zip(sources, targets))
    ]
    for copy in copies:
        copy.start()
    for copy in copies:
        copy.wait()


def pieces_kernel(groups, per, experts, *refs):
    sources, (one_ref, near_ref, far_ref) = refs[:4], refs[4:7]
    tokens_ref, gain_ref, ids_ref, weights_ref = refs[7:11]
    fetch(sources, refs[7:11], refs[11])
    features, lanes = tokens_ref.shape
    quarter = features // groups
    tail = one_ref.shape[0] - quarter
    rep = lax.axis_index("rep")
    values = tokens_ref[...].astype(jnp.float32)
    scale = lax.rsqrt(jnp.mean(values * values, axis=0, keepdims=True) + 1e-05)
    gain = jnp.broadcast_to(gain_ref[...].reshape(1, features), (lanes, features)).T
    normed = values * scale * gain
    row = lax.broadcasted_iota(jnp.int32, (tail, lanes), 0)
    chosen = lax.broadcasted_iota(jnp.int32, (round_up(experts, 8), lanes), 0)
    shares = jnp.zeros(chosen.shape, jnp.float32)
    for k in range(ids_ref.shape[0]):
        shares += jnp.where(ids_ref[k : k + 1] == chosen, weights_ref[k : k + 1], 0.0)
    terms = []
    for _ in range(3):
        term = shares.astype(jnp.bfloat16).astype(jnp.float32)
        terms.append(term)
        shares = shares - term
    for q in range(groups):
        rows = jnp.zeros((tail, lanes), jnp.float32)
        for n, term in enumerate(terms):
            for i in range(per):
                expert = q * per + i
                if expert < experts:
                    rows = jnp.where(row == n * per + i, term[expert : expert + 1], rows)
        piece = jnp.concatenate([normed[q * quarter : (q + 1) * quarter], rows], axis=0)
        piece = piece.astype(jnp.bfloat16)
        k = rep ^ q
        for side, target in enumerate((near_ref, far_ref)):

            @pl.when(k % 2 == side)
            def _(target=target, piece=piece, k=k):
                target[k // 2] = piece

        @pl.when(k == 0)
        def _(piece=piece):
            one_ref[...] = piece


def make_pieces(tokens, norm_gain, expert_ids, route_weights, groups, per, experts):
    features, lanes = tokens.shape
    rows = round_up(features // groups + 3 * per, 16)
    pair = jax.ShapeDtypeStruct((groups // 2, rows, lanes), jnp.bfloat16)
    arrays = (tokens, norm_gain, expert_ids, route_weights)
    return pl.pallas_call(
        functools.partial(pieces_kernel, groups, per, experts),
        in_specs=[pl.BlockSpec(memory_space=pltpu.HBM)] * 4,
        out_specs=[pl.BlockSpec(memory_space=pltpu.VMEM)] * 3,
        out_shape=[jax.ShapeDtypeStruct((rows, lanes), jnp.bfloat16), pair, pair],
        scratch_shapes=[pltpu.VMEM(a.shape, a.dtype) for a in arrays]
        + [pltpu.SemaphoreType.DMA((len(arrays),))],
        compiler_params=pltpu.CompilerParams(vmem_limit_bytes=60 * 2**20),
    )(*arrays)


def expert_kernel(quarter, per, blocks, slots, *refs):
    groups = len(blocks[0])
    counted = 1 + max(at for block in blocks for at, _ in block)
    arrays = refs[:counted]
    gate_up_ref, bias_ref, down_ref, down_bias_ref, keep_ref, send_ref = refs[counted : 6 + counted]
    scratch = refs[6 + counted :]
    _, piece_rows, lanes = arrays[0].shape
    size = gate_up_ref.shape[1] // groups
    hidden = gate_up_ref.shape[0] // 2
    rep, seq = lax.axis_index("rep"), lax.axis_index("seq")
    halves = len(scratch)
    count = len(blocks) // halves
    row = lax.broadcasted_iota(jnp.int32, (piece_rows - quarter, lanes), 0)
    for half in range(halves):
        rows_ref = scratch[half]
        if size > piece_rows:
            for k in range(groups):
                rows_ref[k * size + piece_rows : (k + 1) * size, :] = jnp.zeros(
                    (size - piece_rows, count * lanes), jnp.bfloat16
                )
        shares = [jnp.zeros((1, lanes), jnp.float32)] * count
        for k in range(groups):
            source = rep ^ k
            at_row = pl.ds(pl.multiple_of(source * size, size), piece_rows)
            mine = (lax.rem(row, per) == seq - source * per) & (row < 3 * per)
            for j in range(count):
                at, index = blocks[half * count + j][k]
                values = arrays[at][index]
                rows_ref[at_row, j * lanes : (j + 1) * lanes] = values
                terms = values.astype(jnp.float32)[quarter:]
                shares[j] += jnp.sum(jnp.where(mine, terms, 0.0), axis=0, keepdims=True)
        wide = jnp.concatenate(shares, axis=1)
        both = jnp.dot(gate_up_ref[...], rows_ref[...], preferred_element_type=jnp.float32)
        both = both + jnp.concatenate([bias_ref[...]] * count, axis=1)
        activated = gated(both[:hidden], both[hidden:])
        for k in range(groups):
            own_rows = down_ref[pl.ds(pl.multiple_of((rep ^ k) * size, size), size), :]
            rows = jnp.dot(own_rows, activated, preferred_element_type=jnp.float32)
            if k == 0:
                rows = rows + jnp.concatenate([down_bias_ref[...]] * count, axis=1)
            rows = (rows * wide).astype(jnp.bfloat16)
            target = send_ref if k % 2 else keep_ref
            for j in range(count):
                target[slots[half * count + j][k // 2]] = rows[:quarter, j * lanes : (j + 1) * lanes]


def run_expert(arrays, blocks, slots, weights, sizes, halves):
    quarter, per = sizes
    lanes = arrays[0].shape[2]
    gate_up, down = weights[0], weights[2]
    tokens = len(blocks) * lanes
    whole = pl.BlockSpec(memory_space=pltpu.VMEM)
    out = jax.ShapeDtypeStruct((2 * len(blocks), quarter, lanes), jnp.bfloat16)
    columns = tokens // halves
    return pl.pallas_call(
        functools.partial(expert_kernel, quarter, per, blocks, slots),
        in_specs=[whole] * (len(arrays) + len(weights)),
        out_specs=[whole, whole],
        out_shape=[out, out],
        scratch_shapes=[pltpu.VMEM((gate_up.shape[1], columns), jnp.bfloat16)] * halves,
        compiler_params=pltpu.CompilerParams(vmem_limit_bytes=40 * 2**20),
        cost_estimate=pl.CostEstimate(
            flops=4 * tokens * (gate_up.size + down.size),
            bytes_accessed=2 * (gate_up.size + down.size),
            transcendentals=0,
        ),
    )(*arrays, *weights)


def dense(
    tokens,
    norm_gain,
    expert_ids,
    route_weights,
    gate_weight,
    gate_bias,
    up_weight,
    up_bias,
    down_weight,
    down_bias,
):
    lanes, features = tokens.shape
    experts = lax.axis_size("seq")
    groups = lax.axis_size("rep")
    quarter = features // groups
    devices = experts * groups
    core, along_y, along_x, along_z = 1, 2, groups, 2 * groups

    def swap(array, step):
        return lax.ppermute(array, ("seq", "rep"), [(i, i ^ step) for i in range(devices)])

    per = -(-experts // groups)
    one, near, far = make_pieces(
        tokens.T, norm_gain, expert_ids.T, route_weights.T, groups, per, experts
    )
    z_2, z_3 = swap(one, 2 * along_z), swap(one, 3 * along_z)
    z_1 = swap(near, along_z)
    hidden_pad = round_up(gate_weight.shape[2], 128)
    wide = groups * round_up(quarter, 128)
    biases = jnp.concatenate([gate_bias, up_bias, down_bias], axis=0)
    inward = arrange(
        inward_kernel,
        groups,
        lanes,
        (gate_weight[0], up_weight[0], biases),
        (2 * hidden_pad, wide),
        2 * hidden_pad,
    )
    x_0 = swap(tied((near, inward))[0], along_x)
    z_1, z_2, z_3, inward = tied((z_1, z_2, z_3, inward))
    z_high = jnp.stack([z_2, z_3])
    diagonal = along_x + along_y
    x_all = swap(jnp.concatenate([z_1, z_high], axis=0), along_x)
    d_high, y_high = swap(z_high, diagonal), swap(z_high, along_y)
    outward = arrange(
        outward_kernel,
        groups,
        lanes,
        (down_weight[0], biases),
        (wide, hidden_pad),
        wide // groups,
    )
    weights = (*inward, *outward)

    def pairs(first, step):
        return [[(first + step * x + k % 2, k // 2) for k in range(groups)] for x in range(2)]

    slots = ((0, 1), (2, 3))
    sizes = (quarter, per)
    keep_0, send_0 = run_expert(
        (near, far, x_0, swap(x_0, core)), pairs(0, 2), slots, weights, sizes, 1
    )
    x_all, y_high, d_high, keep_0, send_0 = tied((x_all, y_high, d_high, keep_0, send_0))
    got_0 = swap(send_0, core)
    x_core = swap(x_all, core)
    high = (z_high, swap(z_high, core), y_high, swap(y_high, core))
    high = high + (x_all, x_core, d_high, swap(d_high, core))
    near_1 = (z_1, swap(z_1, core), x_all, x_core)
    line = [
        [[(4 * x + k, n + 2 * (x > k // 2)) for k in range(groups)] for x in range(2)]
        for n in range(2)
    ]
    keep_2, send_2 = run_expert(high, line[0], slots, weights, sizes, 1)
    got_2 = swap(send_2, core)
    keep_2, high = tied((keep_2, high))
    keep_3, send_3 = run_expert(high, line[1], slots, weights, sizes, 1)
    got_2, keep_3, got_0 = tied((got_2, keep_3, got_0))
    got_3 = swap(send_3, core)
    near_1, got_2 = tied((near_1, got_2))
    keep_1, send_1 = run_expert(near_1, pairs(0, 2), slots, weights, sizes, 1)
    got_1 = swap(send_1, core)
    got_3, keep_1, got_0 = tied((got_3, keep_1, got_0))

    def outer(first, second, at):
        return jnp.stack([add_up(keep[at], got[at]) for keep, got in (first, second)])

    far_lines = ((keep_2, got_2), (keep_3, got_3))
    y_sum = swap(outer(*far_lines, 1), along_y)
    x_sum = swap(outer(*far_lines, 2), along_x)
    d_sum = swap(outer(*far_lines, 3), diagonal)
    line_2 = add_up(keep_2[0], got_2[0], x_sum[0], y_sum[0], d_sum[0])
    line_3 = add_up(keep_3[0], got_3[0], x_sum[1], y_sum[1], d_sum[1])
    back_2, back_3 = swap(line_2, 2 * along_z), swap(line_3, 3 * along_z)
    near_lines = ((keep_0, got_0), (keep_1, got_1))
    x_near = swap(outer(*near_lines, 2), along_x)
    y_near = swap(outer(*near_lines, 1), along_y)
    d_near = swap(outer(*near_lines, 3), diagonal)
    _, _, x_near, y_near, d_near = tied((line_2, line_3, x_near, y_near, d_near))
    line_1 = add_up(keep_1[0], got_1[0], x_near[1], y_near[1], d_near[1])
    back_1 = swap(line_1, along_z)
    mixed = add_up(
        keep_0[0], got_0[0], x_near[0], y_near[0], d_near[0], back_1, back_2, back_3
    )
    return mixed.T


def on_device(*args):
    tokens, expert_ids = args[0], args[2]
    experts, groups = lax.axis_size("seq"), lax.axis_size("rep")
    capacity = 2 * tokens.shape[0] * expert_ids.shape[1] // experts
    if capacity >= tokens.shape[0] and experts == 2 * groups and groups == 4:
        return dense(*args)
    return routed(*args, capacity)


def solution(mesh):
    placed = (
        P("seq", None),
        P(),
        P("seq", None),
        P("seq", None),
        P("seq", None, "rep"),
        P("seq", "rep"),
        P("seq", None, "rep"),
        P("seq", "rep"),
        P("seq", "rep", None),
        P("seq", "rep"),
    )
    return jax.shard_map(
        on_device, mesh=mesh, in_specs=placed, out_specs=P("seq", "rep"), check_vma=False
    )
```

```python
import functools

import jax
import jax.numpy as jnp
from jax import lax
from jax.experimental import pallas as pl
from jax.experimental.pallas import tpu as pltpu
from jax.sharding import PartitionSpec as P


def rms_normed(values, norm_gain, axis):
    values = values.astype(jnp.float32)
    scale = lax.rsqrt(jnp.mean(values * values, axis=axis, keepdims=True) + 1e-05)
    return (values * scale * norm_gain).astype(jnp.bfloat16)


def gated(gate_pre, up_pre):
    return (gate_pre * jax.nn.sigmoid(1.702 * gate_pre) * (up_pre + 1.0)).astype(jnp.bfloat16)


def routed(
    tokens,
    norm_gain,
    expert_ids,
    route_weights,
    gate_weight,
    gate_bias,
    up_weight,
    up_bias,
    down_weight,
    down_bias,
    capacity,
):
    tok_rows, features = tokens.shape
    per_token = expert_ids.shape[1]
    experts = lax.axis_size("seq")
    quarter = features // lax.axis_size("rep")
    normed = rms_normed(tokens, norm_gain, -1)
    flat_ids = expert_ids.reshape(-1)
    onehot = (flat_ids[:, None] == jnp.arange(experts, dtype=jnp.int32)[None, :]).astype(jnp.int32)
    before = jnp.cumsum(onehot, axis=0) - onehot
    slot_index = jnp.sum(before * onehot, axis=1)
    destination = flat_ids * capacity + slot_index
    owner_row = jnp.arange(tok_rows * per_token, dtype=jnp.int32) // per_token
    buffer = jnp.zeros((experts * capacity, features), jnp.bfloat16)
    buffer = buffer.at[destination].set(normed[owner_row])
    received = lax.all_to_all(
        buffer.reshape(experts, capacity, features), "seq", split_axis=0, concat_axis=0, tiled=True
    )
    in_rows = received.reshape(-1, features)
    gate_pre = jnp.dot(in_rows, gate_weight[0], preferred_element_type=jnp.float32) + gate_bias[0]
    up_pre = jnp.dot(in_rows, up_weight[0], preferred_element_type=jnp.float32) + up_bias[0]
    partial_value = jnp.dot(
        gated(gate_pre, up_pre), down_weight[0], preferred_element_type=jnp.float32
    ).astype(jnp.bfloat16)
    summed = lax.psum_scatter(
        partial_value.reshape(experts, capacity, features),
        "rep",
        scatter_dimension=2,
        tiled=True,
    ).astype(jnp.float32)
    expert_out = (summed + down_bias[0][None, None, :]).astype(jnp.bfloat16)
    returned = lax.all_to_all(expert_out, "seq", split_axis=0, concat_axis=0, tiled=True)
    picked = returned.reshape(-1, quarter)[destination].reshape(tok_rows, per_token, quarter)
    mixed = jnp.sum(route_weights[:, :, None] * picked.astype(jnp.float32), axis=1)
    return mixed.astype(jnp.bfloat16)


tied = lax.optimization_barrier


def round_up(number, step):
    return -(-number // step) * step


def add_up(*terms):
    total = terms[0].astype(jnp.float32)
    for term in terms[1:]:
        total = total + term.astype(jnp.float32)
    return total.astype(jnp.bfloat16)


def padded(array, rows, columns):
    return jnp.pad(array, ((0, rows - array.shape[0]), (0, columns - array.shape[1])))


def column(row, size, lanes):
    return jnp.broadcast_to(padded(row, 1, size), (lanes, size)).T


def inward_kernel(groups, gate_ref, up_ref, biases_ref, weight_out, bias_out):
    features, hidden = gate_ref.shape
    quarter = features // groups
    hidden_pad, size = round_up(hidden, 128), round_up(quarter, 128)
    for n, weight in enumerate((gate_ref, up_ref)):
        values = weight[...].astype(jnp.float32)
        rows = slice(n * hidden_pad, (n + 1) * hidden_pad)
        for q in range(groups):
            part = padded(values[q * quarter : (q + 1) * quarter], size, hidden_pad)
            weight_out[rows, q * size : (q + 1) * size] = part.T.astype(jnp.bfloat16)
        bias_out[rows] = column(biases_ref[n : n + 1], hidden_pad, bias_out.shape[1])


def outward_kernel(groups, down_ref, biases_ref, weight_out, bias_out):
    hidden, features = down_ref.shape
    quarter = features // groups
    hidden_pad, size = round_up(hidden, 128), round_up(quarter, 128)
    values = padded(down_ref[...].astype(jnp.float32), hidden_pad, round_up(features, 128)).T
    for q in range(groups):
        part = padded(values[q * quarter : (q + 1) * quarter], size, hidden_pad)
        weight_out[q * size : (q + 1) * size] = part.astype(jnp.bfloat16)
    bias_out[...] = column(biases_ref[2:3], size, bias_out.shape[1])


def arrange(kernel, groups, lanes, arrays, shape, bias_rows):
    return pl.pallas_call(
        functools.partial(kernel, groups),
        out_shape=[
            jax.ShapeDtypeStruct(shape, jnp.bfloat16),
            jax.ShapeDtypeStruct((bias_rows, lanes), jnp.float32),
        ],
        compiler_params=pltpu.CompilerParams(vmem_limit_bytes=40 * 2**20),
        cost_estimate=pl.CostEstimate(
            flops=0, bytes_accessed=16 * arrays[0].size, transcendentals=0
        ),
    )(*arrays)


def fetch(sources, targets, sems):
    copies = [
        pltpu.make_async_copy(source, target, sems.at[n])
        for n, (source, target) in enumerate(zip(sources, targets))
    ]
    for copy in copies:
        copy.start()
    for copy in copies:
        copy.wait()


def pieces_kernel(groups, per, experts, *refs):
    sources, (one_ref, near_ref, far_ref) = refs[:4], refs[4:7]
    tokens_ref, gain_ref, ids_ref, weights_ref = refs[7:11]
    fetch(sources, refs[7:11], refs[11])
    features, lanes = tokens_ref.shape
    quarter = features // groups
    tail = one_ref.shape[0] - quarter
    rep = lax.axis_index("rep")
    values = tokens_ref[...].astype(jnp.float32)
    scale = lax.rsqrt(jnp.mean(values * values, axis=0, keepdims=True) + 1e-05)
    gain = jnp.broadcast_to(gain_ref[...].reshape(1, features), (lanes, features)).T
    normed = values * scale * gain
    row = lax.broadcasted_iota(jnp.int32, (tail, lanes), 0)
    chosen = lax.broadcasted_iota(jnp.int32, (round_up(experts, 8), lanes), 0)
    shares = jnp.zeros(chosen.shape, jnp.float32)
    for k in range(ids_ref.shape[0]):
        shares += jnp.where(ids_ref[k : k + 1] == chosen, weights_ref[k : k + 1], 0.0)
    terms = []
    for _ in range(3):
        term = shares.astype(jnp.bfloat16).astype(jnp.float32)
        terms.append(term)
        shares = shares - term
    for q in range(groups):
        rows = jnp.zeros((tail, lanes), jnp.float32)
        for n, term in enumerate(terms):
            for i in range(per):
                expert = q * per + i
                if expert < experts:
                    rows = jnp.where(row == n * per + i, term[expert : expert + 1], rows)
        piece = jnp.concatenate([normed[q * quarter : (q + 1) * quarter], rows], axis=0)
        piece = piece.astype(jnp.bfloat16)
        k = rep ^ q
        for side, target in enumerate((near_ref, far_ref)):

            @pl.when(k % 2 == side)
            def _(target=target, piece=piece, k=k):
                target[k // 2] = piece

        @pl.when(k == 0)
        def _(piece=piece):
            one_ref[...] = piece


def make_pieces(tokens, norm_gain, expert_ids, route_weights, groups, per, experts):
    features, lanes = tokens.shape
    rows = round_up(features // groups + 3 * per, 16)
    pair = jax.ShapeDtypeStruct((groups // 2, rows, lanes), jnp.bfloat16)
    arrays = (tokens, norm_gain, expert_ids, route_weights)
    return pl.pallas_call(
        functools.partial(pieces_kernel, groups, per, experts),
        in_specs=[pl.BlockSpec(memory_space=pltpu.HBM)] * 4,
        out_specs=[pl.BlockSpec(memory_space=pltpu.VMEM)] * 3,
        out_shape=[jax.ShapeDtypeStruct((rows, lanes), jnp.bfloat16), pair, pair],
        scratch_shapes=[pltpu.VMEM(a.shape, a.dtype) for a in arrays]
        + [pltpu.SemaphoreType.DMA((len(arrays),))],
        compiler_params=pltpu.CompilerParams(vmem_limit_bytes=60 * 2**20),
    )(*arrays)


def expert_kernel(quarter, per, blocks, slots, *refs):
    groups = len(blocks[0])
    counted = 1 + max(at for block in blocks for at, _ in block)
    arrays = refs[:counted]
    gate_up_ref, bias_ref, down_ref, down_bias_ref, keep_ref, send_ref = refs[counted : 6 + counted]
    scratch = refs[6 + counted :]
    _, piece_rows, lanes = arrays[0].shape
    size = gate_up_ref.shape[1] // groups
    hidden = gate_up_ref.shape[0] // 2
    rep, seq = lax.axis_index("rep"), lax.axis_index("seq")
    halves = len(scratch)
    count = len(blocks) // halves
    row = lax.broadcasted_iota(jnp.int32, (piece_rows - quarter, lanes), 0)
    for half in range(halves):
        rows_ref = scratch[half]
        if size > piece_rows:
            for k in range(groups):
                rows_ref[k * size + piece_rows : (k + 1) * size, :] = jnp.zeros(
                    (size - piece_rows, count * lanes), jnp.bfloat16
                )
        shares = [jnp.zeros((1, lanes), jnp.float32)] * count
        for k in range(groups):
            source = rep ^ k
            at_row = pl.ds(pl.multiple_of(source * size, size), piece_rows)
            mine = (lax.rem(row, per) == seq - source * per) & (row < 3 * per)
            for j in range(count):
                at, index = blocks[half * count + j][k]
                values = arrays[at][index]
                rows_ref[at_row, j * lanes : (j + 1) * lanes] = values
                terms = values.astype(jnp.float32)[quarter:]
                shares[j] += jnp.sum(jnp.where(mine, terms, 0.0), axis=0, keepdims=True)
        wide = jnp.concatenate(shares, axis=1)
        both = jnp.dot(gate_up_ref[...], rows_ref[...], preferred_element_type=jnp.float32)
        both = both + jnp.concatenate([bias_ref[...]] * count, axis=1)
        activated = gated(both[:hidden], both[hidden:])
        for k in range(groups):
            own_rows = down_ref[pl.ds(pl.multiple_of((rep ^ k) * size, size), size), :]
            rows = jnp.dot(own_rows, activated, preferred_element_type=jnp.float32)
            if k == 0:
                rows = rows + jnp.concatenate([down_bias_ref[...]] * count, axis=1)
            rows = (rows * wide).astype(jnp.bfloat16)
            target = send_ref if k % 2 else keep_ref
            for j in range(count):
                target[slots[half * count + j][k // 2]] = rows[:quarter, j * lanes : (j + 1) * lanes]


def run_expert(arrays, blocks, slots, weights, sizes, halves):
    quarter, per = sizes
    lanes = arrays[0].shape[2]
    gate_up, down = weights[0], weights[2]
    tokens = len(blocks) * lanes
    whole = pl.BlockSpec(memory_space=pltpu.VMEM)
    out = jax.ShapeDtypeStruct((2 * len(blocks), quarter, lanes), jnp.bfloat16)
    columns = tokens // halves
    return pl.pallas_call(
        functools.partial(expert_kernel, quarter, per, blocks, slots),
        in_specs=[whole] * (len(arrays) + len(weights)),
        out_specs=[whole, whole],
        out_shape=[out, out],
        scratch_shapes=[pltpu.VMEM((gate_up.shape[1], columns), jnp.bfloat16)] * halves,
        compiler_params=pltpu.CompilerParams(vmem_limit_bytes=40 * 2**20),
        cost_estimate=pl.CostEstimate(
            flops=4 * tokens * (gate_up.size + down.size),
            bytes_accessed=2 * (gate_up.size + down.size),
            transcendentals=0,
        ),
    )(*arrays, *weights)


def dense(
    tokens,
    norm_gain,
    expert_ids,
    route_weights,
    gate_weight,
    gate_bias,
    up_weight,
    up_bias,
    down_weight,
    down_bias,
):
    lanes, features = tokens.shape
    experts = lax.axis_size("seq")
    groups = lax.axis_size("rep")
    quarter = features // groups
    devices = experts * groups
    core, along_y, along_x, along_z = 1, 2, groups, 2 * groups

    def swap(array, step):
        return lax.ppermute(array, ("seq", "rep"), [(i, i ^ step) for i in range(devices)])

    per = -(-experts // groups)
    one, near, far = make_pieces(
        tokens.T, norm_gain, expert_ids.T, route_weights.T, groups, per, experts
    )
    z_2, z_3 = swap(one, 2 * along_z), swap(one, 3 * along_z)
    z_1 = swap(near, along_z)
    hidden_pad = round_up(gate_weight.shape[2], 128)
    wide = groups * round_up(quarter, 128)
    biases = jnp.concatenate([gate_bias, up_bias, down_bias], axis=0)
    inward = arrange(
        inward_kernel,
        groups,
        lanes,
        (gate_weight[0], up_weight[0], biases),
        (2 * hidden_pad, wide),
        2 * hidden_pad,
    )
    x_0 = swap(tied((near, inward))[0], along_x)
    z_1, z_2, z_3, inward = tied((z_1, z_2, z_3, inward))
    z_high = jnp.stack([z_2, z_3])
    x_high, y_high = swap(z_high, along_x), swap(z_high, along_y)
    outward = arrange(
        outward_kernel,
        groups,
        lanes,
        (down_weight[0], biases),
        (wide, hidden_pad),
        wide // groups,
    )
    weights = (*inward, *outward)

    def expert(arrays, blocks):
        return run_expert(arrays, blocks, ((0, 2), (1, 3)), weights, (quarter, per), 1)

    def line(arrays, index):
        return [(at, n) for at, n in zip(arrays, index)]

    twice = [0, 0, 1, 1]
    near_blocks = [line([0, 1, 0, 1], twice), line([2, 3, 2, 3], twice)]
    far_blocks = [line([0, 1, 2, 3], [n] * groups) for n in range(2)]

    keep_p, send_p = expert((near, far, z_1, swap(z_1, core)), near_blocks)
    x_high, z_1, x_0, keep_p, send_p = tied((x_high, z_1, x_0, keep_p, send_p))
    corner, x_1 = swap(x_high, along_y), swap(z_1, along_x)
    got_p = swap(send_p, core)
    keep_q, send_q = expert((z_high, swap(z_high, core), y_high, swap(y_high, core)), far_blocks)
    corner, x_1, keep_q, send_q = tied((corner, x_1, keep_q, send_q))
    got_q = swap(send_q, core)
    y_p = swap(add_up(keep_p[2:4], got_p[2:4]), along_y)
    y_q = swap(add_up(keep_q[2:4], got_q[2:4]), along_y)
    keep_s, send_s = expert((x_high, swap(x_high, core), corner, swap(corner, core)), far_blocks)
    keep_s, send_s, y_p, x_1 = tied((keep_s, send_s, y_p, x_1))
    got_s = swap(send_s, core)
    keep_r, send_r = expert((x_0, swap(x_0, core), x_1, swap(x_1, core)), near_blocks)
    keep_r, send_r, y_q = tied((keep_r, send_r, y_q))
    got_r = swap(send_r, core)

    y_s = swap(add_up(keep_s[2:4], got_s[2:4]), along_y)
    y_r = swap(add_up(keep_r[2:4], got_r[2:4]), along_y)
    x_s = swap(add_up(keep_s[0:2], got_s[0:2], y_s), along_x)
    x_r = swap(add_up(keep_r[0:2], got_r[0:2], y_r), along_x)
    line_2, line_3 = [add_up(keep_q[n], got_q[n], y_q[n], x_s[n]) for n in range(2)]
    back_2, back_3 = swap(line_2, 2 * along_z), swap(line_3, 3 * along_z)
    back_1 = swap(add_up(keep_p[1], got_p[1], y_p[1], x_r[1]), along_z)
    mixed = add_up(keep_p[0], got_p[0], y_p[0], x_r[0], back_1, back_2, back_3)
    return mixed.T


def on_device(*args):
    tokens, expert_ids = args[0], args[2]
    experts, groups = lax.axis_size("seq"), lax.axis_size("rep")
    capacity = 2 * tokens.shape[0] * expert_ids.shape[1] // experts
    if capacity >= tokens.shape[0] and experts == 2 * groups and groups == 4:
        return dense(*args)
    return routed(*args, capacity)


def solution(mesh):
    placed = (
        P("seq", None),
        P(),
        P("seq", None),
        P("seq", None),
        P("seq", None, "rep"),
        P("seq", "rep"),
        P("seq", None, "rep"),
        P("seq", "rep"),
        P("seq", "rep", None),
        P("seq", "rep"),
    )
    return jax.shard_map(
        on_device, mesh=mesh, in_specs=placed, out_specs=P("seq", "rep"), check_vma=False
    )
```

```python
import functools

import jax
import jax.numpy as jnp
from jax import lax
from jax.experimental import pallas as pl
from jax.experimental.pallas import tpu as pltpu
from jax.sharding import PartitionSpec as P


def rms_normed(values, norm_gain, axis):
    values = values.astype(jnp.float32)
    scale = lax.rsqrt(jnp.mean(values * values, axis=axis, keepdims=True) + 1e-05)
    return (values * scale * norm_gain).astype(jnp.bfloat16)


def gated(gate_pre, up_pre):
    return (gate_pre * jax.nn.sigmoid(1.702 * gate_pre) * (up_pre + 1.0)).astype(jnp.bfloat16)


def routed(
    tokens,
    norm_gain,
    expert_ids,
    route_weights,
    gate_weight,
    gate_bias,
    up_weight,
    up_bias,
    down_weight,
    down_bias,
    capacity,
):
    tok_rows, features = tokens.shape
    per_token = expert_ids.shape[1]
    experts = lax.axis_size("seq")
    quarter = features // lax.axis_size("rep")
    normed = rms_normed(tokens, norm_gain, -1)
    flat_ids = expert_ids.reshape(-1)
    onehot = (flat_ids[:, None] == jnp.arange(experts, dtype=jnp.int32)[None, :]).astype(jnp.int32)
    before = jnp.cumsum(onehot, axis=0) - onehot
    slot_index = jnp.sum(before * onehot, axis=1)
    destination = flat_ids * capacity + slot_index
    owner_row = jnp.arange(tok_rows * per_token, dtype=jnp.int32) // per_token
    buffer = jnp.zeros((experts * capacity, features), jnp.bfloat16)
    buffer = buffer.at[destination].set(normed[owner_row])
    received = lax.all_to_all(
        buffer.reshape(experts, capacity, features), "seq", split_axis=0, concat_axis=0, tiled=True
    )
    in_rows = received.reshape(-1, features)
    gate_pre = jnp.dot(in_rows, gate_weight[0], preferred_element_type=jnp.float32) + gate_bias[0]
    up_pre = jnp.dot(in_rows, up_weight[0], preferred_element_type=jnp.float32) + up_bias[0]
    partial_value = jnp.dot(
        gated(gate_pre, up_pre), down_weight[0], preferred_element_type=jnp.float32
    ).astype(jnp.bfloat16)
    summed = lax.psum_scatter(
        partial_value.reshape(experts, capacity, features),
        "rep",
        scatter_dimension=2,
        tiled=True,
    ).astype(jnp.float32)
    expert_out = (summed + down_bias[0][None, None, :]).astype(jnp.bfloat16)
    returned = lax.all_to_all(expert_out, "seq", split_axis=0, concat_axis=0, tiled=True)
    picked = returned.reshape(-1, quarter)[destination].reshape(tok_rows, per_token, quarter)
    mixed = jnp.sum(route_weights[:, :, None] * picked.astype(jnp.float32), axis=1)
    return mixed.astype(jnp.bfloat16)


tied = lax.optimization_barrier


def round_up(number, step):
    return -(-number // step) * step


def add_up(*terms):
    total = terms[0].astype(jnp.float32)
    for term in terms[1:]:
        total = total + term.astype(jnp.float32)
    return total.astype(jnp.bfloat16)


def padded(array, rows, columns):
    return jnp.pad(array, ((0, rows - array.shape[0]), (0, columns - array.shape[1])))


def column(row, size, lanes):
    return jnp.broadcast_to(padded(row, 1, size), (lanes, size)).T


def inward_kernel(groups, gate_ref, up_ref, biases_ref, weight_out, bias_out):
    features, hidden = gate_ref.shape
    quarter = features // groups
    hidden_pad, size = round_up(hidden, 128), round_up(quarter, 128)
    for n, weight in enumerate((gate_ref, up_ref)):
        values = weight[...].astype(jnp.float32)
        rows = slice(n * hidden_pad, (n + 1) * hidden_pad)
        for q in range(groups):
            part = padded(values[q * quarter : (q + 1) * quarter], size, hidden_pad)
            weight_out[rows, q * size : (q + 1) * size] = part.T.astype(jnp.bfloat16)
        bias_out[rows] = column(biases_ref[n : n + 1], hidden_pad, bias_out.shape[1])


def outward_kernel(groups, down_ref, biases_ref, weight_out, bias_out):
    hidden, features = down_ref.shape
    quarter = features // groups
    hidden_pad, size = round_up(hidden, 128), round_up(quarter, 128)
    values = padded(down_ref[...].astype(jnp.float32), hidden_pad, round_up(features, 128)).T
    for q in range(groups):
        part = padded(values[q * quarter : (q + 1) * quarter], size, hidden_pad)
        weight_out[q * size : (q + 1) * size] = part.astype(jnp.bfloat16)
    bias_out[...] = column(biases_ref[2:3], size, bias_out.shape[1])


def arrange(kernel, groups, lanes, arrays, shape, bias_rows):
    return pl.pallas_call(
        functools.partial(kernel, groups),
        out_shape=[
            jax.ShapeDtypeStruct(shape, jnp.bfloat16),
            jax.ShapeDtypeStruct((bias_rows, lanes), jnp.float32),
        ],
        compiler_params=pltpu.CompilerParams(vmem_limit_bytes=40 * 2**20),
        cost_estimate=pl.CostEstimate(
            flops=0, bytes_accessed=16 * arrays[0].size, transcendentals=0
        ),
    )(*arrays)


def fetch(sources, targets, sems):
    copies = [
        pltpu.make_async_copy(source, target, sems.at[n])
        for n, (source, target) in enumerate(zip(sources, targets))
    ]
    for copy in copies:
        copy.start()
    for copy in copies:
        copy.wait()


def pieces_kernel(groups, per, experts, *refs):
    sources, (one_ref, near_ref, far_ref) = refs[:4], refs[4:7]
    tokens_ref, gain_ref, ids_ref, weights_ref = refs[7:11]
    fetch(sources, refs[7:11], refs[11])
    features, lanes = tokens_ref.shape
    quarter = features // groups
    tail = one_ref.shape[0] - quarter
    rep = lax.axis_index("rep")
    values = tokens_ref[...].astype(jnp.float32)
    scale = lax.rsqrt(jnp.mean(values * values, axis=0, keepdims=True) + 1e-05)
    gain = jnp.broadcast_to(gain_ref[...].reshape(1, features), (lanes, features)).T
    normed = values * scale * gain
    row = lax.broadcasted_iota(jnp.int32, (tail, lanes), 0)
    chosen = lax.broadcasted_iota(jnp.int32, (round_up(experts, 8), lanes), 0)
    shares = jnp.zeros(chosen.shape, jnp.float32)
    for k in range(ids_ref.shape[0]):
        shares += jnp.where(ids_ref[k : k + 1] == chosen, weights_ref[k : k + 1], 0.0)
    terms = []
    for _ in range(3):
        term = shares.astype(jnp.bfloat16).astype(jnp.float32)
        terms.append(term)
        shares = shares - term
    for q in range(groups):
        rows = jnp.zeros((tail, lanes), jnp.float32)
        for n, term in enumerate(terms):
            for i in range(per):
                expert = q * per + i
                if expert < experts:
                    rows = jnp.where(row == n * per + i, term[expert : expert + 1], rows)
        piece = jnp.concatenate([normed[q * quarter : (q + 1) * quarter], rows], axis=0)
        piece = piece.astype(jnp.bfloat16)
        k = rep ^ q
        for side, target in enumerate((near_ref, far_ref)):

            @pl.when(k % 2 == side)
            def _(target=target, piece=piece, k=k):
                target[k // 2] = piece

        @pl.when(k == 0)
        def _(piece=piece):
            one_ref[...] = piece


def make_pieces(tokens, norm_gain, expert_ids, route_weights, groups, per, experts):
    features, lanes = tokens.shape
    rows = round_up(features // groups + 3 * per, 16)
    pair = jax.ShapeDtypeStruct((groups // 2, rows, lanes), jnp.bfloat16)
    arrays = (tokens, norm_gain, expert_ids, route_weights)
    return pl.pallas_call(
        functools.partial(pieces_kernel, groups, per, experts),
        in_specs=[pl.BlockSpec(memory_space=pltpu.HBM)] * 4,
        out_specs=[pl.BlockSpec(memory_space=pltpu.VMEM)] * 3,
        out_shape=[jax.ShapeDtypeStruct((rows, lanes), jnp.bfloat16), pair, pair],
        scratch_shapes=[pltpu.VMEM(a.shape, a.dtype) for a in arrays]
        + [pltpu.SemaphoreType.DMA((len(arrays),))],
        compiler_params=pltpu.CompilerParams(vmem_limit_bytes=60 * 2**20),
    )(*arrays)


def expert_kernel(quarter, per, blocks, slots, *refs):
    groups = len(blocks[0])
    counted = 1 + max(at for block in blocks for at, _ in block)
    arrays = refs[:counted]
    gate_up_ref, bias_ref, down_ref, down_bias_ref, keep_ref, send_ref = refs[counted : 6 + counted]
    scratch = refs[6 + counted :]
    _, piece_rows, lanes = arrays[0].shape
    size = gate_up_ref.shape[1] // groups
    hidden = gate_up_ref.shape[0] // 2
    rep, seq = lax.axis_index("rep"), lax.axis_index("seq")
    halves = len(scratch)
    count = len(blocks) // halves
    row = lax.broadcasted_iota(jnp.int32, (piece_rows - quarter, lanes), 0)
    for half in range(halves):
        rows_ref = scratch[half]
        if size > piece_rows:
            for k in range(groups):
                rows_ref[k * size + piece_rows : (k + 1) * size, :] = jnp.zeros(
                    (size - piece_rows, count * lanes), jnp.bfloat16
                )
        shares = [jnp.zeros((1, lanes), jnp.float32)] * count
        for k in range(groups):
            source = rep ^ k
            at_row = pl.ds(pl.multiple_of(source * size, size), piece_rows)
            mine = (lax.rem(row, per) == seq - source * per) & (row < 3 * per)
            for j in range(count):
                at, index = blocks[half * count + j][k]
                values = arrays[at][index]
                rows_ref[at_row, j * lanes : (j + 1) * lanes] = values
                terms = values.astype(jnp.float32)[quarter:]
                shares[j] += jnp.sum(jnp.where(mine, terms, 0.0), axis=0, keepdims=True)
        wide = jnp.concatenate(shares, axis=1)
        both = jnp.dot(gate_up_ref[...], rows_ref[...], preferred_element_type=jnp.float32)
        both = both + jnp.concatenate([bias_ref[...]] * count, axis=1)
        activated = gated(both[:hidden], both[hidden:])
        for k in range(groups):
            own_rows = down_ref[pl.ds(pl.multiple_of((rep ^ k) * size, size), size), :]
            rows = jnp.dot(own_rows, activated, preferred_element_type=jnp.float32)
            if k == 0:
                rows = rows + jnp.concatenate([down_bias_ref[...]] * count, axis=1)
            rows = (rows * wide).astype(jnp.bfloat16)
            target = send_ref if k % 2 else keep_ref
            for j in range(count):
                target[slots[half * count + j][k // 2]] = rows[:quarter, j * lanes : (j + 1) * lanes]


def run_expert(arrays, blocks, slots, weights, sizes, halves):
    quarter, per = sizes
    lanes = arrays[0].shape[2]
    gate_up, down = weights[0], weights[2]
    tokens = len(blocks) * lanes
    whole = pl.BlockSpec(memory_space=pltpu.VMEM)
    out = jax.ShapeDtypeStruct((2 * len(blocks), quarter, lanes), jnp.bfloat16)
    columns = tokens // halves
    return pl.pallas_call(
        functools.partial(expert_kernel, quarter, per, blocks, slots),
        in_specs=[whole] * (len(arrays) + len(weights)),
        out_specs=[whole, whole],
        out_shape=[out, out],
        scratch_shapes=[pltpu.VMEM((gate_up.shape[1], columns), jnp.bfloat16)] * halves,
        compiler_params=pltpu.CompilerParams(vmem_limit_bytes=40 * 2**20),
        cost_estimate=pl.CostEstimate(
            flops=4 * tokens * (gate_up.size + down.size),
            bytes_accessed=2 * (gate_up.size + down.size),
            transcendentals=0,
        ),
    )(*arrays, *weights)


def dense(
    tokens,
    norm_gain,
    expert_ids,
    route_weights,
    gate_weight,
    gate_bias,
    up_weight,
    up_bias,
    down_weight,
    down_bias,
):
    lanes, features = tokens.shape
    experts = lax.axis_size("seq")
    groups = lax.axis_size("rep")
    quarter = features // groups
    devices = experts * groups
    core, along_y, along_x, along_z = 1, 2, groups, 2 * groups

    def swap(array, step):
        return lax.ppermute(array, ("seq", "rep"), [(i, i ^ step) for i in range(devices)])

    per = -(-experts // groups)
    one, near, far = make_pieces(
        tokens.T, norm_gain, expert_ids.T, route_weights.T, groups, per, experts
    )
    z_2, z_3 = swap(one, 2 * along_z), swap(one, 3 * along_z)
    x_0 = swap(near, along_x)
    z_1, x_1 = swap(near, along_z), swap(near, along_z + along_x)
    hidden_pad = round_up(gate_weight.shape[2], 128)
    wide = groups * round_up(quarter, 128)
    biases = jnp.concatenate([gate_bias, up_bias, down_bias], axis=0)
    inward = arrange(
        inward_kernel,
        groups,
        lanes,
        (gate_weight[0], up_weight[0], biases),
        (2 * hidden_pad, wide),
        2 * hidden_pad,
    )
    z_2, z_3, inward = tied((z_2, z_3, inward))
    z_high = jnp.stack([z_2, z_3])
    diagonal = along_x + along_y
    x_high, y_high = swap(z_high, along_x), swap(z_high, along_y)
    d_high = swap(z_high, diagonal)
    outward = arrange(
        outward_kernel,
        groups,
        lanes,
        (down_weight[0], biases),
        (wide, hidden_pad),
        wide // groups,
    )
    x_0, outward = tied((x_0, outward))
    weights = (*inward, *outward)

    def pairs(first, step):
        return [[(first + step * x + k % 2, k // 2) for k in range(groups)] for x in range(2)]

    slots = ((0, 1), (2, 3))
    sizes = (quarter, per)
    keep_0, send_0 = run_expert(
        (near, far, x_0, swap(x_0, core)), pairs(0, 2), slots, weights, sizes, 1
    )
    y_high, d_high, keep_0, send_0, z_1, x_1 = tied(
        (y_high, d_high, keep_0, send_0, z_1, x_1)
    )
    got_0 = swap(send_0, core)
    high = (z_high, swap(z_high, core), y_high, swap(y_high, core))
    high = high + (x_high, swap(x_high, core), d_high, swap(d_high, core))
    got_0, high = tied((got_0, high))
    line = [[[(4 * x + k, n) for k in range(groups)] for x in range(2)] for n in range(2)]
    keep_2, send_2 = run_expert(high, line[0], slots, weights, sizes, 1)
    got_2 = swap(send_2, core)
    keep_2, high = tied((keep_2, high))
    keep_3, send_3 = run_expert(high, line[1], slots, weights, sizes, 1)
    got_2, keep_3, send_3 = tied((got_2, keep_3, send_3))
    got_3 = swap(send_3, core)

    def outer(first, second, at):
        return jnp.stack([add_up(keep[at], got[at]) for keep, got in (first, second)])

    far_lines = ((keep_2, got_2), (keep_3, got_3))
    y_sum, x_sum, d_sum = [outer(*far_lines, n) for n in (1, 2, 3)]
    near_1 = (z_1, swap(z_1, core), x_1, swap(x_1, core))
    y_sum, x_sum, d_sum, near_1, got_0 = tied((y_sum, x_sum, d_sum, near_1, got_0))
    y_sum = swap(y_sum, along_y)
    x_sum = swap(x_sum, along_x)
    d_sum = swap(d_sum, diagonal)
    keep_1, send_1 = run_expert(near_1, pairs(0, 2), slots, weights, sizes, 1)
    got_1 = swap(send_1, core)
    line_2 = add_up(keep_2[0], got_2[0], x_sum[0], y_sum[0], d_sum[0])
    line_3 = add_up(keep_3[0], got_3[0], x_sum[1], y_sum[1], d_sum[1])
    back_2, back_3 = swap(line_2, 2 * along_z), swap(line_3, 3 * along_z)
    near_lines = ((keep_0, got_0), (keep_1, got_1))
    x_near = swap(outer(*near_lines, 2), along_x)
    y_near = swap(outer(*near_lines, 1), along_y)
    d_near = swap(outer(*near_lines, 3), diagonal)
    _, _, x_near, y_near, d_near = tied((line_2, line_3, x_near, y_near, d_near))
    line_1 = add_up(keep_1[0], got_1[0], x_near[1], y_near[1], d_near[1])
    back_1 = swap(line_1, along_z)
    mixed = add_up(
        keep_0[0], got_0[0], x_near[0], y_near[0], d_near[0], back_1, back_2, back_3
    )
    return mixed.T


def on_device(*args):
    tokens, expert_ids = args[0], args[2]
    experts, groups = lax.axis_size("seq"), lax.axis_size("rep")
    capacity = 2 * tokens.shape[0] * expert_ids.shape[1] // experts
    if capacity >= tokens.shape[0] and experts == 2 * groups and groups == 4:
        return dense(*args)
    return routed(*args, capacity)


def solution(mesh):
    placed = (
        P("seq", None),
        P(),
        P("seq", None),
        P("seq", None),
        P("seq", None, "rep"),
        P("seq", "rep"),
        P("seq", None, "rep"),
        P("seq", "rep"),
        P("seq", "rep", None),
        P("seq", "rep"),
    )
    return jax.shard_map(
        on_device, mesh=mesh, in_specs=placed, out_specs=P("seq", "rep"), check_vma=False
    )
```

```python
import functools

import jax
import jax.numpy as jnp
from jax import lax
from jax.experimental import pallas as pl
from jax.experimental.pallas import tpu as pltpu
from jax.sharding import PartitionSpec as P


def rms_normed(values, norm_gain, axis):
    values = values.astype(jnp.float32)
    scale = lax.rsqrt(jnp.mean(values * values, axis=axis, keepdims=True) + 1e-05)
    return (values * scale * norm_gain).astype(jnp.bfloat16)


def gated(gate_pre, up_pre):
    return (gate_pre * jax.nn.sigmoid(1.702 * gate_pre) * (up_pre + 1.0)).astype(jnp.bfloat16)


def routed(
    tokens,
    norm_gain,
    expert_ids,
    route_weights,
    gate_weight,
    gate_bias,
    up_weight,
    up_bias,
    down_weight,
    down_bias,
    capacity,
):
    tok_rows, features = tokens.shape
    per_token = expert_ids.shape[1]
    experts = lax.axis_size("seq")
    quarter = features // lax.axis_size("rep")
    normed = rms_normed(tokens, norm_gain, -1)
    flat_ids = expert_ids.reshape(-1)
    onehot = (flat_ids[:, None] == jnp.arange(experts, dtype=jnp.int32)[None, :]).astype(jnp.int32)
    before = jnp.cumsum(onehot, axis=0) - onehot
    slot_index = jnp.sum(before * onehot, axis=1)
    destination = flat_ids * capacity + slot_index
    owner_row = jnp.arange(tok_rows * per_token, dtype=jnp.int32) // per_token
    buffer = jnp.zeros((experts * capacity, features), jnp.bfloat16)
    buffer = buffer.at[destination].set(normed[owner_row])
    received = lax.all_to_all(
        buffer.reshape(experts, capacity, features), "seq", split_axis=0, concat_axis=0, tiled=True
    )
    in_rows = received.reshape(-1, features)
    gate_pre = jnp.dot(in_rows, gate_weight[0], preferred_element_type=jnp.float32) + gate_bias[0]
    up_pre = jnp.dot(in_rows, up_weight[0], preferred_element_type=jnp.float32) + up_bias[0]
    partial_value = jnp.dot(
        gated(gate_pre, up_pre), down_weight[0], preferred_element_type=jnp.float32
    ).astype(jnp.bfloat16)
    summed = lax.psum_scatter(
        partial_value.reshape(experts, capacity, features),
        "rep",
        scatter_dimension=2,
        tiled=True,
    ).astype(jnp.float32)
    expert_out = (summed + down_bias[0][None, None, :]).astype(jnp.bfloat16)
    returned = lax.all_to_all(expert_out, "seq", split_axis=0, concat_axis=0, tiled=True)
    picked = returned.reshape(-1, quarter)[destination].reshape(tok_rows, per_token, quarter)
    mixed = jnp.sum(route_weights[:, :, None] * picked.astype(jnp.float32), axis=1)
    return mixed.astype(jnp.bfloat16)


tied = lax.optimization_barrier


def round_up(number, step):
    return -(-number // step) * step


def add_up(*terms):
    total = terms[0].astype(jnp.float32)
    for term in terms[1:]:
        total = total + term.astype(jnp.float32)
    return total.astype(jnp.bfloat16)


def padded(array, rows, columns):
    return jnp.pad(array, ((0, rows - array.shape[0]), (0, columns - array.shape[1])))


def column(row, size, lanes):
    return jnp.broadcast_to(padded(row, 1, size), (lanes, size)).T


def inward_kernel(groups, gate_ref, up_ref, biases_ref, weight_out, bias_out):
    features, hidden = gate_ref.shape
    quarter = features // groups
    hidden_pad, size = round_up(hidden, 128), round_up(quarter, 128)
    for n, weight in enumerate((gate_ref, up_ref)):
        values = weight[...].astype(jnp.float32)
        rows = slice(n * hidden_pad, (n + 1) * hidden_pad)
        for q in range(groups):
            part = padded(values[q * quarter : (q + 1) * quarter], size, hidden_pad)
            weight_out[rows, q * size : (q + 1) * size] = part.T.astype(jnp.bfloat16)
        bias_out[rows] = column(biases_ref[n : n + 1], hidden_pad, bias_out.shape[1])


def outward_kernel(groups, down_ref, biases_ref, weight_out, bias_out):
    hidden, features = down_ref.shape
    quarter = features // groups
    hidden_pad, size = round_up(hidden, 128), round_up(quarter, 128)
    values = padded(down_ref[...].astype(jnp.float32), hidden_pad, round_up(features, 128)).T
    for q in range(groups):
        part = padded(values[q * quarter : (q + 1) * quarter], size, hidden_pad)
        weight_out[q * size : (q + 1) * size] = part.astype(jnp.bfloat16)
    bias_out[...] = column(biases_ref[2:3], size, bias_out.shape[1])


def arrange(kernel, groups, lanes, arrays, shape, bias_rows):
    return pl.pallas_call(
        functools.partial(kernel, groups),
        out_shape=[
            jax.ShapeDtypeStruct(shape, jnp.bfloat16),
            jax.ShapeDtypeStruct((bias_rows, lanes), jnp.float32),
        ],
        compiler_params=pltpu.CompilerParams(vmem_limit_bytes=40 * 2**20),
        cost_estimate=pl.CostEstimate(flops=1, bytes_accessed=1, transcendentals=0),
    )(*arrays)


def fetch(sources, targets, sems):
    copies = [
        pltpu.make_async_copy(source, target, sems.at[n])
        for n, (source, target) in enumerate(zip(sources, targets))
    ]
    for copy in copies:
        copy.start()
    for copy in copies:
        copy.wait()


def pieces_kernel(groups, per, experts, *refs):
    sources, (one_ref, near_ref, far_ref) = refs[:4], refs[4:7]
    tokens_ref, gain_ref, ids_ref, weights_ref = refs[7:11]
    fetch(sources, refs[7:11], refs[11])
    features, lanes = tokens_ref.shape
    quarter = features // groups
    tail = one_ref.shape[0] - quarter
    rep = lax.axis_index("rep")
    values = tokens_ref[...].astype(jnp.float32)
    scale = lax.rsqrt(jnp.mean(values * values, axis=0, keepdims=True) + 1e-05)
    gain = jnp.broadcast_to(gain_ref[...].reshape(1, features), (lanes, features)).T
    normed = values * scale * gain
    row = lax.broadcasted_iota(jnp.int32, (tail, lanes), 0)
    chosen = lax.broadcasted_iota(jnp.int32, (round_up(experts, 8), lanes), 0)
    shares = jnp.zeros(chosen.shape, jnp.float32)
    for k in range(ids_ref.shape[0]):
        shares += jnp.where(ids_ref[k : k + 1] == chosen, weights_ref[k : k + 1], 0.0)
    terms = []
    for _ in range(3):
        term = shares.astype(jnp.bfloat16).astype(jnp.float32)
        terms.append(term)
        shares = shares - term
    for q in range(groups):
        rows = jnp.zeros((tail, lanes), jnp.float32)
        for n, term in enumerate(terms):
            for i in range(per):
                expert = q * per + i
                if expert < experts:
                    rows = jnp.where(row == n * per + i, term[expert : expert + 1], rows)
        piece = jnp.concatenate([normed[q * quarter : (q + 1) * quarter], rows], axis=0)
        piece = piece.astype(jnp.bfloat16)
        k = rep ^ q
        for side, target in enumerate((near_ref, far_ref)):

            @pl.when(k % 2 == side)
            def _(target=target, piece=piece, k=k):
                target[k // 2] = piece

        @pl.when(k == 0)
        def _(piece=piece):
            one_ref[...] = piece


def make_pieces(tokens, norm_gain, expert_ids, route_weights, groups, per, experts):
    features, lanes = tokens.shape
    rows = round_up(features // groups + 3 * per, 16)
    pair = jax.ShapeDtypeStruct((groups // 2, rows, lanes), jnp.bfloat16)
    arrays = (tokens, norm_gain, expert_ids, route_weights)
    return pl.pallas_call(
        functools.partial(pieces_kernel, groups, per, experts),
        in_specs=[pl.BlockSpec(memory_space=pltpu.HBM)] * 4,
        out_specs=[pl.BlockSpec(memory_space=pltpu.VMEM)] * 3,
        out_shape=[jax.ShapeDtypeStruct((rows, lanes), jnp.bfloat16), pair, pair],
        scratch_shapes=[pltpu.VMEM(a.shape, a.dtype) for a in arrays]
        + [pltpu.SemaphoreType.DMA((len(arrays),))],
        compiler_params=pltpu.CompilerParams(vmem_limit_bytes=60 * 2**20),
    )(*arrays)


def expert_kernel(quarter, per, blocks, slots, *refs):
    groups = len(blocks[0])
    counted = 1 + max(at for block in blocks for at, _ in block)
    arrays = refs[:counted]
    gate_up_ref, bias_ref, down_ref, down_bias_ref, keep_ref, send_ref = refs[counted : 6 + counted]
    scratch = refs[6 + counted :]
    _, piece_rows, lanes = arrays[0].shape
    size = gate_up_ref.shape[1] // groups
    hidden = gate_up_ref.shape[0] // 2
    rep, seq = lax.axis_index("rep"), lax.axis_index("seq")
    halves = len(scratch)
    count = len(blocks) // halves
    row = lax.broadcasted_iota(jnp.int32, (piece_rows - quarter, lanes), 0)
    for half in range(halves):
        rows_ref = scratch[half]
        if size > piece_rows:
            for k in range(groups):
                rows_ref[k * size + piece_rows : (k + 1) * size, :] = jnp.zeros(
                    (size - piece_rows, count * lanes), jnp.bfloat16
                )
        shares = [jnp.zeros((1, lanes), jnp.float32)] * count
        for k in range(groups):
            source = rep ^ k
            at_row = pl.ds(pl.multiple_of(source * size, size), piece_rows)
            mine = (lax.rem(row, per) == seq - source * per) & (row < 3 * per)
            for j in range(count):
                at, index = blocks[half * count + j][k]
                values = arrays[at][index]
                rows_ref[at_row, j * lanes : (j + 1) * lanes] = values
                terms = values.astype(jnp.float32)[quarter:]
                shares[j] += jnp.sum(jnp.where(mine, terms, 0.0), axis=0, keepdims=True)
        wide = jnp.concatenate(shares, axis=1)
        both = jnp.dot(gate_up_ref[...], rows_ref[...], preferred_element_type=jnp.float32)
        both = both + jnp.concatenate([bias_ref[...]] * count, axis=1)
        activated = gated(both[:hidden], both[hidden:])
        for k in range(groups):
            own_rows = down_ref[pl.ds(pl.multiple_of((rep ^ k) * size, size), size), :]
            rows = jnp.dot(own_rows, activated, preferred_element_type=jnp.float32)
            if k == 0:
                rows = rows + jnp.concatenate([down_bias_ref[...]] * count, axis=1)
            rows = (rows * wide).astype(jnp.bfloat16)
            target = send_ref if k % 2 else keep_ref
            for j in range(count):
                target[slots[half * count + j][k // 2]] = rows[:quarter, j * lanes : (j + 1) * lanes]


def run_expert(arrays, blocks, slots, weights, sizes, halves):
    quarter, per = sizes
    lanes = arrays[0].shape[2]
    gate_up, down = weights[0], weights[2]
    tokens = len(blocks) * lanes
    whole = pl.BlockSpec(memory_space=pltpu.VMEM)
    out = jax.ShapeDtypeStruct((2 * len(blocks), quarter, lanes), jnp.bfloat16)
    columns = tokens // halves
    return pl.pallas_call(
        functools.partial(expert_kernel, quarter, per, blocks, slots),
        in_specs=[whole] * (len(arrays) + len(weights)),
        out_specs=[whole, whole],
        out_shape=[out, out],
        scratch_shapes=[pltpu.VMEM((gate_up.shape[1], columns), jnp.bfloat16)] * halves,
        compiler_params=pltpu.CompilerParams(vmem_limit_bytes=40 * 2**20),
        cost_estimate=pl.CostEstimate(flops=1, bytes_accessed=1, transcendentals=0),
    )(*arrays, *weights)


def dense(
    tokens,
    norm_gain,
    expert_ids,
    route_weights,
    gate_weight,
    gate_bias,
    up_weight,
    up_bias,
    down_weight,
    down_bias,
):
    lanes, features = tokens.shape
    experts = lax.axis_size("seq")
    groups = lax.axis_size("rep")
    quarter = features // groups
    devices = experts * groups
    core, along_y, along_x, along_z = 1, 2, groups, 2 * groups

    def swap(array, step):
        return lax.ppermute(array, ("seq", "rep"), [(i, i ^ step) for i in range(devices)])

    per = -(-experts // groups)
    one, near, far = make_pieces(
        tokens.T, norm_gain, expert_ids.T, route_weights.T, groups, per, experts
    )
    z_2, z_3 = swap(one, 2 * along_z), swap(one, 3 * along_z)
    x_0 = swap(near, along_x)
    z_1 = swap(near, along_z)
    hidden_pad = round_up(gate_weight.shape[2], 128)
    wide = groups * round_up(quarter, 128)
    biases = jnp.concatenate([gate_bias, up_bias, down_bias], axis=0)
    inward = arrange(
        inward_kernel,
        groups,
        lanes,
        (gate_weight[0], up_weight[0], biases),
        (2 * hidden_pad, wide),
        2 * hidden_pad,
    )
    z_2, z_3, inward = tied((z_2, z_3, inward))
    z_high = jnp.stack([z_2, z_3])
    diagonal = along_x + along_y
    x_high, y_high = swap(z_high, along_x), swap(z_high, along_y)
    d_high = swap(z_high, diagonal)
    outward = arrange(
        outward_kernel,
        groups,
        lanes,
        (down_weight[0], biases),
        (wide, hidden_pad),
        wide // groups,
    )
    x_0, outward = tied((x_0, outward))
    weights = (*inward, *outward)

    def pairs(first, step):
        return [[(first + step * x + k % 2, k // 2) for k in range(groups)] for x in range(2)]

    slots = ((0, 1), (2, 3))
    sizes = (quarter, per)
    keep_0, send_0 = run_expert(
        (near, far, x_0, swap(x_0, core)), pairs(0, 2), slots, weights, sizes, 1
    )
    x_high, y_high, d_high, keep_0, send_0, z_1 = tied(
        (x_high, y_high, d_high, keep_0, send_0, z_1)
    )
    got_0 = swap(send_0, core)
    high = (z_high, swap(z_high, core), y_high, swap(y_high, core))
    high = high + (x_high, swap(x_high, core), d_high, swap(d_high, core))
    got_0, high = tied((got_0, high))
    line = [[[(4 * x + k, n) for k in range(groups)] for x in range(2)] for n in range(2)]
    keep_3, send_3 = run_expert(high, line[1], slots, weights, sizes, 1)
    got_3 = swap(send_3, core)
    keep_3, high, z_1 = tied((keep_3, high, z_1))
    x_1 = swap(z_1, along_x)
    keep_2, send_2 = run_expert(high, line[0], slots, weights, sizes, 1)
    got_3, keep_2, send_2 = tied((got_3, keep_2, send_2))
    got_2 = swap(send_2, core)

    def spread(keep, got):
        return [add_up(keep[n], got[n]) for n in (1, 2, 3)]

    def gather(parts):
        return [swap(part, step) for part, step in zip(parts, (along_y, along_x, diagonal))]

    parts_3 = gather(spread(keep_3, got_3))
    x_1, parts_3[0] = tied((x_1, parts_3[0]))
    near_1 = (z_1, swap(z_1, core), x_1, swap(x_1, core))
    near_1, got_2 = tied((near_1, got_2))
    keep_1, send_1 = run_expert(near_1, pairs(0, 2), slots, weights, sizes, 1)
    keep_1, send_1, got_2 = tied((keep_1, send_1, got_2))
    got_1 = swap(send_1, core)
    line_3 = add_up(keep_3[0], got_3[0], *parts_3)
    back_3 = swap(line_3, 3 * along_z)
    parts_2 = gather(spread(keep_2, got_2))
    near_parts = [
        jnp.stack(pair) for pair in zip(spread(keep_0, got_0), spread(keep_1, got_1))
    ]
    near_parts = gather(near_parts)
    line_2 = add_up(keep_2[0], got_2[0], *parts_2)
    back_2 = swap(line_2, 2 * along_z)
    near_parts, _ = tied((near_parts, line_2))
    line_1 = add_up(keep_1[0], got_1[0], *[part[1] for part in near_parts])
    back_1 = swap(line_1, along_z)
    mixed = add_up(
        keep_0[0], got_0[0], *[part[0] for part in near_parts], back_1, back_2, back_3
    )
    return mixed.T


def on_device(*args):
    tokens, expert_ids = args[0], args[2]
    experts, groups = lax.axis_size("seq"), lax.axis_size("rep")
    capacity = 2 * tokens.shape[0] * expert_ids.shape[1] // experts
    if capacity >= tokens.shape[0] and experts == 2 * groups and groups == 4:
        return dense(*args)
    return routed(*args, capacity)


def solution(mesh):
    placed = (
        P("seq", None),
        P(),
        P("seq", None),
        P("seq", None),
        P("seq", None, "rep"),
        P("seq", "rep"),
        P("seq", None, "rep"),
        P("seq", "rep"),
        P("seq", "rep", None),
        P("seq", "rep"),
    )
    return jax.shard_map(
        on_device, mesh=mesh, in_specs=placed, out_specs=P("seq", "rep"), check_vma=False
    )
```

```python
import functools

import jax
import jax.numpy as jnp
from jax import lax
from jax.experimental import pallas as pl
from jax.experimental.pallas import tpu as pltpu
from jax.sharding import PartitionSpec as P


def rms_normed(values, norm_gain, axis):
    values = values.astype(jnp.float32)
    scale = lax.rsqrt(jnp.mean(values * values, axis=axis, keepdims=True) + 1e-05)
    return (values * scale * norm_gain).astype(jnp.bfloat16)


def gated(gate_pre, up_pre):
    return (gate_pre * jax.nn.sigmoid(1.702 * gate_pre) * (up_pre + 1.0)).astype(jnp.bfloat16)


def routed(
    tokens,
    norm_gain,
    expert_ids,
    route_weights,
    gate_weight,
    gate_bias,
    up_weight,
    up_bias,
    down_weight,
    down_bias,
    capacity,
):
    tok_rows, features = tokens.shape
    per_token = expert_ids.shape[1]
    experts = lax.axis_size("seq")
    quarter = features // lax.axis_size("rep")
    normed = rms_normed(tokens, norm_gain, -1)
    flat_ids = expert_ids.reshape(-1)
    onehot = (flat_ids[:, None] == jnp.arange(experts, dtype=jnp.int32)[None, :]).astype(jnp.int32)
    before = jnp.cumsum(onehot, axis=0) - onehot
    slot_index = jnp.sum(before * onehot, axis=1)
    destination = flat_ids * capacity + slot_index
    owner_row = jnp.arange(tok_rows * per_token, dtype=jnp.int32) // per_token
    buffer = jnp.zeros((experts * capacity, features), jnp.bfloat16)
    buffer = buffer.at[destination].set(normed[owner_row])
    received = lax.all_to_all(
        buffer.reshape(experts, capacity, features), "seq", split_axis=0, concat_axis=0, tiled=True
    )
    in_rows = received.reshape(-1, features)
    gate_pre = jnp.dot(in_rows, gate_weight[0], preferred_element_type=jnp.float32) + gate_bias[0]
    up_pre = jnp.dot(in_rows, up_weight[0], preferred_element_type=jnp.float32) + up_bias[0]
    partial_value = jnp.dot(
        gated(gate_pre, up_pre), down_weight[0], preferred_element_type=jnp.float32
    ).astype(jnp.bfloat16)
    summed = lax.psum_scatter(
        partial_value.reshape(experts, capacity, features),
        "rep",
        scatter_dimension=2,
        tiled=True,
    ).astype(jnp.float32)
    expert_out = (summed + down_bias[0][None, None, :]).astype(jnp.bfloat16)
    returned = lax.all_to_all(expert_out, "seq", split_axis=0, concat_axis=0, tiled=True)
    picked = returned.reshape(-1, quarter)[destination].reshape(tok_rows, per_token, quarter)
    mixed = jnp.sum(route_weights[:, :, None] * picked.astype(jnp.float32), axis=1)
    return mixed.astype(jnp.bfloat16)


tied = lax.optimization_barrier


def round_up(number, step):
    return -(-number // step) * step


def add_up(*terms):
    total = terms[0].astype(jnp.float32)
    for term in terms[1:]:
        total = total + term.astype(jnp.float32)
    return total.astype(jnp.bfloat16)


def padded(array, rows, columns):
    return jnp.pad(array, ((0, rows - array.shape[0]), (0, columns - array.shape[1])))


def column(row, size, lanes):
    return jnp.broadcast_to(padded(row, 1, size), (lanes, size)).T


def inward_kernel(groups, gate_ref, up_ref, biases_ref, weight_out, bias_out):
    features, hidden = gate_ref.shape
    quarter = features // groups
    hidden_pad, size = round_up(hidden, 128), round_up(quarter, 128)
    for n, weight in enumerate((gate_ref, up_ref)):
        values = weight[...].astype(jnp.float32)
        rows = slice(n * hidden_pad, (n + 1) * hidden_pad)
        for q in range(groups):
            part = padded(values[q * quarter : (q + 1) * quarter], size, hidden_pad)
            weight_out[rows, q * size : (q + 1) * size] = part.T.astype(jnp.bfloat16)
        bias_out[rows] = column(biases_ref[n : n + 1], hidden_pad, bias_out.shape[1])


def outward_kernel(groups, down_ref, biases_ref, weight_out, bias_out):
    hidden, features = down_ref.shape
    quarter = features // groups
    hidden_pad, size = round_up(hidden, 128), round_up(quarter, 128)
    values = padded(down_ref[...].astype(jnp.float32), hidden_pad, round_up(features, 128)).T
    for q in range(groups):
        part = padded(values[q * quarter : (q + 1) * quarter], size, hidden_pad)
        weight_out[q * size : (q + 1) * size] = part.astype(jnp.bfloat16)
    bias_out[...] = column(biases_ref[2:3], size, bias_out.shape[1])


def arrange(kernel, groups, lanes, arrays, shape, bias_rows):
    return pl.pallas_call(
        functools.partial(kernel, groups),
        out_shape=[
            jax.ShapeDtypeStruct(shape, jnp.bfloat16),
            jax.ShapeDtypeStruct((bias_rows, lanes), jnp.float32),
        ],
        compiler_params=pltpu.CompilerParams(vmem_limit_bytes=40 * 2**20),
        cost_estimate=pl.CostEstimate(
            flops=0, bytes_accessed=16 * arrays[0].size, transcendentals=0
        ),
    )(*arrays)


def fetch(sources, targets, sems):
    copies = [
        pltpu.make_async_copy(source, target, sems.at[n])
        for n, (source, target) in enumerate(zip(sources, targets))
    ]
    for copy in copies:
        copy.start()
    for copy in copies:
        copy.wait()


def pieces_kernel(groups, per, experts, *refs):
    sources, (one_ref, near_ref, far_ref) = refs[:4], refs[4:7]
    tokens_ref, gain_ref, ids_ref, weights_ref = refs[7:11]
    fetch(sources, refs[7:11], refs[11])
    features, lanes = tokens_ref.shape
    quarter = features // groups
    tail = one_ref.shape[0] - quarter
    rep = lax.axis_index("rep")
    values = tokens_ref[...].astype(jnp.float32)
    scale = lax.rsqrt(jnp.mean(values * values, axis=0, keepdims=True) + 1e-05)
    gain = jnp.broadcast_to(gain_ref[...].reshape(1, features), (lanes, features)).T
    normed = values * scale * gain
    row = lax.broadcasted_iota(jnp.int32, (tail, lanes), 0)
    chosen = lax.broadcasted_iota(jnp.int32, (round_up(experts, 8), lanes), 0)
    shares = jnp.zeros(chosen.shape, jnp.float32)
    for k in range(ids_ref.shape[0]):
        shares += jnp.where(ids_ref[k : k + 1] == chosen, weights_ref[k : k + 1], 0.0)
    terms = []
    for _ in range(3):
        term = shares.astype(jnp.bfloat16).astype(jnp.float32)
        terms.append(term)
        shares = shares - term
    for q in range(groups):
        rows = jnp.zeros((tail, lanes), jnp.float32)
        for n, term in enumerate(terms):
            for i in range(per):
                expert = q * per + i
                if expert < experts:
                    rows = jnp.where(row == n * per + i, term[expert : expert + 1], rows)
        piece = jnp.concatenate([normed[q * quarter : (q + 1) * quarter], rows], axis=0)
        piece = piece.astype(jnp.bfloat16)
        k = rep ^ q
        for side, target in enumerate((near_ref, far_ref)):

            @pl.when(k % 2 == side)
            def _(target=target, piece=piece, k=k):
                target[k // 2] = piece

        @pl.when(k == 0)
        def _(piece=piece):
            one_ref[...] = piece


def make_pieces(tokens, norm_gain, expert_ids, route_weights, groups, per, experts):
    features, lanes = tokens.shape
    rows = round_up(features // groups + 3 * per, 16)
    pair = jax.ShapeDtypeStruct((groups // 2, rows, lanes), jnp.bfloat16)
    arrays = (tokens, norm_gain, expert_ids, route_weights)
    return pl.pallas_call(
        functools.partial(pieces_kernel, groups, per, experts),
        in_specs=[pl.BlockSpec(memory_space=pltpu.HBM)] * 4,
        out_specs=[pl.BlockSpec(memory_space=pltpu.VMEM)] * 3,
        out_shape=[jax.ShapeDtypeStruct((rows, lanes), jnp.bfloat16), pair, pair],
        scratch_shapes=[pltpu.VMEM(a.shape, a.dtype) for a in arrays]
        + [pltpu.SemaphoreType.DMA((len(arrays),))],
        compiler_params=pltpu.CompilerParams(vmem_limit_bytes=60 * 2**20),
    )(*arrays)


def expert_kernel(quarter, per, blocks, slots, *refs):
    groups = len(blocks[0])
    counted = 1 + max(at for block in blocks for at, _ in block)
    arrays = refs[:counted]
    gate_up_ref, bias_ref, down_ref, down_bias_ref, keep_ref, send_ref = refs[counted : 6 + counted]
    scratch = refs[6 + counted :]
    _, piece_rows, lanes = arrays[0].shape
    size = gate_up_ref.shape[1] // groups
    hidden = gate_up_ref.shape[0] // 2
    rep, seq = lax.axis_index("rep"), lax.axis_index("seq")
    halves = len(scratch)
    count = len(blocks) // halves
    row = lax.broadcasted_iota(jnp.int32, (piece_rows - quarter, lanes), 0)
    for half in range(halves):
        rows_ref = scratch[half]
        if size > piece_rows:
            for k in range(groups):
                rows_ref[k * size + piece_rows : (k + 1) * size, :] = jnp.zeros(
                    (size - piece_rows, count * lanes), jnp.bfloat16
                )
        shares = [jnp.zeros((1, lanes), jnp.float32)] * count
        for k in range(groups):
            source = rep ^ k
            at_row = pl.ds(pl.multiple_of(source * size, size), piece_rows)
            mine = (lax.rem(row, per) == seq - source * per) & (row < 3 * per)
            for j in range(count):
                at, index = blocks[half * count + j][k]
                values = arrays[at][index]
                rows_ref[at_row, j * lanes : (j + 1) * lanes] = values
                terms = values.astype(jnp.float32)[quarter:]
                shares[j] += jnp.sum(jnp.where(mine, terms, 0.0), axis=0, keepdims=True)
        wide = jnp.concatenate(shares, axis=1)
        both = jnp.dot(gate_up_ref[...], rows_ref[...], preferred_element_type=jnp.float32)
        both = both + jnp.concatenate([bias_ref[...]] * count, axis=1)
        activated = gated(both[:hidden], both[hidden:])
        for k in range(groups):
            own_rows = down_ref[pl.ds(pl.multiple_of((rep ^ k) * size, size), size), :]
            rows = jnp.dot(own_rows, activated, preferred_element_type=jnp.float32)
            if k == 0:
                rows = rows + jnp.concatenate([down_bias_ref[...]] * count, axis=1)
            rows = (rows * wide).astype(jnp.bfloat16)
            target = send_ref if k % 2 else keep_ref
            for j in range(count):
                target[slots[half * count + j][k // 2]] = rows[:quarter, j * lanes : (j + 1) * lanes]


def run_expert(arrays, blocks, slots, weights, sizes, halves):
    quarter, per = sizes
    lanes = arrays[0].shape[2]
    gate_up, down = weights[0], weights[2]
    tokens = len(blocks) * lanes
    whole = pl.BlockSpec(memory_space=pltpu.VMEM)
    out = jax.ShapeDtypeStruct((2 * len(blocks), quarter, lanes), jnp.bfloat16)
    columns = tokens // halves
    return pl.pallas_call(
        functools.partial(expert_kernel, quarter, per, blocks, slots),
        in_specs=[whole] * (len(arrays) + len(weights)),
        out_specs=[whole, whole],
        out_shape=[out, out],
        scratch_shapes=[pltpu.VMEM((gate_up.shape[1], columns), jnp.bfloat16)] * halves,
        compiler_params=pltpu.CompilerParams(vmem_limit_bytes=40 * 2**20),
        cost_estimate=pl.CostEstimate(
            flops=4 * tokens * (gate_up.size + down.size),
            bytes_accessed=2 * (gate_up.size + down.size),
            transcendentals=0,
        ),
    )(*arrays, *weights)


def dense(
    tokens,
    norm_gain,
    expert_ids,
    route_weights,
    gate_weight,
    gate_bias,
    up_weight,
    up_bias,
    down_weight,
    down_bias,
):
    lanes, features = tokens.shape
    experts = lax.axis_size("seq")
    groups = lax.axis_size("rep")
    quarter = features // groups
    devices = experts * groups
    core, along_y, along_x, along_z = 1, 2, groups, 2 * groups

    def swap(array, step):
        return lax.ppermute(array, ("seq", "rep"), [(i, i ^ step) for i in range(devices)])

    per = -(-experts // groups)
    one, near, far = make_pieces(
        tokens.T, norm_gain, expert_ids.T, route_weights.T, groups, per, experts
    )
    z_2, z_3 = swap(one, 2 * along_z), swap(one, 3 * along_z)
    x_0 = swap(near, along_x)
    hidden_pad = round_up(gate_weight.shape[2], 128)
    wide = groups * round_up(quarter, 128)
    biases = jnp.concatenate([gate_bias, up_bias, down_bias], axis=0)
    inward = arrange(
        inward_kernel,
        groups,
        lanes,
        (gate_weight[0], up_weight[0], biases),
        (2 * hidden_pad, wide),
        2 * hidden_pad,
    )
    z_2, z_3, inward = tied((z_2, z_3, inward))
    z_high = jnp.stack([z_2, z_3])
    diagonal = along_x + along_y
    x_high, y_high = swap(z_high, along_x), swap(z_high, along_y)
    d_high = swap(z_high, diagonal)
    outward = arrange(
        outward_kernel,
        groups,
        lanes,
        (down_weight[0], biases),
        (wide, hidden_pad),
        wide // groups,
    )
    x_0, outward = tied((x_0, outward))
    weights = (*inward, *outward)

    def pairs(first, step):
        return [[(first + step * x + k % 2, k // 2) for k in range(groups)] for x in range(2)]

    slots = ((0, 1), (2, 3))
    sizes = (quarter, per)
    keep_0, send_0 = run_expert(
        (near, far, x_0, swap(x_0, core)), pairs(0, 2), slots, weights, sizes, 1
    )
    z_near = swap(jnp.concatenate([near, x_0], axis=0), along_z)
    x_high, y_high, d_high, keep_0, send_0, z_near = tied(
        (x_high, y_high, d_high, keep_0, send_0, z_near)
    )
    got_0 = swap(send_0, core)
    high = (z_high, swap(z_high, core), y_high, swap(y_high, core))
    high = high + (x_high, swap(x_high, core), d_high, swap(d_high, core))
    near_1 = (z_near, swap(z_near, core))
    blocks = [[(k % 2, 2 * x + k // 2) for k in range(groups)] for x in range(2)]
    keep_1, send_1 = run_expert(near_1, blocks, slots, weights, sizes, 1)
    got_0, high, keep_1, send_1 = tied((got_0, high, keep_1, send_1))
    got_1 = swap(send_1, core)
    line = [[[(4 * x + k, n) for k in range(groups)] for x in range(2)] for n in range(2)]
    keep_2, send_2 = run_expert(high, line[0], slots, weights, sizes, 1)
    got_2 = swap(send_2, core)
    keep_2, high = tied((keep_2, high))
    keep_3, send_3 = run_expert(high, line[1], slots, weights, sizes, 1)
    got_2, keep_3, send_3 = tied((got_2, keep_3, send_3))
    got_3 = swap(send_3, core)
    got_1, got_3 = tied((got_1, got_3))
    z_back = swap(add_up(keep_1, got_1), along_z)

    def spread(*terms):
        return [add_up(*[term[n] for term in terms]) for n in (1, 2, 3)]

    def gather(parts):
        return [swap(part, step) for part, step in zip(parts, (along_y, along_x, diagonal))]

    far_sums = [jnp.stack(pair) for pair in zip(spread(keep_2, got_2), spread(keep_3, got_3))]
    far_sums = gather(far_sums)
    line_2 = add_up(keep_2[0], got_2[0], *[part[0] for part in far_sums])
    line_3 = add_up(keep_3[0], got_3[0], *[part[1] for part in far_sums])
    back_2, back_3 = swap(line_2, 2 * along_z), swap(line_3, 3 * along_z)
    z_back, _, _ = tied((z_back, line_2, line_3))
    near_sums = gather(spread(keep_0, got_0, z_back))
    mixed = add_up(keep_0[0], got_0[0], z_back[0], *near_sums, back_2, back_3)
    return mixed.T


def on_device(*args):
    tokens, expert_ids = args[0], args[2]
    experts, groups = lax.axis_size("seq"), lax.axis_size("rep")
    capacity = 2 * tokens.shape[0] * expert_ids.shape[1] // experts
    if capacity >= tokens.shape[0] and experts == 2 * groups and groups == 4:
        return dense(*args)
    return routed(*args, capacity)


def solution(mesh):
    placed = (
        P("seq", None),
        P(),
        P("seq", None),
        P("seq", None),
        P("seq", None, "rep"),
        P("seq", "rep"),
        P("seq", None, "rep"),
        P("seq", "rep"),
        P("seq", "rep", None),
        P("seq", "rep"),
    )
    return jax.shard_map(
        on_device, mesh=mesh, in_specs=placed, out_specs=P("seq", "rep"), check_vma=False
    )
```

```python
import functools

import jax
import jax.numpy as jnp
from jax import lax
from jax.experimental import pallas as pl
from jax.experimental.pallas import tpu as pltpu
from jax.sharding import PartitionSpec as P


def rms_normed(values, norm_gain, axis):
    values = values.astype(jnp.float32)
    scale = lax.rsqrt(jnp.mean(values * values, axis=axis, keepdims=True) + 1e-05)
    return (values * scale * norm_gain).astype(jnp.bfloat16)


def gated(gate_pre, up_pre):
    return (gate_pre * jax.nn.sigmoid(1.702 * gate_pre) * (up_pre + 1.0)).astype(jnp.bfloat16)


def routed(
    tokens,
    norm_gain,
    expert_ids,
    route_weights,
    gate_weight,
    gate_bias,
    up_weight,
    up_bias,
    down_weight,
    down_bias,
    capacity,
):
    tok_rows, features = tokens.shape
    per_token = expert_ids.shape[1]
    experts = lax.axis_size("seq")
    quarter = features // lax.axis_size("rep")
    normed = rms_normed(tokens, norm_gain, -1)
    flat_ids = expert_ids.reshape(-1)
    onehot = (flat_ids[:, None] == jnp.arange(experts, dtype=jnp.int32)[None, :]).astype(jnp.int32)
    before = jnp.cumsum(onehot, axis=0) - onehot
    slot_index = jnp.sum(before * onehot, axis=1)
    destination = flat_ids * capacity + slot_index
    owner_row = jnp.arange(tok_rows * per_token, dtype=jnp.int32) // per_token
    buffer = jnp.zeros((experts * capacity, features), jnp.bfloat16)
    buffer = buffer.at[destination].set(normed[owner_row])
    received = lax.all_to_all(
        buffer.reshape(experts, capacity, features), "seq", split_axis=0, concat_axis=0, tiled=True
    )
    in_rows = received.reshape(-1, features)
    gate_pre = jnp.dot(in_rows, gate_weight[0], preferred_element_type=jnp.float32) + gate_bias[0]
    up_pre = jnp.dot(in_rows, up_weight[0], preferred_element_type=jnp.float32) + up_bias[0]
    partial_value = jnp.dot(
        gated(gate_pre, up_pre), down_weight[0], preferred_element_type=jnp.float32
    ).astype(jnp.bfloat16)
    summed = lax.psum_scatter(
        partial_value.reshape(experts, capacity, features),
        "rep",
        scatter_dimension=2,
        tiled=True,
    ).astype(jnp.float32)
    expert_out = (summed + down_bias[0][None, None, :]).astype(jnp.bfloat16)
    returned = lax.all_to_all(expert_out, "seq", split_axis=0, concat_axis=0, tiled=True)
    picked = returned.reshape(-1, quarter)[destination].reshape(tok_rows, per_token, quarter)
    mixed = jnp.sum(route_weights[:, :, None] * picked.astype(jnp.float32), axis=1)
    return mixed.astype(jnp.bfloat16)


tied = lax.optimization_barrier


def round_up(number, step):
    return -(-number // step) * step


def add_up(*terms):
    total = terms[0].astype(jnp.float32)
    for term in terms[1:]:
        total = total + term.astype(jnp.float32)
    return total.astype(jnp.bfloat16)


def padded(array, rows, columns):
    return jnp.pad(array, ((0, rows - array.shape[0]), (0, columns - array.shape[1])))


def column(row, size, lanes):
    return jnp.broadcast_to(padded(row, 1, size), (lanes, size)).T


def inward_kernel(groups, gate_ref, up_ref, biases_ref, weight_out, bias_out):
    features, hidden = gate_ref.shape
    quarter = features // groups
    hidden_pad, size = round_up(hidden, 128), round_up(quarter, 128)
    for n, weight in enumerate((gate_ref, up_ref)):
        values = weight[...].astype(jnp.float32)
        rows = slice(n * hidden_pad, (n + 1) * hidden_pad)
        for q in range(groups):
            part = padded(values[q * quarter : (q + 1) * quarter], size, hidden_pad)
            weight_out[rows, q * size : (q + 1) * size] = part.T.astype(jnp.bfloat16)
        bias_out[rows] = column(biases_ref[n : n + 1], hidden_pad, bias_out.shape[1])


def outward_kernel(groups, down_ref, biases_ref, weight_out, bias_out):
    hidden, features = down_ref.shape
    quarter = features // groups
    hidden_pad, size = round_up(hidden, 128), round_up(quarter, 128)
    values = padded(down_ref[...].astype(jnp.float32), hidden_pad, round_up(features, 128)).T
    for q in range(groups):
        part = padded(values[q * quarter : (q + 1) * quarter], size, hidden_pad)
        weight_out[q * size : (q + 1) * size] = part.astype(jnp.bfloat16)
    bias_out[...] = column(biases_ref[2:3], size, bias_out.shape[1])


def arrange(kernel, groups, lanes, arrays, shape, bias_rows):
    return pl.pallas_call(
        functools.partial(kernel, groups),
        out_shape=[
            jax.ShapeDtypeStruct(shape, jnp.bfloat16),
            jax.ShapeDtypeStruct((bias_rows, lanes), jnp.float32),
        ],
        compiler_params=pltpu.CompilerParams(vmem_limit_bytes=40 * 2**20),
        cost_estimate=pl.CostEstimate(
            flops=0, bytes_accessed=16 * arrays[0].size, transcendentals=0
        ),
    )(*arrays)


def fetch(sources, targets, sems):
    copies = [
        pltpu.make_async_copy(source, target, sems.at[n])
        for n, (source, target) in enumerate(zip(sources, targets))
    ]
    for copy in copies:
        copy.start()
    for copy in copies:
        copy.wait()


def pieces_kernel(groups, per, experts, *refs):
    sources, (one_ref, near_ref, far_ref) = refs[:4], refs[4:7]
    tokens_ref, gain_ref, ids_ref, weights_ref = refs[7:11]
    fetch(sources, refs[7:11], refs[11])
    features, lanes = tokens_ref.shape
    quarter = features // groups
    tail = one_ref.shape[0] - quarter
    rep = lax.axis_index("rep")
    values = tokens_ref[...].astype(jnp.float32)
    scale = lax.rsqrt(jnp.mean(values * values, axis=0, keepdims=True) + 1e-05)
    gain = jnp.broadcast_to(gain_ref[...].reshape(1, features), (lanes, features)).T
    normed = values * scale * gain
    row = lax.broadcasted_iota(jnp.int32, (tail, lanes), 0)
    chosen = lax.broadcasted_iota(jnp.int32, (round_up(experts, 8), lanes), 0)
    shares = jnp.zeros(chosen.shape, jnp.float32)
    for k in range(ids_ref.shape[0]):
        shares += jnp.where(ids_ref[k : k + 1] == chosen, weights_ref[k : k + 1], 0.0)
    terms = []
    for _ in range(3):
        term = shares.astype(jnp.bfloat16).astype(jnp.float32)
        terms.append(term)
        shares = shares - term
    for q in range(groups):
        rows = jnp.zeros((tail, lanes), jnp.float32)
        for n, term in enumerate(terms):
            for i in range(per):
                expert = q * per + i
                if expert < experts:
                    rows = jnp.where(row == n * per + i, term[expert : expert + 1], rows)
        piece = jnp.concatenate([normed[q * quarter : (q + 1) * quarter], rows], axis=0)
        piece = piece.astype(jnp.bfloat16)
        k = rep ^ q
        for side, target in enumerate((near_ref, far_ref)):

            @pl.when(k % 2 == side)
            def _(target=target, piece=piece, k=k):
                target[k // 2] = piece

        @pl.when(k == 0)
        def _(piece=piece):
            one_ref[...] = piece


def make_pieces(tokens, norm_gain, expert_ids, route_weights, groups, per, experts):
    features, lanes = tokens.shape
    rows = round_up(features // groups + 3 * per, 16)
    pair = jax.ShapeDtypeStruct((groups // 2, rows, lanes), jnp.bfloat16)
    arrays = (tokens, norm_gain, expert_ids, route_weights)
    return pl.pallas_call(
        functools.partial(pieces_kernel, groups, per, experts),
        in_specs=[pl.BlockSpec(memory_space=pltpu.HBM)] * 4,
        out_specs=[pl.BlockSpec(memory_space=pltpu.VMEM)] * 3,
        out_shape=[jax.ShapeDtypeStruct((rows, lanes), jnp.bfloat16), pair, pair],
        scratch_shapes=[pltpu.VMEM(a.shape, a.dtype) for a in arrays]
        + [pltpu.SemaphoreType.DMA((len(arrays),))],
        compiler_params=pltpu.CompilerParams(vmem_limit_bytes=60 * 2**20),
    )(*arrays)


def expert_kernel(quarter, per, blocks, slots, *refs):
    groups = len(blocks[0])
    counted = 1 + max(at for block in blocks for at, _ in block)
    arrays = refs[:counted]
    gate_up_ref, bias_ref, down_ref, down_bias_ref, keep_ref, send_ref = refs[counted : 6 + counted]
    scratch = refs[6 + counted :]
    _, piece_rows, lanes = arrays[0].shape
    size = gate_up_ref.shape[1] // groups
    hidden = gate_up_ref.shape[0] // 2
    rep, seq = lax.axis_index("rep"), lax.axis_index("seq")
    halves = len(scratch)
    count = len(blocks) // halves
    row = lax.broadcasted_iota(jnp.int32, (piece_rows - quarter, lanes), 0)
    for half in range(halves):
        rows_ref = scratch[half]
        if size > piece_rows:
            for k in range(groups):
                rows_ref[k * size + piece_rows : (k + 1) * size, :] = jnp.zeros(
                    (size - piece_rows, count * lanes), jnp.bfloat16
                )
        shares = [jnp.zeros((1, lanes), jnp.float32)] * count
        for k in range(groups):
            source = rep ^ k
            at_row = pl.ds(pl.multiple_of(source * size, size), piece_rows)
            mine = (lax.rem(row, per) == seq - source * per) & (row < 3 * per)
            for j in range(count):
                at, index = blocks[half * count + j][k]
                values = arrays[at][index]
                rows_ref[at_row, j * lanes : (j + 1) * lanes] = values
                terms = values.astype(jnp.float32)[quarter:]
                shares[j] += jnp.sum(jnp.where(mine, terms, 0.0), axis=0, keepdims=True)
        wide = jnp.concatenate(shares, axis=1)
        both = jnp.dot(gate_up_ref[...], rows_ref[...], preferred_element_type=jnp.float32)
        both = both + jnp.concatenate([bias_ref[...]] * count, axis=1)
        activated = gated(both[:hidden], both[hidden:])
        for k in range(groups):
            own_rows = down_ref[pl.ds(pl.multiple_of((rep ^ k) * size, size), size), :]
            rows = jnp.dot(own_rows, activated, preferred_element_type=jnp.float32)
            if k == 0:
                rows = rows + jnp.concatenate([down_bias_ref[...]] * count, axis=1)
            rows = (rows * wide).astype(jnp.bfloat16)
            target = send_ref if k % 2 else keep_ref
            for j in range(count):
                target[slots[half * count + j][k // 2]] = rows[:quarter, j * lanes : (j + 1) * lanes]


def run_expert(arrays, blocks, slots, weights, sizes, halves):
    quarter, per = sizes
    lanes = arrays[0].shape[2]
    gate_up, down = weights[0], weights[2]
    tokens = len(blocks) * lanes
    whole = pl.BlockSpec(memory_space=pltpu.VMEM)
    out = jax.ShapeDtypeStruct((2 * len(blocks), quarter, lanes), jnp.bfloat16)
    columns = tokens // halves
    return pl.pallas_call(
        functools.partial(expert_kernel, quarter, per, blocks, slots),
        in_specs=[whole] * (len(arrays) + len(weights)),
        out_specs=[whole, whole],
        out_shape=[out, out],
        scratch_shapes=[pltpu.VMEM((gate_up.shape[1], columns), jnp.bfloat16)] * halves,
        compiler_params=pltpu.CompilerParams(vmem_limit_bytes=40 * 2**20),
        cost_estimate=pl.CostEstimate(
            flops=4 * tokens * (gate_up.size + down.size),
            bytes_accessed=2 * (gate_up.size + down.size),
            transcendentals=0,
        ),
    )(*arrays, *weights)


def dense(
    tokens,
    norm_gain,
    expert_ids,
    route_weights,
    gate_weight,
    gate_bias,
    up_weight,
    up_bias,
    down_weight,
    down_bias,
):
    lanes, features = tokens.shape
    experts = lax.axis_size("seq")
    groups = lax.axis_size("rep")
    quarter = features // groups
    devices = experts * groups
    core, along_y, along_x, along_z = 1, 2, groups, 2 * groups

    def swap(array, step):
        return lax.ppermute(array, ("seq", "rep"), [(i, i ^ step) for i in range(devices)])

    per = -(-experts // groups)
    one, near, far = make_pieces(
        tokens.T, norm_gain, expert_ids.T, route_weights.T, groups, per, experts
    )
    z_2, z_3 = swap(one, 2 * along_z), swap(one, 3 * along_z)
    x_0 = swap(near, along_x)
    hidden_pad = round_up(gate_weight.shape[2], 128)
    wide = groups * round_up(quarter, 128)
    biases = jnp.concatenate([gate_bias, up_bias, down_bias], axis=0)
    inward = arrange(
        inward_kernel,
        groups,
        lanes,
        (gate_weight[0], up_weight[0], biases),
        (2 * hidden_pad, wide),
        2 * hidden_pad,
    )
    z_2, z_3, inward = tied((z_2, z_3, inward))
    z_high = jnp.stack([z_2, z_3])
    diagonal = along_x + along_y
    x_high, y_high = swap(z_high, along_x), swap(z_high, along_y)
    d_high = swap(z_high, diagonal)
    outward = arrange(
        outward_kernel,
        groups,
        lanes,
        (down_weight[0], biases),
        (wide, hidden_pad),
        wide // groups,
    )
    x_0, outward = tied((x_0, outward))
    weights = (*inward, *outward)

    def pairs(first, step):
        return [[(first + step * x + k % 2, k // 2) for k in range(groups)] for x in range(2)]

    slots = ((0, 1), (2, 3))
    sizes = (quarter, per)
    keep_0, send_0 = run_expert(
        (near, far, x_0, swap(x_0, core)), pairs(0, 2), slots, weights, sizes, 1
    )
    z_near = swap(jnp.concatenate([near, x_0], axis=0), along_z)
    x_high, y_high, d_high, keep_0, send_0, z_near = tied(
        (x_high, y_high, d_high, keep_0, send_0, z_near)
    )
    got_0 = swap(send_0, core)
    high = (z_high, swap(z_high, core), y_high, swap(y_high, core))
    high = high + (x_high, swap(x_high, core), d_high, swap(d_high, core))
    got_0, high = tied((got_0, high))
    line = [[[(4 * x + k, n) for k in range(groups)] for x in range(2)] for n in range(2)]
    keep_2, send_2 = run_expert(high, line[0], slots, weights, sizes, 1)
    got_2 = swap(send_2, core)
    keep_2, high, z_near = tied((keep_2, high, z_near))
    near_1 = (z_near, swap(z_near, core))
    keep_3, send_3 = run_expert(high, line[1], slots, weights, sizes, 1)
    got_2, keep_3, send_3, near_1 = tied((got_2, keep_3, send_3, near_1))
    got_3 = swap(send_3, core)
    blocks = [[(k % 2, 2 * x + k // 2) for k in range(groups)] for x in range(2)]
    keep_1, send_1 = run_expert(near_1, blocks, slots, weights, sizes, 1)
    got_1 = swap(send_1, core)
    keep_1, got_3 = tied((keep_1, got_3))
    z_back = swap(add_up(keep_1, got_1), along_z)

    def spread(*terms):
        return [add_up(*[term[n] for term in terms]) for n in (2, 3, 1)]

    def gather(parts):
        return [swap(part, step) for part, step in zip(parts, (along_x, diagonal, along_y))]

    far_sums = [jnp.stack(pair) for pair in zip(spread(keep_2, got_2), spread(keep_3, got_3))]
    far_sums = gather(far_sums)
    line_2 = add_up(keep_2[0], got_2[0], *[part[0] for part in far_sums])
    line_3 = add_up(keep_3[0], got_3[0], *[part[1] for part in far_sums])
    back_2, back_3 = swap(line_2, 2 * along_z), swap(line_3, 3 * along_z)
    z_back, _, _ = tied((z_back, line_2, line_3))
    near_sums = gather(spread(keep_0, got_0, z_back))
    mixed = add_up(keep_0[0], got_0[0], z_back[0], *near_sums, back_2, back_3)
    return mixed.T


def on_device(*args):
    tokens, expert_ids = args[0], args[2]
    experts, groups = lax.axis_size("seq"), lax.axis_size("rep")
    capacity = 2 * tokens.shape[0] * expert_ids.shape[1] // experts
    if capacity >= tokens.shape[0] and experts == 2 * groups and groups == 4:
        return dense(*args)
    return routed(*args, capacity)


def solution(mesh):
    placed = (
        P("seq", None),
        P(),
        P("seq", None),
        P("seq", None),
        P("seq", None, "rep"),
        P("seq", "rep"),
        P("seq", None, "rep"),
        P("seq", "rep"),
        P("seq", "rep", None),
        P("seq", "rep"),
    )
    return jax.shard_map(
        on_device, mesh=mesh, in_specs=placed, out_specs=P("seq", "rep"), check_vma=False
    )
```

```python
import functools

import jax
import jax.numpy as jnp
from jax import lax
from jax.experimental import pallas as pl
from jax.experimental.pallas import tpu as pltpu
from jax.sharding import PartitionSpec as P


def rms_normed(values, norm_gain, axis):
    values = values.astype(jnp.float32)
    scale = lax.rsqrt(jnp.mean(values * values, axis=axis, keepdims=True) + 1e-05)
    return (values * scale * norm_gain).astype(jnp.bfloat16)


def gated(gate_pre, up_pre):
    return (gate_pre * jax.nn.sigmoid(1.702 * gate_pre) * (up_pre + 1.0)).astype(jnp.bfloat16)


def routed(
    tokens,
    norm_gain,
    expert_ids,
    route_weights,
    gate_weight,
    gate_bias,
    up_weight,
    up_bias,
    down_weight,
    down_bias,
    capacity,
):
    tok_rows, features = tokens.shape
    per_token = expert_ids.shape[1]
    experts = lax.axis_size("seq")
    quarter = features // lax.axis_size("rep")
    normed = rms_normed(tokens, norm_gain, -1)
    flat_ids = expert_ids.reshape(-1)
    onehot = (flat_ids[:, None] == jnp.arange(experts, dtype=jnp.int32)[None, :]).astype(jnp.int32)
    before = jnp.cumsum(onehot, axis=0) - onehot
    slot_index = jnp.sum(before * onehot, axis=1)
    destination = flat_ids * capacity + slot_index
    owner_row = jnp.arange(tok_rows * per_token, dtype=jnp.int32) // per_token
    buffer = jnp.zeros((experts * capacity, features), jnp.bfloat16)
    buffer = buffer.at[destination].set(normed[owner_row])
    received = lax.all_to_all(
        buffer.reshape(experts, capacity, features), "seq", split_axis=0, concat_axis=0, tiled=True
    )
    in_rows = received.reshape(-1, features)
    gate_pre = jnp.dot(in_rows, gate_weight[0], preferred_element_type=jnp.float32) + gate_bias[0]
    up_pre = jnp.dot(in_rows, up_weight[0], preferred_element_type=jnp.float32) + up_bias[0]
    partial_value = jnp.dot(
        gated(gate_pre, up_pre), down_weight[0], preferred_element_type=jnp.float32
    ).astype(jnp.bfloat16)
    summed = lax.psum_scatter(
        partial_value.reshape(experts, capacity, features),
        "rep",
        scatter_dimension=2,
        tiled=True,
    ).astype(jnp.float32)
    expert_out = (summed + down_bias[0][None, None, :]).astype(jnp.bfloat16)
    returned = lax.all_to_all(expert_out, "seq", split_axis=0, concat_axis=0, tiled=True)
    picked = returned.reshape(-1, quarter)[destination].reshape(tok_rows, per_token, quarter)
    mixed = jnp.sum(route_weights[:, :, None] * picked.astype(jnp.float32), axis=1)
    return mixed.astype(jnp.bfloat16)


tied = lax.optimization_barrier


def round_up(number, step):
    return -(-number // step) * step


def add_up(*terms):
    total = terms[0].astype(jnp.float32)
    for term in terms[1:]:
        total = total + term.astype(jnp.float32)
    return total.astype(jnp.bfloat16)


def padded(array, rows, columns):
    return jnp.pad(array, ((0, rows - array.shape[0]), (0, columns - array.shape[1])))


def column(row, size, lanes):
    return jnp.broadcast_to(padded(row, 1, size), (lanes, size)).T


def inward_kernel(groups, gate_ref, up_ref, biases_ref, weight_out, bias_out):
    features, hidden = gate_ref.shape
    quarter = features // groups
    hidden_pad, size = round_up(hidden, 128), round_up(quarter, 128)
    for n, weight in enumerate((gate_ref, up_ref)):
        values = weight[...].astype(jnp.float32)
        rows = slice(n * hidden_pad, (n + 1) * hidden_pad)
        for q in range(groups):
            part = padded(values[q * quarter : (q + 1) * quarter], size, hidden_pad)
            weight_out[rows, q * size : (q + 1) * size] = part.T.astype(jnp.bfloat16)
        bias_out[rows] = column(biases_ref[n : n + 1], hidden_pad, bias_out.shape[1])


def outward_kernel(groups, down_ref, biases_ref, weight_out, bias_out):
    hidden, features = down_ref.shape
    quarter = features // groups
    hidden_pad, size = round_up(hidden, 128), round_up(quarter, 128)
    values = padded(down_ref[...].astype(jnp.float32), hidden_pad, round_up(features, 128)).T
    for q in range(groups):
        part = padded(values[q * quarter : (q + 1) * quarter], size, hidden_pad)
        weight_out[q * size : (q + 1) * size] = part.astype(jnp.bfloat16)
    bias_out[...] = column(biases_ref[2:3], size, bias_out.shape[1])


def arrange(kernel, groups, lanes, arrays, shape, bias_rows):
    return pl.pallas_call(
        functools.partial(kernel, groups),
        out_shape=[
            jax.ShapeDtypeStruct(shape, jnp.bfloat16),
            jax.ShapeDtypeStruct((bias_rows, lanes), jnp.float32),
        ],
        compiler_params=pltpu.CompilerParams(vmem_limit_bytes=40 * 2**20),
        cost_estimate=pl.CostEstimate(
            flops=0, bytes_accessed=16 * arrays[0].size, transcendentals=0
        ),
    )(*arrays)


def fetch(sources, targets, sems):
    copies = [
        pltpu.make_async_copy(source, target, sems.at[n])
        for n, (source, target) in enumerate(zip(sources, targets))
    ]
    for copy in copies:
        copy.start()
    for copy in copies:
        copy.wait()


def pieces_kernel(groups, per, experts, *refs):
    sources, (one_ref, near_ref, far_ref) = refs[:4], refs[4:7]
    tokens_ref, gain_ref, ids_ref, weights_ref = refs[7:11]
    fetch(sources, refs[7:11], refs[11])
    features, lanes = tokens_ref.shape
    quarter = features // groups
    tail = one_ref.shape[0] - quarter
    rep = lax.axis_index("rep")
    values = tokens_ref[...].astype(jnp.float32)
    scale = lax.rsqrt(jnp.mean(values * values, axis=0, keepdims=True) + 1e-05)
    gain = jnp.broadcast_to(gain_ref[...].reshape(1, features), (lanes, features)).T
    normed = values * scale * gain
    row = lax.broadcasted_iota(jnp.int32, (tail, lanes), 0)
    chosen = lax.broadcasted_iota(jnp.int32, (round_up(experts, 8), lanes), 0)
    shares = jnp.zeros(chosen.shape, jnp.float32)
    for k in range(ids_ref.shape[0]):
        shares += jnp.where(ids_ref[k : k + 1] == chosen, weights_ref[k : k + 1], 0.0)
    terms = []
    for _ in range(3):
        term = shares.astype(jnp.bfloat16).astype(jnp.float32)
        terms.append(term)
        shares = shares - term
    for q in range(groups):
        rows = jnp.zeros((tail, lanes), jnp.float32)
        for n, term in enumerate(terms):
            for i in range(per):
                expert = q * per + i
                if expert < experts:
                    rows = jnp.where(row == n * per + i, term[expert : expert + 1], rows)
        piece = jnp.concatenate([normed[q * quarter : (q + 1) * quarter], rows], axis=0)
        piece = piece.astype(jnp.bfloat16)
        k = rep ^ q
        for side, target in enumerate((near_ref, far_ref)):

            @pl.when(k % 2 == side)
            def _(target=target, piece=piece, k=k):
                target[k // 2] = piece

        @pl.when(k == 0)
        def _(piece=piece):
            one_ref[...] = piece


def make_pieces(tokens, norm_gain, expert_ids, route_weights, groups, per, experts):
    features, lanes = tokens.shape
    rows = round_up(features // groups + 3 * per, 16)
    pair = jax.ShapeDtypeStruct((groups // 2, rows, lanes), jnp.bfloat16)
    arrays = (tokens, norm_gain, expert_ids, route_weights)
    return pl.pallas_call(
        functools.partial(pieces_kernel, groups, per, experts),
        in_specs=[pl.BlockSpec(memory_space=pltpu.HBM)] * 4,
        out_specs=[pl.BlockSpec(memory_space=pltpu.VMEM)] * 3,
        out_shape=[jax.ShapeDtypeStruct((rows, lanes), jnp.bfloat16), pair, pair],
        scratch_shapes=[pltpu.VMEM(a.shape, a.dtype) for a in arrays]
        + [pltpu.SemaphoreType.DMA((len(arrays),))],
        compiler_params=pltpu.CompilerParams(vmem_limit_bytes=60 * 2**20),
    )(*arrays)


def expert_kernel(quarter, per, blocks, slots, *refs):
    groups = len(blocks[0])
    counted = 1 + max(at for block in blocks for at, _ in block)
    arrays = refs[:counted]
    gate_up_ref, bias_ref, down_ref, down_bias_ref, keep_ref, send_ref = refs[counted : 6 + counted]
    scratch = refs[6 + counted :]
    _, piece_rows, lanes = arrays[0].shape
    size = gate_up_ref.shape[1] // groups
    hidden = gate_up_ref.shape[0] // 2
    rep, seq = lax.axis_index("rep"), lax.axis_index("seq")
    halves = len(scratch)
    count = len(blocks) // halves
    row = lax.broadcasted_iota(jnp.int32, (piece_rows - quarter, lanes), 0)
    for half in range(halves):
        rows_ref = scratch[half]
        if size > piece_rows:
            for k in range(groups):
                rows_ref[k * size + piece_rows : (k + 1) * size, :] = jnp.zeros(
                    (size - piece_rows, count * lanes), jnp.bfloat16
                )
        shares = [jnp.zeros((1, lanes), jnp.float32)] * count
        for k in range(groups):
            source = rep ^ k
            at_row = pl.ds(pl.multiple_of(source * size, size), piece_rows)
            mine = (lax.rem(row, per) == seq - source * per) & (row < 3 * per)
            for j in range(count):
                at, index = blocks[half * count + j][k]
                values = arrays[at][index]
                rows_ref[at_row, j * lanes : (j + 1) * lanes] = values
                terms = values.astype(jnp.float32)[quarter:]
                shares[j] += jnp.sum(jnp.where(mine, terms, 0.0), axis=0, keepdims=True)
        wide = jnp.concatenate(shares, axis=1)
        both = jnp.dot(gate_up_ref[...], rows_ref[...], preferred_element_type=jnp.float32)
        both = both + jnp.concatenate([bias_ref[...]] * count, axis=1)
        activated = gated(both[:hidden], both[hidden:])
        for k in range(groups):
            own_rows = down_ref[pl.ds(pl.multiple_of((rep ^ k) * size, size), size), :]
            rows = jnp.dot(own_rows, activated, preferred_element_type=jnp.float32)
            if k == 0:
                rows = rows + jnp.concatenate([down_bias_ref[...]] * count, axis=1)
            rows = (rows * wide).astype(jnp.bfloat16)
            target = send_ref if k % 2 else keep_ref
            for j in range(count):
                target[slots[half * count + j][k // 2]] = rows[:quarter, j * lanes : (j + 1) * lanes]


def run_expert(arrays, blocks, slots, weights, sizes, halves):
    quarter, per = sizes
    lanes = arrays[0].shape[2]
    gate_up, down = weights[0], weights[2]
    tokens = len(blocks) * lanes
    whole = pl.BlockSpec(memory_space=pltpu.VMEM)
    out = jax.ShapeDtypeStruct((2 * len(blocks), quarter, lanes), jnp.bfloat16)
    columns = tokens // halves
    return pl.pallas_call(
        functools.partial(expert_kernel, quarter, per, blocks, slots),
        in_specs=[whole] * (len(arrays) + len(weights)),
        out_specs=[whole, whole],
        out_shape=[out, out],
        scratch_shapes=[pltpu.VMEM((gate_up.shape[1], columns), jnp.bfloat16)] * halves,
        compiler_params=pltpu.CompilerParams(vmem_limit_bytes=40 * 2**20),
        cost_estimate=pl.CostEstimate(
            flops=4 * tokens * (gate_up.size + down.size),
            bytes_accessed=2 * (gate_up.size + down.size),
            transcendentals=0,
        ),
    )(*arrays, *weights)


def dense(
    tokens,
    norm_gain,
    expert_ids,
    route_weights,
    gate_weight,
    gate_bias,
    up_weight,
    up_bias,
    down_weight,
    down_bias,
):
    lanes, features = tokens.shape
    experts = lax.axis_size("seq")
    groups = lax.axis_size("rep")
    quarter = features // groups
    devices = experts * groups
    core, along_y, along_x, along_z = 1, 2, groups, 2 * groups

    def swap(array, step):
        return lax.ppermute(array, ("seq", "rep"), [(i, i ^ step) for i in range(devices)])

    per = -(-experts // groups)
    one, near, far = make_pieces(
        tokens.T, norm_gain, expert_ids.T, route_weights.T, groups, per, experts
    )
    z_2, z_3 = swap(one, 2 * along_z), swap(one, 3 * along_z)
    x_0 = swap(near, along_x)
    hidden_pad = round_up(gate_weight.shape[2], 128)
    wide = groups * round_up(quarter, 128)
    biases = jnp.concatenate([gate_bias, up_bias, down_bias], axis=0)
    inward = arrange(
        inward_kernel,
        groups,
        lanes,
        (gate_weight[0], up_weight[0], biases),
        (2 * hidden_pad, wide),
        2 * hidden_pad,
    )
    z_2, z_3, inward = tied((z_2, z_3, inward))
    z_high = jnp.stack([z_2, z_3])
    diagonal = along_x + along_y
    y_high, d_high = swap(z_high, along_y), swap(z_high, diagonal)
    x_high = swap(z_high, along_x)
    outward = arrange(
        outward_kernel,
        groups,
        lanes,
        (down_weight[0], biases),
        (wide, hidden_pad),
        wide // groups,
    )
    x_0, outward = tied((x_0, outward))
    weights = (*inward, *outward)

    def expert(arrays, blocks):
        return run_expert(arrays, blocks, ((0, 2), (1, 3)), weights, (quarter, per), 1)

    def pieces(arrays, first):
        return [(arrays[k % 2], first + k // 2) for k in range(groups)]

    z_near = swap(jnp.concatenate([near, x_0], axis=0), along_z)
    own, other = pieces((0, 1), 0), pieces((2, 3), 0)
    lines = [[(k, n) for k in range(groups)] for n in range(2)]

    keep_0, send_0 = expert((near, far, x_0, swap(x_0, core)), [own, other])
    z_core, y_core, d_core = [swap(array, core) for array in (z_high, y_high, d_high)]
    x_high, y_core, d_core, z_core, keep_0, z_near = tied(
        (x_high, y_core, d_core, z_core, keep_0, z_near)
    )
    far_own = (z_high, z_core, y_high, y_core)
    far_other = (x_high, swap(x_high, core), d_high, d_core)
    keep_q, send_q = expert(far_own, lines)
    keep_q, far_other, z_near = tied((keep_q, far_other, z_near))
    near_1 = (z_near, swap(z_near, core))
    keep_s, send_s = expert(far_other, lines)
    got_q = swap(send_q, core)
    got_q, keep_s = tied((got_q, keep_s))
    keep_s, send_s, near_1 = tied((keep_s, send_s, near_1))
    keep_1, send_1 = expert(near_1, [pieces((0, 1), 0), pieces((0, 1), 2)])
    got_s = swap(send_s, core)
    keep_1, send_0, got_s = tied((keep_1, send_0, got_s))
    got_1, got_0 = swap(send_1, core), swap(send_0, core)
    far_y, far_x, far_d = [
        add_up(keep[at : at + 2], got[at : at + 2])
        for keep, got, at in ((keep_q, got_q, 2), (keep_s, got_s, 0), (keep_s, got_s, 2))
    ]
    far_x, far_d, far_y = tied((far_x, far_d, far_y))
    z_back = swap(add_up(keep_1, got_1), along_z)
    far_sums = [swap(far_x, along_x), swap(far_d, diagonal), swap(far_y, along_y)]
    line_2, line_3 = [
        add_up(keep_q[n], got_q[n], *[part[n] for part in far_sums]) for n in range(2)
    ]
    back_2, back_3 = swap(line_2, 2 * along_z), swap(line_3, 3 * along_z)
    z_back, _, _ = tied((z_back, line_2, line_3))
    terms = (keep_0, got_0, z_back)
    near_sums = [
        swap(add_up(*[term[at] for term in terms]), step)
        for at, step in ((1, along_x), (3, diagonal), (2, along_y))
    ]
    mixed = add_up(*[term[0] for term in terms], *near_sums, back_2, back_3)
    return mixed.T


def on_device(*args):
    tokens, expert_ids = args[0], args[2]
    experts, groups = lax.axis_size("seq"), lax.axis_size("rep")
    capacity = 2 * tokens.shape[0] * expert_ids.shape[1] // experts
    if capacity >= tokens.shape[0] and experts == 2 * groups and groups == 4:
        return dense(*args)
    return routed(*args, capacity)


def solution(mesh):
    placed = (
        P("seq", None),
        P(),
        P("seq", None),
        P("seq", None),
        P("seq", None, "rep"),
        P("seq", "rep"),
        P("seq", None, "rep"),
        P("seq", "rep"),
        P("seq", "rep", None),
        P("seq", "rep"),
    )
    return jax.shard_map(
        on_device, mesh=mesh, in_specs=placed, out_specs=P("seq", "rep"), check_vma=False
    )
```

```python
import functools

import jax
import jax.numpy as jnp
from jax import lax
from jax.experimental import pallas as pl
from jax.experimental.pallas import tpu as pltpu
from jax.sharding import PartitionSpec as P


def rms_normed(values, norm_gain, axis):
    values = values.astype(jnp.float32)
    scale = lax.rsqrt(jnp.mean(values * values, axis=axis, keepdims=True) + 1e-05)
    return (values * scale * norm_gain).astype(jnp.bfloat16)


def gated(gate_pre, up_pre):
    return (gate_pre * jax.nn.sigmoid(1.702 * gate_pre) * (up_pre + 1.0)).astype(jnp.bfloat16)


def routed(
    tokens,
    norm_gain,
    expert_ids,
    route_weights,
    gate_weight,
    gate_bias,
    up_weight,
    up_bias,
    down_weight,
    down_bias,
    capacity,
):
    tok_rows, features = tokens.shape
    per_token = expert_ids.shape[1]
    experts = lax.axis_size("seq")
    quarter = features // lax.axis_size("rep")
    normed = rms_normed(tokens, norm_gain, -1)
    flat_ids = expert_ids.reshape(-1)
    onehot = (flat_ids[:, None] == jnp.arange(experts, dtype=jnp.int32)[None, :]).astype(jnp.int32)
    before = jnp.cumsum(onehot, axis=0) - onehot
    slot_index = jnp.sum(before * onehot, axis=1)
    destination = flat_ids * capacity + slot_index
    owner_row = jnp.arange(tok_rows * per_token, dtype=jnp.int32) // per_token
    buffer = jnp.zeros((experts * capacity, features), jnp.bfloat16)
    buffer = buffer.at[destination].set(normed[owner_row])
    received = lax.all_to_all(
        buffer.reshape(experts, capacity, features), "seq", split_axis=0, concat_axis=0, tiled=True
    )
    in_rows = received.reshape(-1, features)
    gate_pre = jnp.dot(in_rows, gate_weight[0], preferred_element_type=jnp.float32) + gate_bias[0]
    up_pre = jnp.dot(in_rows, up_weight[0], preferred_element_type=jnp.float32) + up_bias[0]
    partial_value = jnp.dot(
        gated(gate_pre, up_pre), down_weight[0], preferred_element_type=jnp.float32
    ).astype(jnp.bfloat16)
    summed = lax.psum_scatter(
        partial_value.reshape(experts, capacity, features),
        "rep",
        scatter_dimension=2,
        tiled=True,
    ).astype(jnp.float32)
    expert_out = (summed + down_bias[0][None, None, :]).astype(jnp.bfloat16)
    returned = lax.all_to_all(expert_out, "seq", split_axis=0, concat_axis=0, tiled=True)
    picked = returned.reshape(-1, quarter)[destination].reshape(tok_rows, per_token, quarter)
    mixed = jnp.sum(route_weights[:, :, None] * picked.astype(jnp.float32), axis=1)
    return mixed.astype(jnp.bfloat16)


tied = lax.optimization_barrier


def round_up(number, step):
    return -(-number // step) * step


def add_up(*terms):
    total = terms[0].astype(jnp.float32)
    for term in terms[1:]:
        total = total + term.astype(jnp.float32)
    return total.astype(jnp.bfloat16)


def padded(array, rows, columns):
    return jnp.pad(array, ((0, rows - array.shape[0]), (0, columns - array.shape[1])))


def column(row, size, lanes):
    return jnp.broadcast_to(padded(row, 1, size), (lanes, size)).T


def inward_kernel(groups, gate_ref, up_ref, biases_ref, weight_out, bias_out):
    features, hidden = gate_ref.shape
    quarter = features // groups
    hidden_pad, size = round_up(hidden, 128), round_up(quarter, 128)
    for n, weight in enumerate((gate_ref, up_ref)):
        values = weight[...].astype(jnp.float32)
        rows = slice(n * hidden_pad, (n + 1) * hidden_pad)
        for q in range(groups):
            part = padded(values[q * quarter : (q + 1) * quarter], size, hidden_pad)
            weight_out[rows, q * size : (q + 1) * size] = part.T.astype(jnp.bfloat16)
        bias_out[rows] = column(biases_ref[n : n + 1], hidden_pad, bias_out.shape[1])


def outward_kernel(groups, down_ref, biases_ref, weight_out, bias_out):
    hidden, features = down_ref.shape
    quarter = features // groups
    hidden_pad, size = round_up(hidden, 128), round_up(quarter, 128)
    values = padded(down_ref[...].astype(jnp.float32), hidden_pad, round_up(features, 128)).T
    for q in range(groups):
        part = padded(values[q * quarter : (q + 1) * quarter], size, hidden_pad)
        weight_out[q * size : (q + 1) * size] = part.astype(jnp.bfloat16)
    bias_out[...] = column(biases_ref[2:3], size, bias_out.shape[1])


def arrange(kernel, groups, lanes, arrays, shape, bias_rows):
    return pl.pallas_call(
        functools.partial(kernel, groups),
        out_shape=[
            jax.ShapeDtypeStruct(shape, jnp.bfloat16),
            jax.ShapeDtypeStruct((bias_rows, lanes), jnp.float32),
        ],
        compiler_params=pltpu.CompilerParams(vmem_limit_bytes=40 * 2**20),
        cost_estimate=pl.CostEstimate(
            flops=0, bytes_accessed=16 * arrays[0].size, transcendentals=0
        ),
    )(*arrays)


def fetch(sources, targets, sems):
    copies = [
        pltpu.make_async_copy(source, target, sems.at[n])
        for n, (source, target) in enumerate(zip(sources, targets))
    ]
    for copy in copies:
        copy.start()
    for copy in copies:
        copy.wait()


def pieces_kernel(groups, per, experts, *refs):
    sources, (one_ref, near_ref, far_ref) = refs[:4], refs[4:7]
    tokens_ref, gain_ref, ids_ref, weights_ref = refs[7:11]
    fetch(sources, refs[7:11], refs[11])
    features, lanes = tokens_ref.shape
    quarter = features // groups
    tail = one_ref.shape[0] - quarter
    rep = lax.axis_index("rep")
    values = tokens_ref[...].astype(jnp.float32)
    scale = lax.rsqrt(jnp.mean(values * values, axis=0, keepdims=True) + 1e-05)
    gain = jnp.broadcast_to(gain_ref[...].reshape(1, features), (lanes, features)).T
    normed = values * scale * gain
    row = lax.broadcasted_iota(jnp.int32, (tail, lanes), 0)
    chosen = lax.broadcasted_iota(jnp.int32, (round_up(experts, 8), lanes), 0)
    shares = jnp.zeros(chosen.shape, jnp.float32)
    for k in range(ids_ref.shape[0]):
        shares += jnp.where(ids_ref[k : k + 1] == chosen, weights_ref[k : k + 1], 0.0)
    terms = []
    for _ in range(3):
        term = shares.astype(jnp.bfloat16).astype(jnp.float32)
        terms.append(term)
        shares = shares - term
    for q in range(groups):
        rows = jnp.zeros((tail, lanes), jnp.float32)
        for n, term in enumerate(terms):
            for i in range(per):
                expert = q * per + i
                if expert < experts:
                    rows = jnp.where(row == n * per + i, term[expert : expert + 1], rows)
        piece = jnp.concatenate([normed[q * quarter : (q + 1) * quarter], rows], axis=0)
        piece = piece.astype(jnp.bfloat16)
        k = rep ^ q
        for side, target in enumerate((near_ref, far_ref)):

            @pl.when(k % 2 == side)
            def _(target=target, piece=piece, k=k):
                target[k // 2] = piece

        @pl.when(k == 0)
        def _(piece=piece):
            one_ref[...] = piece


def make_pieces(tokens, norm_gain, expert_ids, route_weights, groups, per, experts):
    features, lanes = tokens.shape
    rows = round_up(features // groups + 3 * per, 16)
    pair = jax.ShapeDtypeStruct((groups // 2, rows, lanes), jnp.bfloat16)
    arrays = (tokens, norm_gain, expert_ids, route_weights)
    return pl.pallas_call(
        functools.partial(pieces_kernel, groups, per, experts),
        in_specs=[pl.BlockSpec(memory_space=pltpu.HBM)] * 4,
        out_specs=[pl.BlockSpec(memory_space=pltpu.VMEM)] * 3,
        out_shape=[jax.ShapeDtypeStruct((rows, lanes), jnp.bfloat16), pair, pair],
        scratch_shapes=[pltpu.VMEM(a.shape, a.dtype) for a in arrays]
        + [pltpu.SemaphoreType.DMA((len(arrays),))],
        compiler_params=pltpu.CompilerParams(vmem_limit_bytes=60 * 2**20),
    )(*arrays)


def expert_kernel(quarter, per, blocks, slots, *refs):
    groups = len(blocks[0])
    counted = 1 + max(at for block in blocks for at, _ in block)
    arrays = refs[:counted]
    gate_up_ref, bias_ref, down_ref, down_bias_ref, keep_ref, send_ref = refs[counted : 6 + counted]
    scratch = refs[6 + counted :]
    _, piece_rows, lanes = arrays[0].shape
    size = gate_up_ref.shape[1] // groups
    hidden = gate_up_ref.shape[0] // 2
    rep, seq = lax.axis_index("rep"), lax.axis_index("seq")
    halves = len(scratch)
    count = len(blocks) // halves
    row = lax.broadcasted_iota(jnp.int32, (piece_rows - quarter, lanes), 0)
    for half in range(halves):
        rows_ref = scratch[half]
        if size > piece_rows:
            for k in range(groups):
                rows_ref[k * size + piece_rows : (k + 1) * size, :] = jnp.zeros(
                    (size - piece_rows, count * lanes), jnp.bfloat16
                )
        shares = [jnp.zeros((1, lanes), jnp.float32)] * count
        for k in range(groups):
            source = rep ^ k
            at_row = pl.ds(pl.multiple_of(source * size, size), piece_rows)
            mine = (lax.rem(row, per) == seq - source * per) & (row < 3 * per)
            for j in range(count):
                at, index = blocks[half * count + j][k]
                values = arrays[at][index]
                rows_ref[at_row, j * lanes : (j + 1) * lanes] = values
                terms = values.astype(jnp.float32)[quarter:]
                shares[j] += jnp.sum(jnp.where(mine, terms, 0.0), axis=0, keepdims=True)
        wide = jnp.concatenate(shares, axis=1)
        both = jnp.dot(gate_up_ref[...], rows_ref[...], preferred_element_type=jnp.float32)
        both = both + jnp.concatenate([bias_ref[...]] * count, axis=1)
        activated = gated(both[:hidden], both[hidden:])
        for k in range(groups):
            own_rows = down_ref[pl.ds(pl.multiple_of((rep ^ k) * size, size), size), :]
            rows = jnp.dot(own_rows, activated, preferred_element_type=jnp.float32)
            if k == 0:
                rows = rows + jnp.concatenate([down_bias_ref[...]] * count, axis=1)
            rows = (rows * wide).astype(jnp.bfloat16)
            target = send_ref if k % 2 else keep_ref
            for j in range(count):
                target[slots[half * count + j][k // 2]] = rows[:quarter, j * lanes : (j + 1) * lanes]


def run_expert(arrays, blocks, slots, weights, sizes, halves):
    quarter, per = sizes
    lanes = arrays[0].shape[2]
    gate_up, down = weights[0], weights[2]
    tokens = len(blocks) * lanes
    whole = pl.BlockSpec(memory_space=pltpu.VMEM)
    out = jax.ShapeDtypeStruct((2 * len(blocks), quarter, lanes), jnp.bfloat16)
    columns = tokens // halves
    return pl.pallas_call(
        functools.partial(expert_kernel, quarter, per, blocks, slots),
        in_specs=[whole] * (len(arrays) + len(weights)),
        out_specs=[whole, whole],
        out_shape=[out, out],
        scratch_shapes=[pltpu.VMEM((gate_up.shape[1], columns), jnp.bfloat16)] * halves,
        compiler_params=pltpu.CompilerParams(vmem_limit_bytes=40 * 2**20),
        cost_estimate=pl.CostEstimate(
            flops=4 * tokens * (gate_up.size + down.size),
            bytes_accessed=2 * (gate_up.size + down.size),
            transcendentals=0,
        ),
    )(*arrays, *weights)


def dense(
    tokens,
    norm_gain,
    expert_ids,
    route_weights,
    gate_weight,
    gate_bias,
    up_weight,
    up_bias,
    down_weight,
    down_bias,
):
    lanes, features = tokens.shape
    experts = lax.axis_size("seq")
    groups = lax.axis_size("rep")
    quarter = features // groups
    devices = experts * groups
    core, along_y, along_x, along_z = 1, 2, groups, 2 * groups

    def swap(array, step):
        return lax.ppermute(array, ("seq", "rep"), [(i, i ^ step) for i in range(devices)])

    per = -(-experts // groups)
    one, near, far = make_pieces(
        tokens.T, norm_gain, expert_ids.T, route_weights.T, groups, per, experts
    )
    z_2, z_3 = swap(one, 2 * along_z), swap(one, 3 * along_z)
    x_0 = swap(near, along_x)
    hidden_pad = round_up(gate_weight.shape[2], 128)
    wide = groups * round_up(quarter, 128)
    biases = jnp.concatenate([gate_bias, up_bias, down_bias], axis=0)
    inward = arrange(
        inward_kernel,
        groups,
        lanes,
        (gate_weight[0], up_weight[0], biases),
        (2 * hidden_pad, wide),
        2 * hidden_pad,
    )
    z_2, z_3, inward = tied((z_2, z_3, inward))
    z_high = jnp.stack([z_2, z_3])
    diagonal = along_x + along_y
    x_high, y_high = swap(z_high, along_x), swap(z_high, along_y)
    d_high = swap(z_high, diagonal)
    outward = arrange(
        outward_kernel,
        groups,
        lanes,
        (down_weight[0], biases),
        (wide, hidden_pad),
        wide // groups,
    )
    x_0, outward = tied((x_0, outward))
    weights = (*inward, *outward)

    def pairs(first, step):
        return [[(first + step * x + k % 2, k // 2) for k in range(groups)] for x in range(2)]

    slots = ((0, 1), (2, 3))
    sizes = (quarter, per)
    keep_0, send_0 = run_expert(
        (near, far, x_0, swap(x_0, core)), pairs(0, 2), slots, weights, sizes, 1
    )
    z_near = swap(jnp.concatenate([near, x_0], axis=0), along_z)
    z_core = swap(z_high, core)
    x_high, y_high, d_high, keep_0, z_core, z_near = tied(
        (x_high, y_high, d_high, keep_0, z_core, z_near)
    )
    high = (z_high, z_core, y_high, swap(y_high, core))
    high = high + (x_high, swap(x_high, core), d_high, swap(d_high, core))
    line = [[[(4 * x + k, n) for k in range(groups)] for x in range(2)] for n in range(2)]
    keep_2, send_2 = run_expert(high, line[0], slots, weights, sizes, 1)
    got_2 = swap(send_2, core)
    keep_2, high, z_near = tied((keep_2, high, z_near))
    near_1 = (z_near, swap(z_near, core))
    keep_3, send_3 = run_expert(high, line[1], slots, weights, sizes, 1)
    got_2, keep_3, send_3, near_1 = tied((got_2, keep_3, send_3, near_1))
    got_3 = swap(send_3, core)
    blocks = [[(k % 2, 2 * x + k // 2) for k in range(groups)] for x in range(2)]
    keep_1, send_1 = run_expert(near_1, blocks, slots, weights, sizes, 1)
    got_1 = swap(send_1, core)
    keep_1, got_3, send_0 = tied((keep_1, got_3, send_0))
    got_0 = swap(send_0, core)
    z_back = swap(add_up(keep_1, got_1), along_z)

    def spread(*terms):
        return [add_up(*[term[n] for term in terms]) for n in (2, 3, 1)]

    def gather(parts):
        return [swap(part, step) for part, step in zip(parts, (along_x, diagonal, along_y))]

    far_sums = [jnp.stack(pair) for pair in zip(spread(keep_2, got_2), spread(keep_3, got_3))]
    far_sums = gather(far_sums)
    line_2 = add_up(keep_2[0], got_2[0], *[part[0] for part in far_sums])
    line_3 = add_up(keep_3[0], got_3[0], *[part[1] for part in far_sums])
    back_2, back_3 = swap(line_2, 2 * along_z), swap(line_3, 3 * along_z)
    z_back, _, _ = tied((z_back, line_2, line_3))
    near_sums = gather(spread(keep_0, got_0, z_back))
    mixed = add_up(keep_0[0], got_0[0], z_back[0], *near_sums, back_2, back_3)
    return mixed.T


def on_device(*args):
    tokens, expert_ids = args[0], args[2]
    experts, groups = lax.axis_size("seq"), lax.axis_size("rep")
    capacity = 2 * tokens.shape[0] * expert_ids.shape[1] // experts
    if capacity >= tokens.shape[0] and experts == 2 * groups and groups == 4:
        return dense(*args)
    return routed(*args, capacity)


def solution(mesh):
    placed = (
        P("seq", None),
        P(),
        P("seq", None),
        P("seq", None),
        P("seq", None, "rep"),
        P("seq", "rep"),
        P("seq", None, "rep"),
        P("seq", "rep"),
        P("seq", "rep", None),
        P("seq", "rep"),
    )
    return jax.shard_map(
        on_device, mesh=mesh, in_specs=placed, out_specs=P("seq", "rep"), check_vma=False
    )
```

```python
import functools

import jax
import jax.numpy as jnp
from jax import lax
from jax.experimental import pallas as pl
from jax.experimental.pallas import tpu as pltpu
from jax.sharding import PartitionSpec as P


def rms_normed(values, norm_gain, axis):
    values = values.astype(jnp.float32)
    scale = lax.rsqrt(jnp.mean(values * values, axis=axis, keepdims=True) + 1e-05)
    return (values * scale * norm_gain).astype(jnp.bfloat16)


def gated(gate_pre, up_pre):
    return (gate_pre * jax.nn.sigmoid(1.702 * gate_pre) * (up_pre + 1.0)).astype(jnp.bfloat16)


def routed(
    tokens,
    norm_gain,
    expert_ids,
    route_weights,
    gate_weight,
    gate_bias,
    up_weight,
    up_bias,
    down_weight,
    down_bias,
    capacity,
):
    tok_rows, features = tokens.shape
    per_token = expert_ids.shape[1]
    experts = lax.axis_size("seq")
    quarter = features // lax.axis_size("rep")
    normed = rms_normed(tokens, norm_gain, -1)
    flat_ids = expert_ids.reshape(-1)
    onehot = (flat_ids[:, None] == jnp.arange(experts, dtype=jnp.int32)[None, :]).astype(jnp.int32)
    before = jnp.cumsum(onehot, axis=0) - onehot
    slot_index = jnp.sum(before * onehot, axis=1)
    destination = flat_ids * capacity + slot_index
    owner_row = jnp.arange(tok_rows * per_token, dtype=jnp.int32) // per_token
    buffer = jnp.zeros((experts * capacity, features), jnp.bfloat16)
    buffer = buffer.at[destination].set(normed[owner_row])
    received = lax.all_to_all(
        buffer.reshape(experts, capacity, features), "seq", split_axis=0, concat_axis=0, tiled=True
    )
    in_rows = received.reshape(-1, features)
    gate_pre = jnp.dot(in_rows, gate_weight[0], preferred_element_type=jnp.float32) + gate_bias[0]
    up_pre = jnp.dot(in_rows, up_weight[0], preferred_element_type=jnp.float32) + up_bias[0]
    partial_value = jnp.dot(
        gated(gate_pre, up_pre), down_weight[0], preferred_element_type=jnp.float32
    ).astype(jnp.bfloat16)
    summed = lax.psum_scatter(
        partial_value.reshape(experts, capacity, features),
        "rep",
        scatter_dimension=2,
        tiled=True,
    ).astype(jnp.float32)
    expert_out = (summed + down_bias[0][None, None, :]).astype(jnp.bfloat16)
    returned = lax.all_to_all(expert_out, "seq", split_axis=0, concat_axis=0, tiled=True)
    picked = returned.reshape(-1, quarter)[destination].reshape(tok_rows, per_token, quarter)
    mixed = jnp.sum(route_weights[:, :, None] * picked.astype(jnp.float32), axis=1)
    return mixed.astype(jnp.bfloat16)


tied = lax.optimization_barrier


def round_up(number, step):
    return -(-number // step) * step


def add_up(*terms):
    total = terms[0].astype(jnp.float32)
    for term in terms[1:]:
        total = total + term.astype(jnp.float32)
    return total.astype(jnp.bfloat16)


def padded(array, rows, columns):
    return jnp.pad(array, ((0, rows - array.shape[0]), (0, columns - array.shape[1])))


def column(row, size, lanes):
    return jnp.broadcast_to(padded(row, 1, size), (lanes, size)).T


def inward_kernel(groups, gate_ref, up_ref, biases_ref, weight_out, bias_out):
    features, hidden = gate_ref.shape
    quarter = features // groups
    hidden_pad, size = round_up(hidden, 128), round_up(quarter, 128)
    for n, weight in enumerate((gate_ref, up_ref)):
        values = weight[...].astype(jnp.float32)
        rows = slice(n * hidden_pad, (n + 1) * hidden_pad)
        for q in range(groups):
            part = padded(values[q * quarter : (q + 1) * quarter], size, hidden_pad)
            weight_out[rows, q * size : (q + 1) * size] = part.T.astype(jnp.bfloat16)
        bias_out[rows] = column(biases_ref[n : n + 1], hidden_pad, bias_out.shape[1])


def outward_kernel(groups, down_ref, biases_ref, weight_out, bias_out):
    hidden, features = down_ref.shape
    quarter = features // groups
    hidden_pad, size = round_up(hidden, 128), round_up(quarter, 128)
    values = padded(down_ref[...].astype(jnp.float32), hidden_pad, round_up(features, 128)).T
    for q in range(groups):
        part = padded(values[q * quarter : (q + 1) * quarter], size, hidden_pad)
        weight_out[q * size : (q + 1) * size] = part.astype(jnp.bfloat16)
    bias_out[...] = column(biases_ref[2:3], size, bias_out.shape[1])


def arrange(kernel, groups, lanes, arrays, shape, bias_rows):
    return pl.pallas_call(
        functools.partial(kernel, groups),
        out_shape=[
            jax.ShapeDtypeStruct(shape, jnp.bfloat16),
            jax.ShapeDtypeStruct((bias_rows, lanes), jnp.float32),
        ],
        compiler_params=pltpu.CompilerParams(vmem_limit_bytes=40 * 2**20),
        cost_estimate=pl.CostEstimate(
            flops=0, bytes_accessed=16 * arrays[0].size, transcendentals=0
        ),
    )(*arrays)


def fetch(sources, targets, sems):
    copies = [
        pltpu.make_async_copy(source, target, sems.at[n])
        for n, (source, target) in enumerate(zip(sources, targets))
    ]
    for copy in copies:
        copy.start()
    for copy in copies:
        copy.wait()


def pieces_kernel(groups, per, experts, *refs):
    sources, (one_ref, near_ref, far_ref) = refs[:4], refs[4:7]
    tokens_ref, gain_ref, ids_ref, weights_ref = refs[7:11]
    fetch(sources, refs[7:11], refs[11])
    features, lanes = tokens_ref.shape
    quarter = features // groups
    tail = one_ref.shape[0] - quarter
    rep = lax.axis_index("rep")
    values = tokens_ref[...].astype(jnp.float32)
    scale = lax.rsqrt(jnp.mean(values * values, axis=0, keepdims=True) + 1e-05)
    gain = jnp.broadcast_to(gain_ref[...].reshape(1, features), (lanes, features)).T
    normed = values * scale * gain
    row = lax.broadcasted_iota(jnp.int32, (tail, lanes), 0)
    chosen = lax.broadcasted_iota(jnp.int32, (round_up(experts, 8), lanes), 0)
    shares = jnp.zeros(chosen.shape, jnp.float32)
    for k in range(ids_ref.shape[0]):
        shares += jnp.where(ids_ref[k : k + 1] == chosen, weights_ref[k : k + 1], 0.0)
    terms = []
    for _ in range(3):
        term = shares.astype(jnp.bfloat16).astype(jnp.float32)
        terms.append(term)
        shares = shares - term
    for q in range(groups):
        rows = jnp.zeros((tail, lanes), jnp.float32)
        for n, term in enumerate(terms):
            for i in range(per):
                expert = q * per + i
                if expert < experts:
                    rows = jnp.where(row == n * per + i, term[expert : expert + 1], rows)
        piece = jnp.concatenate([normed[q * quarter : (q + 1) * quarter], rows], axis=0)
        piece = piece.astype(jnp.bfloat16)
        k = rep ^ q
        for side, target in enumerate((near_ref, far_ref)):

            @pl.when(k % 2 == side)
            def _(target=target, piece=piece, k=k):
                target[k // 2] = piece

        @pl.when(k == 0)
        def _(piece=piece):
            one_ref[...] = piece


def make_pieces(tokens, norm_gain, expert_ids, route_weights, groups, per, experts):
    features, lanes = tokens.shape
    rows = round_up(features // groups + 3 * per, 16)
    pair = jax.ShapeDtypeStruct((groups // 2, rows, lanes), jnp.bfloat16)
    arrays = (tokens, norm_gain, expert_ids, route_weights)
    return pl.pallas_call(
        functools.partial(pieces_kernel, groups, per, experts),
        in_specs=[pl.BlockSpec(memory_space=pltpu.HBM)] * 4,
        out_specs=[pl.BlockSpec(memory_space=pltpu.VMEM)] * 3,
        out_shape=[jax.ShapeDtypeStruct((rows, lanes), jnp.bfloat16), pair, pair],
        scratch_shapes=[pltpu.VMEM(a.shape, a.dtype) for a in arrays]
        + [pltpu.SemaphoreType.DMA((len(arrays),))],
        compiler_params=pltpu.CompilerParams(vmem_limit_bytes=60 * 2**20),
    )(*arrays)


def expert_kernel(quarter, per, blocks, slots, *refs):
    groups = len(blocks[0])
    counted = 1 + max(at for block in blocks for at, _ in block)
    arrays = refs[:counted]
    gate_up_ref, bias_ref, down_ref, down_bias_ref, keep_ref, send_ref = refs[counted : 6 + counted]
    scratch = refs[6 + counted :]
    _, piece_rows, lanes = arrays[0].shape
    size = gate_up_ref.shape[1] // groups
    hidden = gate_up_ref.shape[0] // 2
    rep, seq = lax.axis_index("rep"), lax.axis_index("seq")
    halves = len(scratch)
    count = len(blocks) // halves
    row = lax.broadcasted_iota(jnp.int32, (piece_rows - quarter, lanes), 0)
    for half in range(halves):
        rows_ref = scratch[half]
        if size > piece_rows:
            for k in range(groups):
                rows_ref[k * size + piece_rows : (k + 1) * size, :] = jnp.zeros(
                    (size - piece_rows, count * lanes), jnp.bfloat16
                )
        shares = [jnp.zeros((1, lanes), jnp.float32)] * count
        for k in range(groups):
            source = rep ^ k
            at_row = pl.ds(pl.multiple_of(source * size, size), piece_rows)
            mine = (lax.rem(row, per) == seq - source * per) & (row < 3 * per)
            for j in range(count):
                at, index = blocks[half * count + j][k]
                values = arrays[at][index]
                rows_ref[at_row, j * lanes : (j + 1) * lanes] = values
                terms = values.astype(jnp.float32)[quarter:]
                shares[j] += jnp.sum(jnp.where(mine, terms, 0.0), axis=0, keepdims=True)
        wide = jnp.concatenate(shares, axis=1)
        both = jnp.dot(gate_up_ref[...], rows_ref[...], preferred_element_type=jnp.float32)
        both = both + jnp.concatenate([bias_ref[...]] * count, axis=1)
        activated = gated(both[:hidden], both[hidden:])
        for k in range(groups):
            own_rows = down_ref[pl.ds(pl.multiple_of((rep ^ k) * size, size), size), :]
            rows = jnp.dot(own_rows, activated, preferred_element_type=jnp.float32)
            if k == 0:
                rows = rows + jnp.concatenate([down_bias_ref[...]] * count, axis=1)
            rows = (rows * wide).astype(jnp.bfloat16)
            target = send_ref if k % 2 else keep_ref
            for j in range(count):
                target[slots[half * count + j][k // 2]] = rows[:quarter, j * lanes : (j + 1) * lanes]


def run_expert(arrays, blocks, slots, weights, sizes, halves):
    quarter, per = sizes
    lanes = arrays[0].shape[2]
    gate_up, down = weights[0], weights[2]
    tokens = len(blocks) * lanes
    whole = pl.BlockSpec(memory_space=pltpu.VMEM)
    out = jax.ShapeDtypeStruct((2 * len(blocks), quarter, lanes), jnp.bfloat16)
    columns = tokens // halves
    return pl.pallas_call(
        functools.partial(expert_kernel, quarter, per, blocks, slots),
        in_specs=[whole] * (len(arrays) + len(weights)),
        out_specs=[whole, whole],
        out_shape=[out, out],
        scratch_shapes=[pltpu.VMEM((gate_up.shape[1], columns), jnp.bfloat16)] * halves,
        compiler_params=pltpu.CompilerParams(vmem_limit_bytes=40 * 2**20),
        cost_estimate=pl.CostEstimate(
            flops=4 * tokens * (gate_up.size + down.size),
            bytes_accessed=2 * (gate_up.size + down.size),
            transcendentals=0,
        ),
    )(*arrays, *weights)


def dense(
    tokens,
    norm_gain,
    expert_ids,
    route_weights,
    gate_weight,
    gate_bias,
    up_weight,
    up_bias,
    down_weight,
    down_bias,
):
    lanes, features = tokens.shape
    experts = lax.axis_size("seq")
    groups = lax.axis_size("rep")
    quarter = features // groups
    devices = experts * groups
    core, along_y, along_x, along_z = 1, 2, groups, 2 * groups

    def swap(array, step):
        return lax.ppermute(array, ("seq", "rep"), [(i, i ^ step) for i in range(devices)])

    per = -(-experts // groups)
    one, near, far = make_pieces(
        tokens.T, norm_gain, expert_ids.T, route_weights.T, groups, per, experts
    )
    z_2, z_3 = swap(one, 2 * along_z), swap(one, 3 * along_z)
    x_0 = swap(near, along_x)
    hidden_pad = round_up(gate_weight.shape[2], 128)
    wide = groups * round_up(quarter, 128)
    biases = jnp.concatenate([gate_bias, up_bias, down_bias], axis=0)
    inward = arrange(
        inward_kernel,
        groups,
        lanes,
        (gate_weight[0], up_weight[0], biases),
        (2 * hidden_pad, wide),
        2 * hidden_pad,
    )
    z_2, z_3, inward = tied((z_2, z_3, inward))
    z_high = jnp.stack([z_2, z_3])
    diagonal = along_x + along_y
    x_high, y_high = swap(z_high, along_x), swap(z_high, along_y)
    d_high = swap(z_high, diagonal)
    outward = arrange(
        outward_kernel,
        groups,
        lanes,
        (down_weight[0], biases),
        (wide, hidden_pad),
        wide // groups,
    )
    x_0, outward = tied((x_0, outward))
    weights = (*inward, *outward)

    def pairs(first, step):
        return [[(first + step * x + k % 2, k // 2) for k in range(groups)] for x in range(2)]

    slots = ((0, 1), (2, 3))
    sizes = (quarter, per)
    keep_0, send_0 = run_expert(
        (near, far, x_0, swap(x_0, core)), pairs(0, 2), slots, weights, sizes, 1
    )
    z_near = swap(jnp.concatenate([near, x_0], axis=0), along_z)
    z_core = swap(z_high, core)
    x_high, y_high, d_high, keep_0, z_core, z_near = tied(
        (x_high, y_high, d_high, keep_0, z_core, z_near)
    )
    near_1 = (z_near, swap(z_near, core))
    high = (z_high, z_core, y_high, swap(y_high, core))
    high = high + (x_high, swap(x_high, core), d_high, swap(d_high, core))
    blocks = [[(k % 2, 2 * x + k // 2) for k in range(groups)] for x in range(2)]
    keep_1, send_1 = run_expert(near_1, blocks, slots, weights, sizes, 1)
    high, keep_1, send_1 = tied((high, keep_1, send_1))
    got_1 = swap(send_1, core)
    line = [[[(4 * x + k, n) for k in range(groups)] for x in range(2)] for n in range(2)]
    keep_2, send_2 = run_expert(high, line[0], slots, weights, sizes, 1)
    got_2 = swap(send_2, core)
    keep_2, high = tied((keep_2, high))
    keep_3, send_3 = run_expert(high, line[1], slots, weights, sizes, 1)
    got_2, keep_3, send_3 = tied((got_2, keep_3, send_3))
    got_3 = swap(send_3, core)
    got_1, got_3, send_0 = tied((got_1, got_3, send_0))
    got_0 = swap(send_0, core)
    z_back = swap(add_up(keep_1, got_1), along_z)

    def spread(*terms):
        return [add_up(*[term[n] for term in terms]) for n in (2, 3, 1)]

    def gather(parts):
        return [swap(part, step) for part, step in zip(parts, (along_x, diagonal, along_y))]

    far_sums = [jnp.stack(pair) for pair in zip(spread(keep_2, got_2), spread(keep_3, got_3))]
    far_sums = gather(far_sums)
    line_2 = add_up(keep_2[0], got_2[0], *[part[0] for part in far_sums])
    line_3 = add_up(keep_3[0], got_3[0], *[part[1] for part in far_sums])
    back_2, back_3 = swap(line_2, 2 * along_z), swap(line_3, 3 * along_z)
    z_back, _, _ = tied((z_back, line_2, line_3))
    near_sums = gather(spread(keep_0, got_0, z_back))
    mixed = add_up(keep_0[0], got_0[0], z_back[0], *near_sums, back_2, back_3)
    return mixed.T


def on_device(*args):
    tokens, expert_ids = args[0], args[2]
    experts, groups = lax.axis_size("seq"), lax.axis_size("rep")
    capacity = 2 * tokens.shape[0] * expert_ids.shape[1] // experts
    if capacity >= tokens.shape[0] and experts == 2 * groups and groups == 4:
        return dense(*args)
    return routed(*args, capacity)


def solution(mesh):
    placed = (
        P("seq", None),
        P(),
        P("seq", None),
        P("seq", None),
        P("seq", None, "rep"),
        P("seq", "rep"),
        P("seq", None, "rep"),
        P("seq", "rep"),
        P("seq", "rep", None),
        P("seq", "rep"),
    )
    return jax.shard_map(
        on_device, mesh=mesh, in_specs=placed, out_specs=P("seq", "rep"), check_vma=False
    )
```

```python
import functools

import jax
import jax.numpy as jnp
from jax import lax
from jax.experimental import pallas as pl
from jax.experimental.pallas import tpu as pltpu
from jax.sharding import PartitionSpec as P


def rms_normed(values, norm_gain, axis):
    values = values.astype(jnp.float32)
    scale = lax.rsqrt(jnp.mean(values * values, axis=axis, keepdims=True) + 1e-05)
    return (values * scale * norm_gain).astype(jnp.bfloat16)


def gated(gate_pre, up_pre):
    return (gate_pre * jax.nn.sigmoid(1.702 * gate_pre) * (up_pre + 1.0)).astype(jnp.bfloat16)


def routed(
    tokens,
    norm_gain,
    expert_ids,
    route_weights,
    gate_weight,
    gate_bias,
    up_weight,
    up_bias,
    down_weight,
    down_bias,
    capacity,
):
    tok_rows, features = tokens.shape
    per_token = expert_ids.shape[1]
    experts = lax.axis_size("seq")
    quarter = features // lax.axis_size("rep")
    normed = rms_normed(tokens, norm_gain, -1)
    flat_ids = expert_ids.reshape(-1)
    onehot = (flat_ids[:, None] == jnp.arange(experts, dtype=jnp.int32)[None, :]).astype(jnp.int32)
    before = jnp.cumsum(onehot, axis=0) - onehot
    slot_index = jnp.sum(before * onehot, axis=1)
    destination = flat_ids * capacity + slot_index
    owner_row = jnp.arange(tok_rows * per_token, dtype=jnp.int32) // per_token
    buffer = jnp.zeros((experts * capacity, features), jnp.bfloat16)
    buffer = buffer.at[destination].set(normed[owner_row])
    received = lax.all_to_all(
        buffer.reshape(experts, capacity, features), "seq", split_axis=0, concat_axis=0, tiled=True
    )
    in_rows = received.reshape(-1, features)
    gate_pre = jnp.dot(in_rows, gate_weight[0], preferred_element_type=jnp.float32) + gate_bias[0]
    up_pre = jnp.dot(in_rows, up_weight[0], preferred_element_type=jnp.float32) + up_bias[0]
    partial_value = jnp.dot(
        gated(gate_pre, up_pre), down_weight[0], preferred_element_type=jnp.float32
    ).astype(jnp.bfloat16)
    summed = lax.psum_scatter(
        partial_value.reshape(experts, capacity, features),
        "rep",
        scatter_dimension=2,
        tiled=True,
    ).astype(jnp.float32)
    expert_out = (summed + down_bias[0][None, None, :]).astype(jnp.bfloat16)
    returned = lax.all_to_all(expert_out, "seq", split_axis=0, concat_axis=0, tiled=True)
    picked = returned.reshape(-1, quarter)[destination].reshape(tok_rows, per_token, quarter)
    mixed = jnp.sum(route_weights[:, :, None] * picked.astype(jnp.float32), axis=1)
    return mixed.astype(jnp.bfloat16)


tied = lax.optimization_barrier


def round_up(number, step):
    return -(-number // step) * step


def add_up(*terms):
    total = terms[0].astype(jnp.float32)
    for term in terms[1:]:
        total = total + term.astype(jnp.float32)
    return total.astype(jnp.bfloat16)


def padded(array, rows, columns):
    return jnp.pad(array, ((0, rows - array.shape[0]), (0, columns - array.shape[1])))


def column(row, size, lanes):
    return jnp.broadcast_to(padded(row, 1, size), (lanes, size)).T


def inward_kernel(groups, gate_ref, up_ref, biases_ref, weight_out, bias_out):
    features, hidden = gate_ref.shape
    quarter = features // groups
    hidden_pad, size = round_up(hidden, 128), round_up(quarter, 128)
    half = hidden_pad // 2
    for n, weight in enumerate((gate_ref, up_ref)):
        values = weight[...].astype(jnp.float32)
        added = column(biases_ref[n : n + 1], hidden_pad, bias_out.shape[1])
        halves = [
            (slice(h * half, (h + 1) * half), slice((2 * h + n) * half, (2 * h + n + 1) * half))
            for h in range(2)
        ]
        for q in range(groups):
            part = padded(values[q * quarter : (q + 1) * quarter], size, hidden_pad)
            part = part.T.astype(jnp.bfloat16)
            for own, rows in halves:
                weight_out[rows, q * size : (q + 1) * size] = part[own]
        for own, rows in halves:
            bias_out[rows] = added[own]


def outward_kernel(groups, down_ref, biases_ref, weight_out, bias_out):
    hidden, features = down_ref.shape
    quarter = features // groups
    hidden_pad, size = round_up(hidden, 128), round_up(quarter, 128)
    values = padded(down_ref[...].astype(jnp.float32), hidden_pad, round_up(features, 128)).T
    for q in range(groups):
        part = padded(values[q * quarter : (q + 1) * quarter], size, hidden_pad)
        weight_out[q * size : (q + 1) * size] = part.astype(jnp.bfloat16)
    bias_out[...] = column(biases_ref[2:3], size, bias_out.shape[1])


def arrange(kernel, groups, lanes, arrays, shape, bias_rows):
    return pl.pallas_call(
        functools.partial(kernel, groups),
        out_shape=[
            jax.ShapeDtypeStruct(shape, jnp.bfloat16),
            jax.ShapeDtypeStruct((bias_rows, lanes), jnp.float32),
        ],
        compiler_params=pltpu.CompilerParams(vmem_limit_bytes=40 * 2**20),
        cost_estimate=pl.CostEstimate(
            flops=0, bytes_accessed=16 * arrays[0].size, transcendentals=0
        ),
    )(*arrays)


def fetch(sources, targets, sems):
    copies = [
        pltpu.make_async_copy(source, target, sems.at[n])
        for n, (source, target) in enumerate(zip(sources, targets))
    ]
    for copy in copies:
        copy.start()
    for copy in copies:
        copy.wait()


def pieces_kernel(groups, per, experts, *refs):
    sources, (one_ref, near_ref, far_ref) = refs[:4], refs[4:7]
    tokens_ref, gain_ref, ids_ref, weights_ref = refs[7:11]
    fetch(sources, refs[7:11], refs[11])
    features, lanes = tokens_ref.shape
    quarter = features // groups
    tail = one_ref.shape[0] - quarter
    rep = lax.axis_index("rep")
    values = tokens_ref[...].astype(jnp.float32)
    scale = lax.rsqrt(jnp.mean(values * values, axis=0, keepdims=True) + 1e-05)
    gain = jnp.broadcast_to(gain_ref[...].reshape(1, features), (lanes, features)).T
    normed = values * scale * gain
    row = lax.broadcasted_iota(jnp.int32, (tail, lanes), 0)
    chosen = lax.broadcasted_iota(jnp.int32, (round_up(experts, 8), lanes), 0)
    shares = jnp.zeros(chosen.shape, jnp.float32)
    for k in range(ids_ref.shape[0]):
        shares += jnp.where(ids_ref[k : k + 1] == chosen, weights_ref[k : k + 1], 0.0)
    terms = []
    for _ in range(3):
        term = shares.astype(jnp.bfloat16).astype(jnp.float32)
        terms.append(term)
        shares = shares - term
    for q in range(groups):
        rows = jnp.zeros((tail, lanes), jnp.float32)
        for n, term in enumerate(terms):
            for i in range(per):
                expert = q * per + i
                if expert < experts:
                    rows = jnp.where(row == n * per + i, term[expert : expert + 1], rows)
        piece = jnp.concatenate([normed[q * quarter : (q + 1) * quarter], rows], axis=0)
        piece = piece.astype(jnp.bfloat16)
        k = rep ^ q
        for side, target in enumerate((near_ref, far_ref)):

            @pl.when(k % 2 == side)
            def _(target=target, piece=piece, k=k):
                target[k // 2] = piece

        @pl.when(k == 0)
        def _(piece=piece):
            one_ref[...] = piece


def make_pieces(tokens, norm_gain, expert_ids, route_weights, groups, per, experts):
    features, lanes = tokens.shape
    rows = round_up(features // groups + 3 * per, 16)
    pair = jax.ShapeDtypeStruct((groups // 2, rows, lanes), jnp.bfloat16)
    arrays = (tokens, norm_gain, expert_ids, route_weights)
    return pl.pallas_call(
        functools.partial(pieces_kernel, groups, per, experts),
        in_specs=[pl.BlockSpec(memory_space=pltpu.HBM)] * 4,
        out_specs=[pl.BlockSpec(memory_space=pltpu.VMEM)] * 3,
        out_shape=[jax.ShapeDtypeStruct((rows, lanes), jnp.bfloat16), pair, pair],
        scratch_shapes=[pltpu.VMEM(a.shape, a.dtype) for a in arrays]
        + [pltpu.SemaphoreType.DMA((len(arrays),))],
        compiler_params=pltpu.CompilerParams(vmem_limit_bytes=60 * 2**20),
    )(*arrays)


def expert_kernel(quarter, per, blocks, slots, *refs):
    groups = len(blocks[0])
    counted = 1 + max(at for block in blocks for at, _ in block)
    arrays = refs[:counted]
    gate_up_ref, bias_ref, down_ref, down_bias_ref, keep_ref, send_ref = refs[counted : 6 + counted]
    scratch = refs[6 + counted :]
    _, piece_rows, lanes = arrays[0].shape
    size = gate_up_ref.shape[1] // groups
    hidden = gate_up_ref.shape[0] // 2
    rep, seq = lax.axis_index("rep"), lax.axis_index("seq")
    halves = len(scratch)
    count = len(blocks) // halves
    row = lax.broadcasted_iota(jnp.int32, (piece_rows - quarter, lanes), 0)
    for half in range(halves):
        rows_ref = scratch[half]
        if size > piece_rows:
            for k in range(groups):
                rows_ref[k * size + piece_rows : (k + 1) * size, :] = jnp.zeros(
                    (size - piece_rows, count * lanes), jnp.bfloat16
                )
        shares = [jnp.zeros((1, lanes), jnp.float32)] * count
        for k in range(groups):
            source = rep ^ k
            at_row = pl.ds(pl.multiple_of(source * size, size), piece_rows)
            mine = (lax.rem(row, per) == seq - source * per) & (row < 3 * per)
            for j in range(count):
                at, index = blocks[half * count + j][k]
                values = arrays[at][index]
                rows_ref[at_row, j * lanes : (j + 1) * lanes] = values
                terms = values.astype(jnp.float32)[quarter:]
                shares[j] += jnp.sum(jnp.where(mine, terms, 0.0), axis=0, keepdims=True)
        wide = jnp.concatenate(shares, axis=1)
        activated = []
        for part in range(2):
            at = slice(part * hidden, (part + 1) * hidden)
            both = jnp.dot(gate_up_ref[at], rows_ref[...], preferred_element_type=jnp.float32)
            both = both + jnp.concatenate([bias_ref[at]] * count, axis=1)
            activated.append(gated(both[: hidden // 2], both[hidden // 2 :]))
        activated = jnp.concatenate(activated, axis=0)
        for k in range(groups):
            own_rows = down_ref[pl.ds(pl.multiple_of((rep ^ k) * size, size), size), :]
            rows = jnp.dot(own_rows, activated, preferred_element_type=jnp.float32)
            if k == 0:
                rows = rows + jnp.concatenate([down_bias_ref[...]] * count, axis=1)
            rows = (rows * wide).astype(jnp.bfloat16)
            target = send_ref if k % 2 else keep_ref
            for j in range(count):
                target[slots[half * count + j][k // 2]] = rows[:quarter, j * lanes : (j + 1) * lanes]


def run_expert(arrays, blocks, slots, weights, sizes, halves):
    quarter, per = sizes
    lanes = arrays[0].shape[2]
    gate_up, down = weights[0], weights[2]
    tokens = len(blocks) * lanes
    whole = pl.BlockSpec(memory_space=pltpu.VMEM)
    out = jax.ShapeDtypeStruct((2 * len(blocks), quarter, lanes), jnp.bfloat16)
    columns = tokens // halves
    return pl.pallas_call(
        functools.partial(expert_kernel, quarter, per, blocks, slots),
        in_specs=[whole] * (len(arrays) + len(weights)),
        out_specs=[whole, whole],
        out_shape=[out, out],
        scratch_shapes=[pltpu.VMEM((gate_up.shape[1], columns), jnp.bfloat16)] * halves,
        compiler_params=pltpu.CompilerParams(vmem_limit_bytes=40 * 2**20),
        cost_estimate=pl.CostEstimate(
            flops=4 * tokens * (gate_up.size + down.size),
            bytes_accessed=2 * (gate_up.size + down.size),
            transcendentals=0,
        ),
    )(*arrays, *weights)


def dense(
    tokens,
    norm_gain,
    expert_ids,
    route_weights,
    gate_weight,
    gate_bias,
    up_weight,
    up_bias,
    down_weight,
    down_bias,
):
    lanes, features = tokens.shape
    experts = lax.axis_size("seq")
    groups = lax.axis_size("rep")
    quarter = features // groups
    devices = experts * groups
    core, along_y, along_x, along_z = 1, 2, groups, 2 * groups

    def swap(array, step):
        return lax.ppermute(array, ("seq", "rep"), [(i, i ^ step) for i in range(devices)])

    per = -(-experts // groups)
    one, near, far = make_pieces(
        tokens.T, norm_gain, expert_ids.T, route_weights.T, groups, per, experts
    )
    z_2, z_3 = swap(one, 2 * along_z), swap(one, 3 * along_z)
    x_0 = swap(near, along_x)
    hidden_pad = round_up(gate_weight.shape[2], 128)
    wide = groups * round_up(quarter, 128)
    biases = jnp.concatenate([gate_bias, up_bias, down_bias], axis=0)
    inward = arrange(
        inward_kernel,
        groups,
        lanes,
        (gate_weight[0], up_weight[0], biases),
        (2 * hidden_pad, wide),
        2 * hidden_pad,
    )
    z_2, z_3, inward = tied((z_2, z_3, inward))
    z_high = jnp.stack([z_2, z_3])
    diagonal = along_x + along_y
    x_high, y_high = swap(z_high, along_x), swap(z_high, along_y)
    d_high = swap(z_high, diagonal)
    outward = arrange(
        outward_kernel,
        groups,
        lanes,
        (down_weight[0], biases),
        (wide, hidden_pad),
        wide // groups,
    )
    x_0, outward = tied((x_0, outward))
    weights = (*inward, *outward)

    def pairs(first, step):
        return [[(first + step * x + k % 2, k // 2) for k in range(groups)] for x in range(2)]

    slots = ((0, 1), (2, 3))
    sizes = (quarter, per)
    keep_0, send_0 = run_expert(
        (near, far, x_0, swap(x_0, core)), pairs(0, 2), slots, weights, sizes, 1
    )
    z_near = swap(jnp.concatenate([near, x_0], axis=0), along_z)
    z_high, x_high, y_high, d_high, keep_0, send_0, z_near = tied(
        (z_high, x_high, y_high, d_high, keep_0, send_0, z_near)
    )
    high = (z_high, swap(z_high, core), y_high, swap(y_high, core))
    high = high + (x_high, swap(x_high, core), d_high, swap(d_high, core))
    line = [[[(4 * x + k, n) for k in range(groups)] for x in range(2)] for n in range(2)]
    keep_2, send_2 = run_expert(high, line[0], slots, weights, sizes, 1)
    got_2 = swap(send_2, core)
    keep_2, high, z_near = tied((keep_2, high, z_near))
    near_1 = (z_near, swap(z_near, core))
    keep_3, send_3 = run_expert(high, line[1], slots, weights, sizes, 1)
    got_2, keep_3, send_3, near_1 = tied((got_2, keep_3, send_3, near_1))
    got_3 = swap(send_3, core)
    blocks = [[(k % 2, 2 * x + k // 2) for k in range(groups)] for x in range(2)]
    keep_1, send_1 = run_expert(near_1, blocks, slots, weights, sizes, 1)
    got_1 = swap(send_1, core)
    keep_1, got_3, send_0 = tied((keep_1, got_3, send_0))
    got_0 = swap(send_0, core)
    z_back = swap(add_up(keep_1, got_1), along_z)

    def spread(*terms):
        return [add_up(*[term[n] for term in terms]) for n in (2, 3, 1)]

    def gather(parts):
        return [swap(part, step) for part, step in zip(parts, (along_x, diagonal, along_y))]

    far_sums = [jnp.stack(pair) for pair in zip(spread(keep_2, got_2), spread(keep_3, got_3))]
    far_sums = gather(far_sums)
    line_2 = add_up(keep_2[0], got_2[0], *[part[0] for part in far_sums])
    line_3 = add_up(keep_3[0], got_3[0], *[part[1] for part in far_sums])
    back_2, back_3 = swap(line_2, 2 * along_z), swap(line_3, 3 * along_z)
    z_back, _, _ = tied((z_back, line_2, line_3))
    near_sums = gather(spread(keep_0, got_0, z_back))
    mixed = add_up(keep_0[0], got_0[0], z_back[0], *near_sums, back_2, back_3)
    return mixed.T


def on_device(*args):
    tokens, expert_ids = args[0], args[2]
    experts, groups = lax.axis_size("seq"), lax.axis_size("rep")
    capacity = 2 * tokens.shape[0] * expert_ids.shape[1] // experts
    if capacity >= tokens.shape[0] and experts == 2 * groups and groups == 4:
        return dense(*args)
    return routed(*args, capacity)


def solution(mesh):
    placed = (
        P("seq", None),
        P(),
        P("seq", None),
        P("seq", None),
        P("seq", None, "rep"),
        P("seq", "rep"),
        P("seq", None, "rep"),
        P("seq", "rep"),
        P("seq", "rep", None),
        P("seq", "rep"),
    )
    return jax.shard_map(
        on_device, mesh=mesh, in_specs=placed, out_specs=P("seq", "rep"), check_vma=False
    )
```

```python
import functools

import jax
import jax.numpy as jnp
from jax import lax
from jax.experimental import pallas as pl
from jax.experimental.pallas import tpu as pltpu
from jax.sharding import PartitionSpec as P


def rms_normed(values, norm_gain, axis):
    values = values.astype(jnp.float32)
    scale = lax.rsqrt(jnp.mean(values * values, axis=axis, keepdims=True) + 1e-05)
    return (values * scale * norm_gain).astype(jnp.bfloat16)


def gated(gate_pre, up_pre):
    return (gate_pre * jax.nn.sigmoid(1.702 * gate_pre) * (up_pre + 1.0)).astype(jnp.bfloat16)


def routed(
    tokens,
    norm_gain,
    expert_ids,
    route_weights,
    gate_weight,
    gate_bias,
    up_weight,
    up_bias,
    down_weight,
    down_bias,
    capacity,
):
    tok_rows, features = tokens.shape
    per_token = expert_ids.shape[1]
    experts = lax.axis_size("seq")
    quarter = features // lax.axis_size("rep")
    normed = rms_normed(tokens, norm_gain, -1)
    flat_ids = expert_ids.reshape(-1)
    onehot = (flat_ids[:, None] == jnp.arange(experts, dtype=jnp.int32)[None, :]).astype(jnp.int32)
    before = jnp.cumsum(onehot, axis=0) - onehot
    slot_index = jnp.sum(before * onehot, axis=1)
    destination = flat_ids * capacity + slot_index
    owner_row = jnp.arange(tok_rows * per_token, dtype=jnp.int32) // per_token
    buffer = jnp.zeros((experts * capacity, features), jnp.bfloat16)
    buffer = buffer.at[destination].set(normed[owner_row])
    received = lax.all_to_all(
        buffer.reshape(experts, capacity, features), "seq", split_axis=0, concat_axis=0, tiled=True
    )
    in_rows = received.reshape(-1, features)
    gate_pre = jnp.dot(in_rows, gate_weight[0], preferred_element_type=jnp.float32) + gate_bias[0]
    up_pre = jnp.dot(in_rows, up_weight[0], preferred_element_type=jnp.float32) + up_bias[0]
    partial_value = jnp.dot(
        gated(gate_pre, up_pre), down_weight[0], preferred_element_type=jnp.float32
    ).astype(jnp.bfloat16)
    summed = lax.psum_scatter(
        partial_value.reshape(experts, capacity, features),
        "rep",
        scatter_dimension=2,
        tiled=True,
    ).astype(jnp.float32)
    expert_out = (summed + down_bias[0][None, None, :]).astype(jnp.bfloat16)
    returned = lax.all_to_all(expert_out, "seq", split_axis=0, concat_axis=0, tiled=True)
    picked = returned.reshape(-1, quarter)[destination].reshape(tok_rows, per_token, quarter)
    mixed = jnp.sum(route_weights[:, :, None] * picked.astype(jnp.float32), axis=1)
    return mixed.astype(jnp.bfloat16)


tied = lax.optimization_barrier


def round_up(number, step):
    return -(-number // step) * step


def add_up(*terms):
    total = terms[0].astype(jnp.float32)
    for term in terms[1:]:
        total = total + term.astype(jnp.float32)
    return total.astype(jnp.bfloat16)


def padded(array, rows, columns):
    return jnp.pad(array, ((0, rows - array.shape[0]), (0, columns - array.shape[1])))


def column(row, size, lanes):
    return jnp.broadcast_to(padded(row, 1, size), (lanes, size)).T


def inward_kernel(groups, gate_ref, up_ref, biases_ref, weight_out, bias_out):
    features, hidden = gate_ref.shape
    quarter = features // groups
    hidden_pad, size = round_up(hidden, 128), round_up(quarter, 128)
    step = 128
    for n, weight in enumerate((gate_ref, up_ref)):
        values = weight[...].astype(jnp.float32)
        added = column(biases_ref[n : n + 1], hidden_pad, bias_out.shape[1])
        blocks = [
            (slice(b * step, (b + 1) * step), slice((2 * b + n) * step, (2 * b + n + 1) * step))
            for b in range(hidden_pad // step)
        ]
        for q in range(groups):
            part = padded(values[q * quarter : (q + 1) * quarter], size, hidden_pad)
            part = part.T.astype(jnp.bfloat16)
            for own, rows in blocks:
                weight_out[rows, q * size : (q + 1) * size] = part[own]
        for own, rows in blocks:
            bias_out[rows] = added[own]


def outward_kernel(groups, down_ref, biases_ref, weight_out, bias_out):
    hidden, features = down_ref.shape
    quarter = features // groups
    hidden_pad, size = round_up(hidden, 128), round_up(quarter, 128)
    values = padded(down_ref[...].astype(jnp.float32), hidden_pad, round_up(features, 128)).T
    for q in range(groups):
        part = padded(values[q * quarter : (q + 1) * quarter], size, hidden_pad)
        weight_out[q * size : (q + 1) * size] = part.astype(jnp.bfloat16)
    bias_out[...] = column(biases_ref[2:3], size, bias_out.shape[1])


def arrange(kernel, groups, lanes, arrays, shape, bias_rows):
    return pl.pallas_call(
        functools.partial(kernel, groups),
        out_shape=[
            jax.ShapeDtypeStruct(shape, jnp.bfloat16),
            jax.ShapeDtypeStruct((bias_rows, lanes), jnp.float32),
        ],
        compiler_params=pltpu.CompilerParams(vmem_limit_bytes=40 * 2**20),
        cost_estimate=pl.CostEstimate(
            flops=0, bytes_accessed=16 * arrays[0].size, transcendentals=0
        ),
    )(*arrays)


def fetch(sources, targets, sems):
    copies = [
        pltpu.make_async_copy(source, target, sems.at[n])
        for n, (source, target) in enumerate(zip(sources, targets))
    ]
    for copy in copies:
        copy.start()
    for copy in copies:
        copy.wait()


def pieces_kernel(groups, per, experts, *refs):
    sources, (one_ref, near_ref, far_ref) = refs[:4], refs[4:7]
    tokens_ref, gain_ref, ids_ref, weights_ref = refs[7:11]
    fetch(sources, refs[7:11], refs[11])
    features, lanes = tokens_ref.shape
    quarter = features // groups
    tail = one_ref.shape[0] - quarter
    rep = lax.axis_index("rep")
    values = tokens_ref[...].astype(jnp.float32)
    scale = lax.rsqrt(jnp.mean(values * values, axis=0, keepdims=True) + 1e-05)
    gain = jnp.broadcast_to(gain_ref[...].reshape(1, features), (lanes, features)).T
    normed = values * scale * gain
    row = lax.broadcasted_iota(jnp.int32, (tail, lanes), 0)
    chosen = lax.broadcasted_iota(jnp.int32, (round_up(experts, 8), lanes), 0)
    shares = jnp.zeros(chosen.shape, jnp.float32)
    for k in range(ids_ref.shape[0]):
        shares += jnp.where(ids_ref[k : k + 1] == chosen, weights_ref[k : k + 1], 0.0)
    terms = []
    for _ in range(3):
        term = shares.astype(jnp.bfloat16).astype(jnp.float32)
        terms.append(term)
        shares = shares - term
    for q in range(groups):
        rows = jnp.zeros((tail, lanes), jnp.float32)
        for n, term in enumerate(terms):
            for i in range(per):
                expert = q * per + i
                if expert < experts:
                    rows = jnp.where(row == n * per + i, term[expert : expert + 1], rows)
        piece = jnp.concatenate([normed[q * quarter : (q + 1) * quarter], rows], axis=0)
        piece = piece.astype(jnp.bfloat16)
        k = rep ^ q
        for side, target in enumerate((near_ref, far_ref)):

            @pl.when(k % 2 == side)
            def _(target=target, piece=piece, k=k):
                target[k // 2] = piece

        @pl.when(k == 0)
        def _(piece=piece):
            one_ref[...] = piece


def make_pieces(tokens, norm_gain, expert_ids, route_weights, groups, per, experts):
    features, lanes = tokens.shape
    rows = round_up(features // groups + 3 * per, 16)
    pair = jax.ShapeDtypeStruct((groups // 2, rows, lanes), jnp.bfloat16)
    arrays = (tokens, norm_gain, expert_ids, route_weights)
    return pl.pallas_call(
        functools.partial(pieces_kernel, groups, per, experts),
        in_specs=[pl.BlockSpec(memory_space=pltpu.HBM)] * 4,
        out_specs=[pl.BlockSpec(memory_space=pltpu.VMEM)] * 3,
        out_shape=[jax.ShapeDtypeStruct((rows, lanes), jnp.bfloat16), pair, pair],
        scratch_shapes=[pltpu.VMEM(a.shape, a.dtype) for a in arrays]
        + [pltpu.SemaphoreType.DMA((len(arrays),))],
        compiler_params=pltpu.CompilerParams(vmem_limit_bytes=60 * 2**20),
    )(*arrays)


def expert_kernel(quarter, per, blocks, slots, *refs):
    groups = len(blocks[0])
    counted = 1 + max(at for block in blocks for at, _ in block)
    arrays = refs[:counted]
    gate_up_ref, bias_ref, down_ref, down_bias_ref, keep_ref, send_ref = refs[counted : 6 + counted]
    scratch = refs[6 + counted :]
    _, piece_rows, lanes = arrays[0].shape
    size = gate_up_ref.shape[1] // groups
    hidden = gate_up_ref.shape[0] // 2
    rep, seq = lax.axis_index("rep"), lax.axis_index("seq")
    halves = len(scratch)
    count = len(blocks) // halves
    row = lax.broadcasted_iota(jnp.int32, (piece_rows - quarter, lanes), 0)
    for half in range(halves):
        rows_ref = scratch[half]
        if size > piece_rows:
            for k in range(groups):
                rows_ref[k * size + piece_rows : (k + 1) * size, :] = jnp.zeros(
                    (size - piece_rows, count * lanes), jnp.bfloat16
                )
        shares = [jnp.zeros((1, lanes), jnp.float32)] * count
        for k in range(groups):
            source = rep ^ k
            at_row = pl.ds(pl.multiple_of(source * size, size), piece_rows)
            mine = (lax.rem(row, per) == seq - source * per) & (row < 3 * per)
            for j in range(count):
                at, index = blocks[half * count + j][k]
                values = arrays[at][index]
                rows_ref[at_row, j * lanes : (j + 1) * lanes] = values
                terms = values.astype(jnp.float32)[quarter:]
                shares[j] += jnp.sum(jnp.where(mine, terms, 0.0), axis=0, keepdims=True)
        wide = jnp.concatenate(shares, axis=1)
        activated = []
        for part in range(hidden // 128):
            at = slice(part * 256, (part + 1) * 256)
            both = jnp.dot(gate_up_ref[at], rows_ref[...], preferred_element_type=jnp.float32)
            both = both + jnp.concatenate([bias_ref[at]] * count, axis=1)
            activated.append(gated(both[:128], both[128:]))
        activated = jnp.concatenate(activated, axis=0)
        for k in range(groups):
            own_rows = down_ref[pl.ds(pl.multiple_of((rep ^ k) * size, size), size), :]
            rows = jnp.dot(own_rows, activated, preferred_element_type=jnp.float32)
            if k == 0:
                rows = rows + jnp.concatenate([down_bias_ref[...]] * count, axis=1)
            rows = (rows * wide).astype(jnp.bfloat16)
            target = send_ref if k % 2 else keep_ref
            for j in range(count):
                target[slots[half * count + j][k // 2]] = rows[:quarter, j * lanes : (j + 1) * lanes]


def run_expert(arrays, blocks, slots, weights, sizes, halves):
    quarter, per = sizes
    lanes = arrays[0].shape[2]
    gate_up, down = weights[0], weights[2]
    tokens = len(blocks) * lanes
    whole = pl.BlockSpec(memory_space=pltpu.VMEM)
    out = jax.ShapeDtypeStruct((2 * len(blocks), quarter, lanes), jnp.bfloat16)
    columns = tokens // halves
    return pl.pallas_call(
        functools.partial(expert_kernel, quarter, per, blocks, slots),
        in_specs=[whole] * (len(arrays) + len(weights)),
        out_specs=[whole, whole],
        out_shape=[out, out],
        scratch_shapes=[pltpu.VMEM((gate_up.shape[1], columns), jnp.bfloat16)] * halves,
        compiler_params=pltpu.CompilerParams(vmem_limit_bytes=40 * 2**20),
        cost_estimate=pl.CostEstimate(
            flops=4 * tokens * (gate_up.size + down.size),
            bytes_accessed=2 * (gate_up.size + down.size),
            transcendentals=0,
        ),
    )(*arrays, *weights)


def dense(
    tokens,
    norm_gain,
    expert_ids,
    route_weights,
    gate_weight,
    gate_bias,
    up_weight,
    up_bias,
    down_weight,
    down_bias,
):
    lanes, features = tokens.shape
    experts = lax.axis_size("seq")
    groups = lax.axis_size("rep")
    quarter = features // groups
    devices = experts * groups
    core, along_y, along_x, along_z = 1, 2, groups, 2 * groups

    def swap(array, step):
        return lax.ppermute(array, ("seq", "rep"), [(i, i ^ step) for i in range(devices)])

    per = -(-experts // groups)
    one, near, far = make_pieces(
        tokens.T, norm_gain, expert_ids.T, route_weights.T, groups, per, experts
    )
    z_2, z_3 = swap(one, 2 * along_z), swap(one, 3 * along_z)
    x_0 = swap(near, along_x)
    hidden_pad = round_up(gate_weight.shape[2], 128)
    wide = groups * round_up(quarter, 128)
    biases = jnp.concatenate([gate_bias, up_bias, down_bias], axis=0)
    inward = arrange(
        inward_kernel,
        groups,
        lanes,
        (gate_weight[0], up_weight[0], biases),
        (2 * hidden_pad, wide),
        2 * hidden_pad,
    )
    z_2, z_3, inward = tied((z_2, z_3, inward))
    z_high = jnp.stack([z_2, z_3])
    diagonal = along_x + along_y
    x_high, y_high = swap(z_high, along_x), swap(z_high, along_y)
    d_high = swap(z_high, diagonal)
    outward = arrange(
        outward_kernel,
        groups,
        lanes,
        (down_weight[0], biases),
        (wide, hidden_pad),
        wide // groups,
    )
    x_0, outward = tied((x_0, outward))
    weights = (*inward, *outward)

    def pairs(first, step):
        return [[(first + step * x + k % 2, k // 2) for k in range(groups)] for x in range(2)]

    slots = ((0, 1), (2, 3))
    sizes = (quarter, per)
    keep_0, send_0 = run_expert(
        (near, far, x_0, swap(x_0, core)), pairs(0, 2), slots, weights, sizes, 1
    )
    z_near = swap(jnp.concatenate([near, x_0], axis=0), along_z)
    z_high, x_high, y_high, d_high, keep_0, send_0, z_near = tied(
        (z_high, x_high, y_high, d_high, keep_0, send_0, z_near)
    )
    high = (z_high, swap(z_high, core), y_high, swap(y_high, core))
    high = high + (x_high, swap(x_high, core), d_high, swap(d_high, core))
    line = [[[(4 * x + k, n) for k in range(groups)] for x in range(2)] for n in range(2)]
    keep_2, send_2 = run_expert(high, line[0], slots, weights, sizes, 1)
    got_2 = swap(send_2, core)
    keep_2, high, z_near = tied((keep_2, high, z_near))
    near_1 = (z_near, swap(z_near, core))
    keep_3, send_3 = run_expert(high, line[1], slots, weights, sizes, 1)
    got_2, keep_3, send_3, near_1 = tied((got_2, keep_3, send_3, near_1))
    got_3 = swap(send_3, core)
    blocks = [[(k % 2, 2 * x + k // 2) for k in range(groups)] for x in range(2)]
    keep_1, send_1 = run_expert(near_1, blocks, slots, weights, sizes, 1)
    got_1 = swap(send_1, core)
    keep_1, got_3, send_0 = tied((keep_1, got_3, send_0))
    got_0 = swap(send_0, core)
    z_back = swap(add_up(keep_1, got_1), along_z)

    def spread(*terms):
        return [add_up(*[term[n] for term in terms]) for n in (2, 3, 1)]

    def gather(parts):
        return [swap(part, step) for part, step in zip(parts, (along_x, diagonal, along_y))]

    far_sums = [jnp.stack(pair) for pair in zip(spread(keep_2, got_2), spread(keep_3, got_3))]
    far_sums = gather(far_sums)
    line_2 = add_up(keep_2[0], got_2[0], *[part[0] for part in far_sums])
    line_3 = add_up(keep_3[0], got_3[0], *[part[1] for part in far_sums])
    back_2, back_3 = swap(line_2, 2 * along_z), swap(line_3, 3 * along_z)
    z_back, _, _ = tied((z_back, line_2, line_3))
    near_sums = gather(spread(keep_0, got_0, z_back))
    mixed = add_up(keep_0[0], got_0[0], z_back[0], *near_sums, back_2, back_3)
    return mixed.T


def on_device(*args):
    tokens, expert_ids = args[0], args[2]
    experts, groups = lax.axis_size("seq"), lax.axis_size("rep")
    capacity = 2 * tokens.shape[0] * expert_ids.shape[1] // experts
    if capacity >= tokens.shape[0] and experts == 2 * groups and groups == 4:
        return dense(*args)
    return routed(*args, capacity)


def solution(mesh):
    placed = (
        P("seq", None),
        P(),
        P("seq", None),
        P("seq", None),
        P("seq", None, "rep"),
        P("seq", "rep"),
        P("seq", None, "rep"),
        P("seq", "rep"),
        P("seq", "rep", None),
        P("seq", "rep"),
    )
    return jax.shard_map(
        on_device, mesh=mesh, in_specs=placed, out_specs=P("seq", "rep"), check_vma=False
    )
```

```python
import functools

import jax
import jax.numpy as jnp
from jax import lax
from jax.experimental import pallas as pl
from jax.experimental.pallas import tpu as pltpu
from jax.sharding import PartitionSpec as P


def rms_normed(values, norm_gain, axis):
    values = values.astype(jnp.float32)
    scale = lax.rsqrt(jnp.mean(values * values, axis=axis, keepdims=True) + 1e-05)
    return (values * scale * norm_gain).astype(jnp.bfloat16)


def gated(gate_pre, up_pre):
    return (gate_pre * jax.nn.sigmoid(1.702 * gate_pre) * (up_pre + 1.0)).astype(jnp.bfloat16)


def routed(
    tokens,
    norm_gain,
    expert_ids,
    route_weights,
    gate_weight,
    gate_bias,
    up_weight,
    up_bias,
    down_weight,
    down_bias,
    capacity,
):
    tok_rows, features = tokens.shape
    per_token = expert_ids.shape[1]
    experts = lax.axis_size("seq")
    quarter = features // lax.axis_size("rep")
    normed = rms_normed(tokens, norm_gain, -1)
    flat_ids = expert_ids.reshape(-1)
    onehot = (flat_ids[:, None] == jnp.arange(experts, dtype=jnp.int32)[None, :]).astype(jnp.int32)
    before = jnp.cumsum(onehot, axis=0) - onehot
    slot_index = jnp.sum(before * onehot, axis=1)
    destination = flat_ids * capacity + slot_index
    owner_row = jnp.arange(tok_rows * per_token, dtype=jnp.int32) // per_token
    buffer = jnp.zeros((experts * capacity, features), jnp.bfloat16)
    buffer = buffer.at[destination].set(normed[owner_row])
    received = lax.all_to_all(
        buffer.reshape(experts, capacity, features), "seq", split_axis=0, concat_axis=0, tiled=True
    )
    in_rows = received.reshape(-1, features)
    gate_pre = jnp.dot(in_rows, gate_weight[0], preferred_element_type=jnp.float32) + gate_bias[0]
    up_pre = jnp.dot(in_rows, up_weight[0], preferred_element_type=jnp.float32) + up_bias[0]
    partial_value = jnp.dot(
        gated(gate_pre, up_pre), down_weight[0], preferred_element_type=jnp.float32
    ).astype(jnp.bfloat16)
    summed = lax.psum_scatter(
        partial_value.reshape(experts, capacity, features),
        "rep",
        scatter_dimension=2,
        tiled=True,
    ).astype(jnp.float32)
    expert_out = (summed + down_bias[0][None, None, :]).astype(jnp.bfloat16)
    returned = lax.all_to_all(expert_out, "seq", split_axis=0, concat_axis=0, tiled=True)
    picked = returned.reshape(-1, quarter)[destination].reshape(tok_rows, per_token, quarter)
    mixed = jnp.sum(route_weights[:, :, None] * picked.astype(jnp.float32), axis=1)
    return mixed.astype(jnp.bfloat16)


tied = lax.optimization_barrier


def round_up(number, step):
    return -(-number // step) * step


def add_up(*terms):
    total = terms[0].astype(jnp.float32)
    for term in terms[1:]:
        total = total + term.astype(jnp.float32)
    return total.astype(jnp.bfloat16)


def padded(array, rows, columns):
    return jnp.pad(array, ((0, rows - array.shape[0]), (0, columns - array.shape[1])))


def column(row, size, lanes):
    return jnp.broadcast_to(padded(row, 1, size), (lanes, size)).T


def inward_kernel(groups, gate_ref, up_ref, biases_ref, weight_out, bias_out):
    features, hidden = gate_ref.shape
    quarter = features // groups
    hidden_pad, size = round_up(hidden, 128), round_up(quarter, 128)
    half = hidden_pad // 2
    for n, weight in enumerate((gate_ref, up_ref)):
        values = weight[...].astype(jnp.float32)
        added = column(biases_ref[n : n + 1], hidden_pad, bias_out.shape[1])
        halves = [
            (slice(h * half, (h + 1) * half), slice((2 * h + n) * half, (2 * h + n + 1) * half))
            for h in range(2)
        ]
        for q in range(groups):
            part = padded(values[q * quarter : (q + 1) * quarter], size, hidden_pad)
            part = part.T.astype(jnp.bfloat16)
            for own, rows in halves:
                weight_out[rows, q * size : (q + 1) * size] = part[own]
        for own, rows in halves:
            bias_out[rows] = added[own]


def outward_kernel(groups, down_ref, biases_ref, weight_out, bias_out):
    hidden, features = down_ref.shape
    quarter = features // groups
    hidden_pad, size = round_up(hidden, 128), round_up(quarter, 128)
    values = padded(down_ref[...].astype(jnp.float32), hidden_pad, round_up(features, 128)).T
    for q in range(groups):
        part = padded(values[q * quarter : (q + 1) * quarter], size, hidden_pad)
        weight_out[q * size : (q + 1) * size] = part.astype(jnp.bfloat16)
    bias_out[...] = column(biases_ref[2:3], size, bias_out.shape[1])


def arrange(kernel, groups, lanes, arrays, shape, bias_rows):
    return pl.pallas_call(
        functools.partial(kernel, groups),
        out_shape=[
            jax.ShapeDtypeStruct(shape, jnp.bfloat16),
            jax.ShapeDtypeStruct((bias_rows, lanes), jnp.float32),
        ],
        compiler_params=pltpu.CompilerParams(vmem_limit_bytes=40 * 2**20),
        cost_estimate=pl.CostEstimate(
            flops=0, bytes_accessed=16 * arrays[0].size, transcendentals=0
        ),
    )(*arrays)


def pieces_kernel(groups, per, experts, *refs):
    sources, (one_ref, near_ref, far_ref), targets = refs[:4], refs[4:7], refs[7:11]
    tokens_ref, gain_ref, ids_ref, weights_ref = targets
    copies = [
        pltpu.make_async_copy(source, target, refs[11].at[n])
        for n, (source, target) in enumerate(zip(sources, targets))
    ]
    for copy in copies:
        copy.start()
    for copy in copies[1:]:
        copy.wait()
    features, lanes = tokens_ref.shape
    quarter = features // groups
    tail = one_ref.shape[0] - quarter
    rep = lax.axis_index("rep")
    gain = jnp.broadcast_to(gain_ref[...].reshape(1, features), (lanes, features)).T
    row = lax.broadcasted_iota(jnp.int32, (tail, lanes), 0)
    chosen = lax.broadcasted_iota(jnp.int32, (round_up(experts, 8), lanes), 0)
    shares = jnp.zeros(chosen.shape, jnp.float32)
    for k in range(ids_ref.shape[0]):
        shares += jnp.where(ids_ref[k : k + 1] == chosen, weights_ref[k : k + 1], 0.0)
    terms = []
    for _ in range(3):
        term = shares.astype(jnp.bfloat16).astype(jnp.float32)
        terms.append(term)
        shares = shares - term
    tails = []
    for q in range(groups):
        rows = jnp.zeros((tail, lanes), jnp.float32)
        for n, term in enumerate(terms):
            for i in range(per):
                expert = q * per + i
                if expert < experts:
                    rows = jnp.where(row == n * per + i, term[expert : expert + 1], rows)
        tails.append(rows)
    copies[0].wait()
    values = tokens_ref[...].astype(jnp.float32)
    scale = lax.rsqrt(jnp.mean(values * values, axis=0, keepdims=True) + 1e-05)
    normed = values * scale * gain
    for q in range(groups):
        piece = jnp.concatenate([normed[q * quarter : (q + 1) * quarter], tails[q]], axis=0)
        piece = piece.astype(jnp.bfloat16)
        k = rep ^ q
        for side, target in enumerate((near_ref, far_ref)):

            @pl.when(k % 2 == side)
            def _(target=target, piece=piece, k=k):
                target[k // 2] = piece

        @pl.when(k == 0)
        def _(piece=piece):
            one_ref[...] = piece


def make_pieces(tokens, norm_gain, expert_ids, route_weights, groups, per, experts):
    features, lanes = tokens.shape
    rows = round_up(features // groups + 3 * per, 16)
    pair = jax.ShapeDtypeStruct((groups // 2, rows, lanes), jnp.bfloat16)
    arrays = (tokens, norm_gain, expert_ids, route_weights)
    return pl.pallas_call(
        functools.partial(pieces_kernel, groups, per, experts),
        in_specs=[pl.BlockSpec(memory_space=pltpu.HBM)] * 4,
        out_specs=[pl.BlockSpec(memory_space=pltpu.VMEM)] * 3,
        out_shape=[jax.ShapeDtypeStruct((rows, lanes), jnp.bfloat16), pair, pair],
        scratch_shapes=[pltpu.VMEM(a.shape, a.dtype) for a in arrays]
        + [pltpu.SemaphoreType.DMA((len(arrays),))],
        compiler_params=pltpu.CompilerParams(vmem_limit_bytes=60 * 2**20),
    )(*arrays)


def expert_kernel(quarter, per, blocks, slots, *refs):
    groups = len(blocks[0])
    counted = 1 + max(at for block in blocks for at, _ in block)
    arrays = refs[:counted]
    gate_up_ref, bias_ref, down_ref, down_bias_ref, keep_ref, send_ref = refs[counted : 6 + counted]
    scratch = refs[6 + counted :]
    _, piece_rows, lanes = arrays[0].shape
    size = gate_up_ref.shape[1] // groups
    hidden = gate_up_ref.shape[0] // 2
    rep, seq = lax.axis_index("rep"), lax.axis_index("seq")
    halves = len(scratch)
    count = len(blocks) // halves
    row = lax.broadcasted_iota(jnp.int32, (piece_rows - quarter, lanes), 0)
    for half in range(halves):
        rows_ref = scratch[half]
        if size > piece_rows:
            for k in range(groups):
                rows_ref[k * size + piece_rows : (k + 1) * size, :] = jnp.zeros(
                    (size - piece_rows, count * lanes), jnp.bfloat16
                )
        shares = [jnp.zeros((1, lanes), jnp.float32)] * count
        for k in range(groups):
            source = rep ^ k
            at_row = pl.ds(pl.multiple_of(source * size, size), piece_rows)
            mine = (lax.rem(row, per) == seq - source * per) & (row < 3 * per)
            for j in range(count):
                at, index = blocks[half * count + j][k]
                values = arrays[at][index]
                rows_ref[at_row, j * lanes : (j + 1) * lanes] = values
                terms = values.astype(jnp.float32)[quarter:]
                shares[j] += jnp.sum(jnp.where(mine, terms, 0.0), axis=0, keepdims=True)
        wide = jnp.concatenate(shares, axis=1)
        activated = []
        for part in range(2):
            at = slice(part * hidden, (part + 1) * hidden)
            both = jnp.dot(gate_up_ref[at], rows_ref[...], preferred_element_type=jnp.float32)
            both = both + jnp.concatenate([bias_ref[at]] * count, axis=1)
            activated.append(gated(both[: hidden // 2], both[hidden // 2 :]))
        activated = jnp.concatenate(activated, axis=0)
        for k in range(groups):
            own_rows = down_ref[pl.ds(pl.multiple_of((rep ^ k) * size, size), size), :]
            rows = jnp.dot(own_rows, activated, preferred_element_type=jnp.float32)
            if k == 0:
                rows = rows + jnp.concatenate([down_bias_ref[...]] * count, axis=1)
            rows = (rows * wide).astype(jnp.bfloat16)
            target = send_ref if k % 2 else keep_ref
            for j in range(count):
                target[slots[half * count + j][k // 2]] = rows[:quarter, j * lanes : (j + 1) * lanes]


def run_expert(arrays, blocks, slots, weights, sizes, halves):
    quarter, per = sizes
    lanes = arrays[0].shape[2]
    gate_up, down = weights[0], weights[2]
    tokens = len(blocks) * lanes
    whole = pl.BlockSpec(memory_space=pltpu.VMEM)
    out = jax.ShapeDtypeStruct((2 * len(blocks), quarter, lanes), jnp.bfloat16)
    columns = tokens // halves
    return pl.pallas_call(
        functools.partial(expert_kernel, quarter, per, blocks, slots),
        in_specs=[whole] * (len(arrays) + len(weights)),
        out_specs=[whole, whole],
        out_shape=[out, out],
        scratch_shapes=[pltpu.VMEM((gate_up.shape[1], columns), jnp.bfloat16)] * halves,
        compiler_params=pltpu.CompilerParams(vmem_limit_bytes=40 * 2**20),
        cost_estimate=pl.CostEstimate(
            flops=4 * tokens * (gate_up.size + down.size),
            bytes_accessed=2 * (gate_up.size + down.size),
            transcendentals=0,
        ),
    )(*arrays, *weights)


def dense(
    tokens,
    norm_gain,
    expert_ids,
    route_weights,
    gate_weight,
    gate_bias,
    up_weight,
    up_bias,
    down_weight,
    down_bias,
):
    lanes, features = tokens.shape
    experts = lax.axis_size("seq")
    groups = lax.axis_size("rep")
    quarter = features // groups
    devices = experts * groups
    core, along_y, along_x, along_z = 1, 2, groups, 2 * groups

    def swap(array, step):
        return lax.ppermute(array, ("seq", "rep"), [(i, i ^ step) for i in range(devices)])

    per = -(-experts // groups)
    one, near, far = make_pieces(
        tokens.T, norm_gain, expert_ids.T, route_weights.T, groups, per, experts
    )
    z_2, z_3 = swap(one, 2 * along_z), swap(one, 3 * along_z)
    x_0 = swap(near, along_x)
    hidden_pad = round_up(gate_weight.shape[2], 128)
    wide = groups * round_up(quarter, 128)
    biases = jnp.concatenate([gate_bias, up_bias, down_bias], axis=0)
    inward = arrange(
        inward_kernel,
        groups,
        lanes,
        (gate_weight[0], up_weight[0], biases),
        (2 * hidden_pad, wide),
        2 * hidden_pad,
    )
    z_2, z_3, inward = tied((z_2, z_3, inward))
    z_high = jnp.stack([z_2, z_3])
    diagonal = along_x + along_y
    x_high, y_high = swap(z_high, along_x), swap(z_high, along_y)
    d_high = swap(z_high, diagonal)
    outward = arrange(
        outward_kernel,
        groups,
        lanes,
        (down_weight[0], biases),
        (wide, hidden_pad),
        wide // groups,
    )
    x_0, outward = tied((x_0, outward))
    weights = (*inward, *outward)

    def pairs(first, step):
        return [[(first + step * x + k % 2, k // 2) for k in range(groups)] for x in range(2)]

    slots = ((0, 1), (2, 3))
    sizes = (quarter, per)
    keep_0, send_0 = run_expert(
        (near, far, x_0, swap(x_0, core)), pairs(0, 2), slots, weights, sizes, 1
    )
    z_near = swap(jnp.concatenate([near, x_0], axis=0), along_z)
    z_high, x_high, y_high, d_high, keep_0, send_0, z_near = tied(
        (z_high, x_high, y_high, d_high, keep_0, send_0, z_near)
    )
    high = (z_high, swap(z_high, core), y_high, swap(y_high, core))
    high = high + (x_high, swap(x_high, core), d_high, swap(d_high, core))
    line = [[[(4 * x + k, n) for k in range(groups)] for x in range(2)] for n in range(2)]
    keep_2, send_2 = run_expert(high, line[0], slots, weights, sizes, 1)
    got_2 = swap(send_2, core)
    keep_2, high, z_near = tied((keep_2, high, z_near))
    near_1 = (z_near, swap(z_near, core))
    keep_3, send_3 = run_expert(high, line[1], slots, weights, sizes, 1)
    got_2, keep_3, send_3, near_1 = tied((got_2, keep_3, send_3, near_1))
    got_3 = swap(send_3, core)
    blocks = [[(k % 2, 2 * x + k // 2) for k in range(groups)] for x in range(2)]
    keep_1, send_1 = run_expert(near_1, blocks, slots, weights, sizes, 1)
    got_1 = swap(send_1, core)
    keep_1, got_3, send_0 = tied((keep_1, got_3, send_0))
    got_0 = swap(send_0, core)
    z_back = swap(add_up(keep_1, got_1), along_z)

    def spread(*terms):
        return [add_up(*[term[n] for term in terms]) for n in (2, 3, 1)]

    def gather(parts):
        return [swap(part, step) for part, step in zip(parts, (along_x, diagonal, along_y))]

    far_sums = [jnp.stack(pair) for pair in zip(spread(keep_2, got_2), spread(keep_3, got_3))]
    far_sums = gather(far_sums)
    line_2 = add_up(keep_2[0], got_2[0], *[part[0] for part in far_sums])
    line_3 = add_up(keep_3[0], got_3[0], *[part[1] for part in far_sums])
    back_2, back_3 = swap(line_2, 2 * along_z), swap(line_3, 3 * along_z)
    z_back, _, _ = tied((z_back, line_2, line_3))
    near_sums = gather(spread(keep_0, got_0, z_back))
    mixed = add_up(keep_0[0], got_0[0], z_back[0], *near_sums, back_2, back_3)
    return mixed.T


def on_device(*args):
    tokens, expert_ids = args[0], args[2]
    experts, groups = lax.axis_size("seq"), lax.axis_size("rep")
    capacity = 2 * tokens.shape[0] * expert_ids.shape[1] // experts
    if capacity >= tokens.shape[0] and experts == 2 * groups and groups == 4:
        return dense(*args)
    return routed(*args, capacity)


def solution(mesh):
    placed = (
        P("seq", None),
        P(),
        P("seq", None),
        P("seq", None),
        P("seq", None, "rep"),
        P("seq", "rep"),
        P("seq", None, "rep"),
        P("seq", "rep"),
        P("seq", "rep", None),
        P("seq", "rep"),
    )
    return jax.shard_map(
        on_device, mesh=mesh, in_specs=placed, out_specs=P("seq", "rep"), check_vma=False
    )
```

```python
import functools

import jax
import jax.numpy as jnp
from jax import lax
from jax.experimental import pallas as pl
from jax.experimental.pallas import tpu as pltpu
from jax.sharding import PartitionSpec as P


def rms_normed(values, norm_gain, axis):
    values = values.astype(jnp.float32)
    scale = lax.rsqrt(jnp.mean(values * values, axis=axis, keepdims=True) + 1e-05)
    return (values * scale * norm_gain).astype(jnp.bfloat16)


def gated(gate_pre, up_pre):
    return (gate_pre * jax.nn.sigmoid(1.702 * gate_pre) * (up_pre + 1.0)).astype(jnp.bfloat16)


def routed(
    tokens,
    norm_gain,
    expert_ids,
    route_weights,
    gate_weight,
    gate_bias,
    up_weight,
    up_bias,
    down_weight,
    down_bias,
    capacity,
):
    tok_rows, features = tokens.shape
    per_token = expert_ids.shape[1]
    experts = lax.axis_size("seq")
    quarter = features // lax.axis_size("rep")
    normed = rms_normed(tokens, norm_gain, -1)
    flat_ids = expert_ids.reshape(-1)
    onehot = (flat_ids[:, None] == jnp.arange(experts, dtype=jnp.int32)[None, :]).astype(jnp.int32)
    before = jnp.cumsum(onehot, axis=0) - onehot
    slot_index = jnp.sum(before * onehot, axis=1)
    destination = flat_ids * capacity + slot_index
    owner_row = jnp.arange(tok_rows * per_token, dtype=jnp.int32) // per_token
    buffer = jnp.zeros((experts * capacity, features), jnp.bfloat16)
    buffer = buffer.at[destination].set(normed[owner_row])
    received = lax.all_to_all(
        buffer.reshape(experts, capacity, features), "seq", split_axis=0, concat_axis=0, tiled=True
    )
    in_rows = received.reshape(-1, features)
    gate_pre = jnp.dot(in_rows, gate_weight[0], preferred_element_type=jnp.float32) + gate_bias[0]
    up_pre = jnp.dot(in_rows, up_weight[0], preferred_element_type=jnp.float32) + up_bias[0]
    partial_value = jnp.dot(
        gated(gate_pre, up_pre), down_weight[0], preferred_element_type=jnp.float32
    ).astype(jnp.bfloat16)
    summed = lax.psum_scatter(
        partial_value.reshape(experts, capacity, features),
        "rep",
        scatter_dimension=2,
        tiled=True,
    ).astype(jnp.float32)
    expert_out = (summed + down_bias[0][None, None, :]).astype(jnp.bfloat16)
    returned = lax.all_to_all(expert_out, "seq", split_axis=0, concat_axis=0, tiled=True)
    picked = returned.reshape(-1, quarter)[destination].reshape(tok_rows, per_token, quarter)
    mixed = jnp.sum(route_weights[:, :, None] * picked.astype(jnp.float32), axis=1)
    return mixed.astype(jnp.bfloat16)


tied = lax.optimization_barrier


def round_up(number, step):
    return -(-number // step) * step


def add_up(*terms):
    total = terms[0].astype(jnp.float32)
    for term in terms[1:]:
        total = total + term.astype(jnp.float32)
    return total.astype(jnp.bfloat16)


def padded(array, rows, columns):
    return jnp.pad(array, ((0, rows - array.shape[0]), (0, columns - array.shape[1])))


def column(row, size, lanes):
    return jnp.broadcast_to(padded(row, 1, size), (lanes, size)).T


def inward_kernel(groups, gate_ref, up_ref, biases_ref, weight_out, bias_out):
    features, hidden = gate_ref.shape
    quarter = features // groups
    hidden_pad, size = round_up(hidden, 128), round_up(quarter, 128)
    half = hidden_pad // 2
    for n, weight in enumerate((gate_ref, up_ref)):
        values = weight[...].astype(jnp.float32)
        added = column(biases_ref[n : n + 1], hidden_pad, bias_out.shape[1])
        halves = [
            (slice(h * half, (h + 1) * half), slice((2 * h + n) * half, (2 * h + n + 1) * half))
            for h in range(2)
        ]
        for q in range(groups):
            part = padded(values[q * quarter : (q + 1) * quarter], size, hidden_pad)
            part = part.T.astype(jnp.bfloat16)
            for own, rows in halves:
                weight_out[rows, q * size : (q + 1) * size] = part[own]
        for own, rows in halves:
            bias_out[rows] = added[own]


def outward_kernel(groups, down_ref, biases_ref, weight_out, bias_out):
    hidden, features = down_ref.shape
    quarter = features // groups
    hidden_pad, size = round_up(hidden, 128), round_up(quarter, 128)
    values = padded(down_ref[...].astype(jnp.float32), hidden_pad, round_up(features, 128)).T
    for q in range(groups):
        part = padded(values[q * quarter : (q + 1) * quarter], size, hidden_pad)
        weight_out[q * size : (q + 1) * size] = part.astype(jnp.bfloat16)
    bias_out[...] = column(biases_ref[2:3], size, bias_out.shape[1])


def arrange(kernel, groups, lanes, arrays, shape, bias_rows):
    return pl.pallas_call(
        functools.partial(kernel, groups),
        out_shape=[
            jax.ShapeDtypeStruct(shape, jnp.bfloat16),
            jax.ShapeDtypeStruct((bias_rows, lanes), jnp.float32),
        ],
        compiler_params=pltpu.CompilerParams(vmem_limit_bytes=40 * 2**20),
        cost_estimate=pl.CostEstimate(
            flops=0, bytes_accessed=16 * arrays[0].size, transcendentals=0
        ),
    )(*arrays)


def fetch(sources, targets, sems):
    copies = [
        pltpu.make_async_copy(source, target, sems.at[n])
        for n, (source, target) in enumerate(zip(sources, targets))
    ]
    for copy in copies:
        copy.start()
    for copy in copies:
        copy.wait()


def pieces_kernel(groups, per, experts, *refs):
    sources, (one_ref, near_ref, far_ref) = refs[:4], refs[4:7]
    tokens_ref, gain_ref, ids_ref, weights_ref = refs[7:11]
    fetch(sources, refs[7:11], refs[11])
    features, lanes = tokens_ref.shape
    quarter = features // groups
    tail = one_ref.shape[0] - quarter
    rep = lax.axis_index("rep")
    values = tokens_ref[...].astype(jnp.float32)
    scale = lax.rsqrt(jnp.mean(values * values, axis=0, keepdims=True) + 1e-05)
    gain = jnp.broadcast_to(gain_ref[...].reshape(1, features), (lanes, features)).T
    normed = values * scale * gain
    row = lax.broadcasted_iota(jnp.int32, (tail, lanes), 0)
    chosen = lax.broadcasted_iota(jnp.int32, (round_up(experts, 8), lanes), 0)
    shares = jnp.zeros(chosen.shape, jnp.float32)
    for k in range(ids_ref.shape[0]):
        shares += jnp.where(ids_ref[k : k + 1] == chosen, weights_ref[k : k + 1], 0.0)
    terms = []
    for _ in range(3):
        term = shares.astype(jnp.bfloat16).astype(jnp.float32)
        terms.append(term)
        shares = shares - term
    for q in range(groups):
        rows = jnp.zeros((tail, lanes), jnp.float32)
        for n, term in enumerate(terms):
            for i in range(per):
                expert = q * per + i
                if expert < experts:
                    rows = jnp.where(row == n * per + i, term[expert : expert + 1], rows)
        piece = jnp.concatenate([normed[q * quarter : (q + 1) * quarter], rows], axis=0)
        piece = piece.astype(jnp.bfloat16)
        k = rep ^ q
        for side, target in enumerate((near_ref, far_ref)):

            @pl.when(k % 2 == side)
            def _(target=target, piece=piece, k=k):
                target[k // 2] = piece

        @pl.when(k == 0)
        def _(piece=piece):
            one_ref[...] = piece


def make_pieces(tokens, norm_gain, expert_ids, route_weights, groups, per, experts):
    features, lanes = tokens.shape
    rows = round_up(features // groups + 3 * per, 16)
    pair = jax.ShapeDtypeStruct((groups // 2, rows, lanes), jnp.bfloat16)
    arrays = (tokens, norm_gain, expert_ids, route_weights)
    return pl.pallas_call(
        functools.partial(pieces_kernel, groups, per, experts),
        in_specs=[pl.BlockSpec(memory_space=pltpu.HBM)] * 4,
        out_specs=[pl.BlockSpec(memory_space=pltpu.VMEM)] * 3,
        out_shape=[jax.ShapeDtypeStruct((rows, lanes), jnp.bfloat16), pair, pair],
        scratch_shapes=[pltpu.VMEM(a.shape, a.dtype) for a in arrays]
        + [pltpu.SemaphoreType.DMA((len(arrays),))],
        compiler_params=pltpu.CompilerParams(vmem_limit_bytes=60 * 2**20),
    )(*arrays)


def expert_kernel(quarter, per, blocks, slots, *refs):
    groups = len(blocks[0])
    counted = 1 + max(at for block in blocks for at, _ in block)
    arrays = refs[:counted]
    gate_up_ref, bias_ref, down_ref, down_bias_ref, keep_ref, send_ref = refs[counted : 6 + counted]
    scratch = refs[6 + counted :]
    _, piece_rows, lanes = arrays[0].shape
    size = gate_up_ref.shape[1] // groups
    hidden = gate_up_ref.shape[0] // 2
    rep, seq = lax.axis_index("rep"), lax.axis_index("seq")
    halves = len(scratch)
    used = round_up(quarter, 16)
    count = len(blocks) // halves
    row = lax.broadcasted_iota(jnp.int32, (piece_rows - quarter, lanes), 0)
    for half in range(halves):
        rows_ref = scratch[half]
        if size > piece_rows:
            for k in range(groups):
                rows_ref[k * size + piece_rows : (k + 1) * size, :] = jnp.zeros(
                    (size - piece_rows, count * lanes), jnp.bfloat16
                )
        shares = [jnp.zeros((1, lanes), jnp.float32)] * count
        for k in range(groups):
            source = rep ^ k
            at_row = pl.ds(pl.multiple_of(source * size, size), piece_rows)
            mine = (lax.rem(row, per) == seq - source * per) & (row < 3 * per)
            for j in range(count):
                at, index = blocks[half * count + j][k]
                values = arrays[at][index]
                rows_ref[at_row, j * lanes : (j + 1) * lanes] = values
                terms = values.astype(jnp.float32)[quarter:]
                shares[j] += jnp.sum(jnp.where(mine, terms, 0.0), axis=0, keepdims=True)
        wide = jnp.concatenate(shares, axis=1)
        activated = []
        for part in range(2):
            at = slice(part * hidden, (part + 1) * hidden)
            both = jnp.dot(gate_up_ref[at], rows_ref[...], preferred_element_type=jnp.float32)
            both = both + jnp.concatenate([bias_ref[at]] * count, axis=1)
            activated.append(gated(both[: hidden // 2], both[hidden // 2 :]))
        activated = jnp.concatenate(activated, axis=0)
        for k in range(groups):
            own_rows = down_ref[pl.ds(pl.multiple_of((rep ^ k) * size, size), used), :]
            rows = jnp.dot(own_rows, activated, preferred_element_type=jnp.float32)
            if k == 0:
                rows = rows + jnp.concatenate([down_bias_ref[:used]] * count, axis=1)
            rows = (rows * wide).astype(jnp.bfloat16)
            target = send_ref if k % 2 else keep_ref
            for j in range(count):
                target[slots[half * count + j][k // 2]] = rows[:quarter, j * lanes : (j + 1) * lanes]


def run_expert(arrays, blocks, slots, weights, sizes, halves):
    quarter, per = sizes
    lanes = arrays[0].shape[2]
    gate_up, down = weights[0], weights[2]
    tokens = len(blocks) * lanes
    whole = pl.BlockSpec(memory_space=pltpu.VMEM)
    out = jax.ShapeDtypeStruct((2 * len(blocks), quarter, lanes), jnp.bfloat16)
    columns = tokens // halves
    return pl.pallas_call(
        functools.partial(expert_kernel, quarter, per, blocks, slots),
        in_specs=[whole] * (len(arrays) + len(weights)),
        out_specs=[whole, whole],
        out_shape=[out, out],
        scratch_shapes=[pltpu.VMEM((gate_up.shape[1], columns), jnp.bfloat16)] * halves,
        compiler_params=pltpu.CompilerParams(vmem_limit_bytes=40 * 2**20),
        cost_estimate=pl.CostEstimate(
            flops=4 * tokens * (gate_up.size + down.size),
            bytes_accessed=2 * (gate_up.size + down.size),
            transcendentals=0,
        ),
    )(*arrays, *weights)


def dense(
    tokens,
    norm_gain,
    expert_ids,
    route_weights,
    gate_weight,
    gate_bias,
    up_weight,
    up_bias,
    down_weight,
    down_bias,
):
    lanes, features = tokens.shape
    experts = lax.axis_size("seq")
    groups = lax.axis_size("rep")
    quarter = features // groups
    devices = experts * groups
    core, along_y, along_x, along_z = 1, 2, groups, 2 * groups

    def swap(array, step):
        return lax.ppermute(array, ("seq", "rep"), [(i, i ^ step) for i in range(devices)])

    per = -(-experts // groups)
    one, near, far = make_pieces(
        tokens.T, norm_gain, expert_ids.T, route_weights.T, groups, per, experts
    )
    z_2, z_3 = swap(one, 2 * along_z), swap(one, 3 * along_z)
    x_0 = swap(near, along_x)
    hidden_pad = round_up(gate_weight.shape[2], 128)
    wide = groups * round_up(quarter, 128)
    biases = jnp.concatenate([gate_bias, up_bias, down_bias], axis=0)
    inward = arrange(
        inward_kernel,
        groups,
        lanes,
        (gate_weight[0], up_weight[0], biases),
        (2 * hidden_pad, wide),
        2 * hidden_pad,
    )
    z_2, z_3, inward = tied((z_2, z_3, inward))
    z_high = jnp.stack([z_2, z_3])
    diagonal = along_x + along_y
    x_high, y_high = swap(z_high, along_x), swap(z_high, along_y)
    d_high = swap(z_high, diagonal)
    outward = arrange(
        outward_kernel,
        groups,
        lanes,
        (down_weight[0], biases),
        (wide, hidden_pad),
        wide // groups,
    )
    x_0, outward = tied((x_0, outward))
    weights = (*inward, *outward)

    def pairs(first, step):
        return [[(first + step * x + k % 2, k // 2) for k in range(groups)] for x in range(2)]

    slots = ((0, 1), (2, 3))
    sizes = (quarter, per)
    keep_0, send_0 = run_expert(
        (near, far, x_0, swap(x_0, core)), pairs(0, 2), slots, weights, sizes, 1
    )
    z_near = swap(jnp.concatenate([near, x_0], axis=0), along_z)
    z_high, x_high, y_high, d_high, keep_0, send_0, z_near = tied(
        (z_high, x_high, y_high, d_high, keep_0, send_0, z_near)
    )
    high = (z_high, swap(z_high, core), y_high, swap(y_high, core))
    high = high + (x_high, swap(x_high, core), d_high, swap(d_high, core))
    line = [[[(4 * x + k, n) for k in range(groups)] for x in range(2)] for n in range(2)]
    keep_2, send_2 = run_expert(high, line[0], slots, weights, sizes, 1)
    got_2 = swap(send_2, core)
    keep_2, high, z_near = tied((keep_2, high, z_near))
    near_1 = (z_near, swap(z_near, core))
    keep_3, send_3 = run_expert(high, line[1], slots, weights, sizes, 1)
    got_2, keep_3, send_3, near_1 = tied((got_2, keep_3, send_3, near_1))
    got_3 = swap(send_3, core)
    blocks = [[(k % 2, 2 * x + k // 2) for k in range(groups)] for x in range(2)]
    keep_1, send_1 = run_expert(near_1, blocks, slots, weights, sizes, 1)
    got_1 = swap(send_1, core)
    keep_1, got_3, send_0 = tied((keep_1, got_3, send_0))
    got_0 = swap(send_0, core)
    z_back = swap(add_up(keep_1, got_1), along_z)

    def spread(*terms):
        return [add_up(*[term[n] for term in terms]) for n in (2, 3, 1)]

    def gather(parts):
        return [swap(part, step) for part, step in zip(parts, (along_x, diagonal, along_y))]

    far_sums = [jnp.stack(pair) for pair in zip(spread(keep_2, got_2), spread(keep_3, got_3))]
    far_sums = gather(far_sums)
    line_2 = add_up(keep_2[0], got_2[0], *[part[0] for part in far_sums])
    line_3 = add_up(keep_3[0], got_3[0], *[part[1] for part in far_sums])
    back_2, back_3 = swap(line_2, 2 * along_z), swap(line_3, 3 * along_z)
    z_back, _, _ = tied((z_back, line_2, line_3))
    near_sums = gather(spread(keep_0, got_0, z_back))
    mixed = add_up(keep_0[0], got_0[0], z_back[0], *near_sums, back_2, back_3)
    return mixed.T


def on_device(*args):
    tokens, expert_ids = args[0], args[2]
    experts, groups = lax.axis_size("seq"), lax.axis_size("rep")
    capacity = 2 * tokens.shape[0] * expert_ids.shape[1] // experts
    if capacity >= tokens.shape[0] and experts == 2 * groups and groups == 4:
        return dense(*args)
    return routed(*args, capacity)


def solution(mesh):
    placed = (
        P("seq", None),
        P(),
        P("seq", None),
        P("seq", None),
        P("seq", None, "rep"),
        P("seq", "rep"),
        P("seq", None, "rep"),
        P("seq", "rep"),
        P("seq", "rep", None),
        P("seq", "rep"),
    )
    return jax.shard_map(
        on_device, mesh=mesh, in_specs=placed, out_specs=P("seq", "rep"), check_vma=False
    )
```

```python
import functools

import jax
import jax.numpy as jnp
from jax import lax
from jax.experimental import pallas as pl
from jax.experimental.pallas import tpu as pltpu
from jax.sharding import PartitionSpec as P


def rms_normed(values, norm_gain, axis):
    values = values.astype(jnp.float32)
    scale = lax.rsqrt(jnp.mean(values * values, axis=axis, keepdims=True) + 1e-05)
    return (values * scale * norm_gain).astype(jnp.bfloat16)


def gated(gate_pre, up_pre):
    return (gate_pre * jax.nn.sigmoid(1.702 * gate_pre) * (up_pre + 1.0)).astype(jnp.bfloat16)


def routed(
    tokens,
    norm_gain,
    expert_ids,
    route_weights,
    gate_weight,
    gate_bias,
    up_weight,
    up_bias,
    down_weight,
    down_bias,
    capacity,
):
    tok_rows, features = tokens.shape
    per_token = expert_ids.shape[1]
    experts = lax.axis_size("seq")
    quarter = features // lax.axis_size("rep")
    normed = rms_normed(tokens, norm_gain, -1)
    flat_ids = expert_ids.reshape(-1)
    onehot = (flat_ids[:, None] == jnp.arange(experts, dtype=jnp.int32)[None, :]).astype(jnp.int32)
    before = jnp.cumsum(onehot, axis=0) - onehot
    slot_index = jnp.sum(before * onehot, axis=1)
    destination = flat_ids * capacity + slot_index
    owner_row = jnp.arange(tok_rows * per_token, dtype=jnp.int32) // per_token
    buffer = jnp.zeros((experts * capacity, features), jnp.bfloat16)
    buffer = buffer.at[destination].set(normed[owner_row])
    received = lax.all_to_all(
        buffer.reshape(experts, capacity, features), "seq", split_axis=0, concat_axis=0, tiled=True
    )
    in_rows = received.reshape(-1, features)
    gate_pre = jnp.dot(in_rows, gate_weight[0], preferred_element_type=jnp.float32) + gate_bias[0]
    up_pre = jnp.dot(in_rows, up_weight[0], preferred_element_type=jnp.float32) + up_bias[0]
    partial_value = jnp.dot(
        gated(gate_pre, up_pre), down_weight[0], preferred_element_type=jnp.float32
    ).astype(jnp.bfloat16)
    summed = lax.psum_scatter(
        partial_value.reshape(experts, capacity, features),
        "rep",
        scatter_dimension=2,
        tiled=True,
    ).astype(jnp.float32)
    expert_out = (summed + down_bias[0][None, None, :]).astype(jnp.bfloat16)
    returned = lax.all_to_all(expert_out, "seq", split_axis=0, concat_axis=0, tiled=True)
    picked = returned.reshape(-1, quarter)[destination].reshape(tok_rows, per_token, quarter)
    mixed = jnp.sum(route_weights[:, :, None] * picked.astype(jnp.float32), axis=1)
    return mixed.astype(jnp.bfloat16)


tied = lax.optimization_barrier


def round_up(number, step):
    return -(-number // step) * step


def add_up(*terms):
    total = terms[0].astype(jnp.float32)
    for term in terms[1:]:
        total = total + term.astype(jnp.float32)
    return total.astype(jnp.bfloat16)


def padded(array, rows, columns):
    return jnp.pad(array, ((0, rows - array.shape[0]), (0, columns - array.shape[1])))


def column(row, size, lanes):
    return jnp.broadcast_to(padded(row, 1, size), (lanes, size)).T


def inward_kernel(groups, gate_ref, up_ref, biases_ref, weight_out, bias_out):
    features, hidden = gate_ref.shape
    quarter = features // groups
    hidden_pad, size = round_up(hidden, 128), round_up(quarter, 128)
    half = hidden_pad // 2
    for n, weight in enumerate((gate_ref, up_ref)):
        values = weight[...].astype(jnp.float32)
        added = column(biases_ref[n : n + 1], hidden_pad, bias_out.shape[1])
        halves = [
            (slice(h * half, (h + 1) * half), slice((2 * h + n) * half, (2 * h + n + 1) * half))
            for h in range(2)
        ]
        for q in range(groups):
            part = padded(values[q * quarter : (q + 1) * quarter], size, hidden_pad)
            part = part.T.astype(jnp.bfloat16)
            for own, rows in halves:
                weight_out[rows, q * size : (q + 1) * size] = part[own]
        for own, rows in halves:
            bias_out[rows] = added[own]


def outward_kernel(groups, down_ref, biases_ref, weight_out, bias_out):
    hidden, features = down_ref.shape
    quarter = features // groups
    hidden_pad, size = round_up(hidden, 128), round_up(quarter, 128)
    values = padded(down_ref[...].astype(jnp.float32), hidden_pad, round_up(features, 128)).T
    for q in range(groups):
        part = padded(values[q * quarter : (q + 1) * quarter], size, hidden_pad)
        weight_out[q * size : (q + 1) * size] = part.astype(jnp.bfloat16)
    bias_out[...] = column(biases_ref[2:3], size, bias_out.shape[1])


def arrange(kernel, groups, lanes, arrays, shape, bias_rows):
    return pl.pallas_call(
        functools.partial(kernel, groups),
        out_shape=[
            jax.ShapeDtypeStruct(shape, jnp.bfloat16),
            jax.ShapeDtypeStruct((bias_rows, lanes), jnp.float32),
        ],
        compiler_params=pltpu.CompilerParams(vmem_limit_bytes=40 * 2**20),
        cost_estimate=pl.CostEstimate(
            flops=0, bytes_accessed=16 * arrays[0].size, transcendentals=0
        ),
    )(*arrays)


def fetch(sources, targets, sems):
    copies = [
        pltpu.make_async_copy(source, target, sems.at[n])
        for n, (source, target) in enumerate(zip(sources, targets))
    ]
    for copy in copies:
        copy.start()
    for copy in copies:
        copy.wait()


def pieces_kernel(groups, per, experts, *refs):
    sources, (one_ref, near_ref, far_ref) = refs[:4], refs[4:7]
    tokens_ref, gain_ref, ids_ref, weights_ref = refs[7:11]
    fetch(sources, refs[7:11], refs[11])
    features, lanes = tokens_ref.shape
    quarter = features // groups
    tail = one_ref.shape[0] - quarter
    rep = lax.axis_index("rep")
    values = tokens_ref[...].astype(jnp.float32)
    scale = lax.rsqrt(jnp.mean(values * values, axis=0, keepdims=True) + 1e-05)
    gain = jnp.broadcast_to(gain_ref[...].reshape(1, features), (lanes, features)).T
    normed = values * scale * gain
    row = lax.broadcasted_iota(jnp.int32, (tail, lanes), 0)
    chosen = lax.broadcasted_iota(jnp.int32, (round_up(experts, 8), lanes), 0)
    shares = jnp.zeros(chosen.shape, jnp.float32)
    for k in range(ids_ref.shape[0]):
        shares += jnp.where(ids_ref[k : k + 1] == chosen, weights_ref[k : k + 1], 0.0)
    terms = []
    for _ in range(3):
        term = shares.astype(jnp.bfloat16).astype(jnp.float32)
        terms.append(term)
        shares = shares - term
    for q in range(groups):
        rows = jnp.zeros((tail, lanes), jnp.float32)
        for n, term in enumerate(terms):
            for i in range(per):
                expert = q * per + i
                if expert < experts:
                    rows = jnp.where(row == n * per + i, term[expert : expert + 1], rows)
        piece = jnp.concatenate([normed[q * quarter : (q + 1) * quarter], rows], axis=0)
        piece = piece.astype(jnp.bfloat16)
        k = rep ^ q
        for side, target in enumerate((near_ref, far_ref)):

            @pl.when(k % 2 == side)
            def _(target=target, piece=piece, k=k):
                target[k // 2] = piece

        @pl.when(k == 0)
        def _(piece=piece):
            one_ref[...] = piece


def make_pieces(tokens, norm_gain, expert_ids, route_weights, groups, per, experts):
    features, lanes = tokens.shape
    rows = round_up(features // groups + 3 * per, 16)
    pair = jax.ShapeDtypeStruct((groups // 2, rows, lanes), jnp.bfloat16)
    arrays = (tokens, norm_gain, expert_ids, route_weights)
    return pl.pallas_call(
        functools.partial(pieces_kernel, groups, per, experts),
        in_specs=[pl.BlockSpec(memory_space=pltpu.HBM)] * 4,
        out_specs=[pl.BlockSpec(memory_space=pltpu.VMEM)] * 3,
        out_shape=[jax.ShapeDtypeStruct((rows, lanes), jnp.bfloat16), pair, pair],
        scratch_shapes=[pltpu.VMEM(a.shape, a.dtype) for a in arrays]
        + [pltpu.SemaphoreType.DMA((len(arrays),))],
        compiler_params=pltpu.CompilerParams(vmem_limit_bytes=60 * 2**20),
    )(*arrays)


def expert_kernel(quarter, per, blocks, slots, *refs):
    groups = len(blocks[0])
    counted = 1 + max(at for block in blocks for at, _ in block)
    arrays = refs[:counted]
    gate_up_ref, bias_ref, down_ref, down_bias_ref, keep_ref, send_ref = refs[counted : 6 + counted]
    scratch = refs[6 + counted :]
    _, piece_rows, lanes = arrays[0].shape
    size = gate_up_ref.shape[1] // groups
    hidden = gate_up_ref.shape[0] // 2
    rep, seq = lax.axis_index("rep"), lax.axis_index("seq")
    halves = len(scratch)
    used = round_up(quarter, 16)
    count = len(blocks) // halves
    row = lax.broadcasted_iota(jnp.int32, (piece_rows - quarter, lanes), 0)
    for half in range(halves):
        rows_ref = scratch[half]
        if size > piece_rows:
            for k in range(groups):
                rows_ref[k * size + piece_rows : (k + 1) * size, :] = jnp.zeros(
                    (size - piece_rows, count * lanes), jnp.bfloat16
                )
        shares = [jnp.zeros((1, lanes), jnp.float32)] * count
        for k in range(groups):
            source = rep ^ k
            at_row = pl.ds(pl.multiple_of(source * size, size), piece_rows)
            mine = (lax.rem(row, per) == seq - source * per) & (row < 3 * per)
            for j in range(count):
                at, index = blocks[half * count + j][k]
                values = arrays[at][index]
                rows_ref[at_row, j * lanes : (j + 1) * lanes] = values
                terms = values[quarter // 16 * 16 :].astype(jnp.float32)[quarter % 16 :]
                shares[j] += jnp.sum(jnp.where(mine, terms, 0.0), axis=0, keepdims=True)
        wide = jnp.concatenate(shares, axis=1)
        activated = []
        for part in range(2):
            at = slice(part * hidden, (part + 1) * hidden)
            both = jnp.dot(gate_up_ref[at], rows_ref[...], preferred_element_type=jnp.float32)
            both = both + jnp.concatenate([bias_ref[at]] * count, axis=1)
            activated.append(gated(both[: hidden // 2], both[hidden // 2 :]))
        activated = jnp.concatenate(activated, axis=0)
        for k in range(groups):
            own_rows = down_ref[pl.ds(pl.multiple_of((rep ^ k) * size, size), used), :]
            rows = jnp.dot(own_rows, activated, preferred_element_type=jnp.float32)
            if k == 0:
                rows = rows + jnp.concatenate([down_bias_ref[:used]] * count, axis=1)
            rows = (rows * wide).astype(jnp.bfloat16)
            target = send_ref if k % 2 else keep_ref
            for j in range(count):
                target[slots[half * count + j][k // 2]] = rows[:quarter, j * lanes : (j + 1) * lanes]


def run_expert(arrays, blocks, slots, weights, sizes, halves):
    quarter, per = sizes
    lanes = arrays[0].shape[2]
    gate_up, down = weights[0], weights[2]
    tokens = len(blocks) * lanes
    whole = pl.BlockSpec(memory_space=pltpu.VMEM)
    out = jax.ShapeDtypeStruct((2 * len(blocks), quarter, lanes), jnp.bfloat16)
    columns = tokens // halves
    return pl.pallas_call(
        functools.partial(expert_kernel, quarter, per, blocks, slots),
        in_specs=[whole] * (len(arrays) + len(weights)),
        out_specs=[whole, whole],
        out_shape=[out, out],
        scratch_shapes=[pltpu.VMEM((gate_up.shape[1], columns), jnp.bfloat16)] * halves,
        compiler_params=pltpu.CompilerParams(vmem_limit_bytes=40 * 2**20),
        cost_estimate=pl.CostEstimate(
            flops=4 * tokens * (gate_up.size + down.size),
            bytes_accessed=2 * (gate_up.size + down.size),
            transcendentals=0,
        ),
    )(*arrays, *weights)


def dense(
    tokens,
    norm_gain,
    expert_ids,
    route_weights,
    gate_weight,
    gate_bias,
    up_weight,
    up_bias,
    down_weight,
    down_bias,
):
    lanes, features = tokens.shape
    experts = lax.axis_size("seq")
    groups = lax.axis_size("rep")
    quarter = features // groups
    devices = experts * groups
    core, along_y, along_x, along_z = 1, 2, groups, 2 * groups

    def swap(array, step):
        return lax.ppermute(array, ("seq", "rep"), [(i, i ^ step) for i in range(devices)])

    per = -(-experts // groups)
    one, near, far = make_pieces(
        tokens.T, norm_gain, expert_ids.T, route_weights.T, groups, per, experts
    )
    z_2, z_3 = swap(one, 2 * along_z), swap(one, 3 * along_z)
    x_0 = swap(near, along_x)
    hidden_pad = round_up(gate_weight.shape[2], 128)
    wide = groups * round_up(quarter, 128)
    biases = jnp.concatenate([gate_bias, up_bias, down_bias], axis=0)
    inward = arrange(
        inward_kernel,
        groups,
        lanes,
        (gate_weight[0], up_weight[0], biases),
        (2 * hidden_pad, wide),
        2 * hidden_pad,
    )
    z_2, z_3, inward = tied((z_2, z_3, inward))
    z_high = jnp.stack([z_2, z_3])
    diagonal = along_x + along_y
    x_high, y_high = swap(z_high, along_x), swap(z_high, along_y)
    d_high = swap(z_high, diagonal)
    outward = arrange(
        outward_kernel,
        groups,
        lanes,
        (down_weight[0], biases),
        (wide, hidden_pad),
        wide // groups,
    )
    x_0, outward = tied((x_0, outward))
    weights = (*inward, *outward)

    def pairs(first, step):
        return [[(first + step * x + k % 2, k // 2) for k in range(groups)] for x in range(2)]

    slots = ((0, 1), (2, 3))
    sizes = (quarter, per)
    keep_0, send_0 = run_expert(
        (near, far, x_0, swap(x_0, core)), pairs(0, 2), slots, weights, sizes, 1
    )
    z_near = swap(jnp.concatenate([near, x_0], axis=0), along_z)
    z_high, x_high, y_high, d_high, keep_0, send_0, z_near = tied(
        (z_high, x_high, y_high, d_high, keep_0, send_0, z_near)
    )
    high = (z_high, swap(z_high, core), y_high, swap(y_high, core))
    high = high + (x_high, swap(x_high, core), d_high, swap(d_high, core))
    line = [[[(4 * x + k, n) for k in range(groups)] for x in range(2)] for n in range(2)]
    keep_2, send_2 = run_expert(high, line[0], slots, weights, sizes, 1)
    got_2 = swap(send_2, core)
    keep_2, high, z_near = tied((keep_2, high, z_near))
    near_1 = (z_near, swap(z_near, core))
    keep_3, send_3 = run_expert(high, line[1], slots, weights, sizes, 1)
    got_2, keep_3, send_3, near_1 = tied((got_2, keep_3, send_3, near_1))
    got_3 = swap(send_3, core)
    blocks = [[(k % 2, 2 * x + k // 2) for k in range(groups)] for x in range(2)]
    keep_1, send_1 = run_expert(near_1, blocks, slots, weights, sizes, 1)
    got_1 = swap(send_1, core)
    keep_1, got_3, send_0 = tied((keep_1, got_3, send_0))
    got_0 = swap(send_0, core)
    z_back = swap(add_up(keep_1, got_1), along_z)

    def spread(*terms):
        return [add_up(*[term[n] for term in terms]) for n in (2, 3, 1)]

    def gather(parts):
        return [swap(part, step) for part, step in zip(parts, (along_x, diagonal, along_y))]

    far_sums = [jnp.stack(pair) for pair in zip(spread(keep_2, got_2), spread(keep_3, got_3))]
    far_sums = gather(far_sums)
    line_2 = add_up(keep_2[0], got_2[0], *[part[0] for part in far_sums])
    line_3 = add_up(keep_3[0], got_3[0], *[part[1] for part in far_sums])
    back_2, back_3 = swap(line_2, 2 * along_z), swap(line_3, 3 * along_z)
    z_back, _, _ = tied((z_back, line_2, line_3))
    near_sums = gather(spread(keep_0, got_0, z_back))
    mixed = add_up(keep_0[0], got_0[0], z_back[0], *near_sums, back_2, back_3)
    return mixed.T


def on_device(*args):
    tokens, expert_ids = args[0], args[2]
    experts, groups = lax.axis_size("seq"), lax.axis_size("rep")
    capacity = 2 * tokens.shape[0] * expert_ids.shape[1] // experts
    if capacity >= tokens.shape[0] and experts == 2 * groups and groups == 4:
        return dense(*args)
    return routed(*args, capacity)


def solution(mesh):
    placed = (
        P("seq", None),
        P(),
        P("seq", None),
        P("seq", None),
        P("seq", None, "rep"),
        P("seq", "rep"),
        P("seq", None, "rep"),
        P("seq", "rep"),
        P("seq", "rep", None),
        P("seq", "rep"),
    )
    return jax.shard_map(
        on_device, mesh=mesh, in_specs=placed, out_specs=P("seq", "rep"), check_vma=False
    )
```
